32 devices in a mesh: fsdp: 4 (over z), context: 4 (over y, core), tensor: 2 (over x).
Axes of the slice: x: 2, y: 2, z: 4, core: 2. Of those that a mesh axis runs over, the one named last changes fastest.
Arguments:
- tokens: bfloat16 [4, 1024, 2048], P('fsdp', 'context', 'tensor'), may hold values from -6 to 6
- span_order: int32 [4, 2], replicated, may hold values from 0 to 7, as said below
- attn_gain: bfloat16 [2048], P('fsdp'), may hold values from 0.099609375 to 1.8984375
- w_query: bfloat16 [2048, 2048], P('fsdp', 'tensor'), may hold values from -0.125 to 0.125
- key_weight: bfloat16 [2048, 512], P('fsdp', 'tensor'), may hold values from -0.125 to 0.125
- value_weight: bfloat16 [2048, 512], P('fsdp', 'tensor'), may hold values from -0.125 to 0.125
- w_out: bfloat16 [2048, 2048], P('tensor', 'fsdp'), may hold values from -3 to 3
- mlp_gain: bfloat16 [2048], P('fsdp'), may hold values from 0.099609375 to 1.8984375
- w_gate: bfloat16 [2048, 8192], P('fsdp', 'tensor'), may hold values from -0.125 to 0.125
- w_up: bfloat16 [2048, 8192], P('fsdp', 'tensor'), may hold values from -0.125 to 0.125
- w_down: bfloat16 [8192, 2048], P('tensor', 'fsdp'), may hold values from -0.0625 to 0.0625
- out_grad: bfloat16 [4, 1024, 2048], P('fsdp', 'context', 'tensor'), may hold values from -6 to 6
Outputs:
- output: bfloat16 [4, 1024, 2048], P('fsdp', 'context', 'tensor')
- input_grad: bfloat16 [4, 1024, 2048], P('fsdp', 'context', 'tensor')
- attn_gain_grad: float32 [2048], P('fsdp')
- w_query_grad: float32 [2048, 2048], P('fsdp', 'tensor')
- w_key_grad: float32 [2048, 512], P('fsdp', 'tensor')
- w_value_grad: float32 [2048, 512], P('fsdp', 'tensor')
- w_out_grad: float32 [2048, 2048], P('tensor', 'fsdp')
- mlp_gain_grad: float32 [2048], P('fsdp')
- w_gate_grad: float32 [2048, 8192], P('fsdp', 'tensor')
- w_up_grad: float32 [2048, 8192], P('fsdp', 'tensor')
- w_down_grad: float32 [8192, 2048], P('tensor', 'fsdp')
The draws below stay inside these ranges and needn't reach their ends.
Inputs may be any that keep to these rules, and one draw needn't show every extreme that they name: `span_order`: row c holds j and 2 * 4 - 1 - j for some j, in either order; the smaller entries of the rows are a permutation of 0 to 4 - 1.
All inputs are finite; a program needn't handle non-finite values.
Results may differ from the reference program's by a relative error of at most 0.019.
Values may be sent and summed in bfloat16 or wider, within the bound.
A program may use at most 384 MiB of HBM per device.

```python
import math
from functools import partial
import jax
import jax.numpy as jnp
from jax import lax

MODEL_WIDTH = 2048
QUERY_HEADS = 32
KEY_VALUE_HEADS = 8
HEAD_WIDTH = 64
FF = 8192
TOK_DEV = 256
SPAN = 128
SEQUENCE_LENGTH = 1024
SEQS = 4
N_CONTEXT = 4


def draw_span_order(key, part):
    order_perm = jax.random.permutation(jax.random.fold_in(key, 1), N_CONTEXT).astype(jnp.int32)
    flips = jax.random.randint(jax.random.fold_in(key, 2), (N_CONTEXT,), 0, 2).astype(jnp.int32)
    mirror = (2 * N_CONTEXT - 1 - order_perm).astype(jnp.int32)
    first = jnp.where(flips == 1, mirror, order_perm).astype(jnp.int32)
    second = (2 * N_CONTEXT - 1 - first).astype(jnp.int32)
    return jnp.stack([first, second], -1)


def block_levels(rng, shape, cuts, least, high):
    def one(axis_at, shards_of):
        heights = jax.random.uniform(jax.random.fold_in(jax.random.fold_in(rng, 6), axis_at), (shards_of,), jnp.float32, least / len(cuts), high / len(cuts))
        return jnp.repeat(jnp.exp(heights), shape[axis_at] // shards_of).reshape((-1,) + (1,) * (len(shape) - axis_at - 1))

    gain = one(*cuts[0])
    for cut in cuts[1:]:
        gain = gain * one(*cut)
    return gain


def centred(stream_key, extent, scale, reach, cuts=(), held_as=jnp.bfloat16):
    drawn = scale * jax.random.normal(stream_key, extent, jnp.float32)
    if cuts:
        drawn = drawn * block_levels(stream_key, extent, cuts, -0.22, 0.18)
    return jnp.clip(drawn, -reach, reach).astype(held_as)


def setup_inputs(seed: int = 0) -> dict:
    key_of = jax.random.split(jax.random.key(seed), 13)
    return {
        "tokens": centred(key_of[0], (SEQS, SEQUENCE_LENGTH, MODEL_WIDTH), 1.0, 6.0, ((0, 4), (1, 4), (2, 2))),
        "span_order": draw_span_order(jax.random.fold_in(key_of[12], 71), 0),
        "attn_gain": jnp.clip(1.0 + 0.18 * jax.random.normal(key_of[2], (MODEL_WIDTH,), jnp.float32), 0.099609375, 1.8984375).astype(jnp.bfloat16),
        "w_query": centred(key_of[3], (MODEL_WIDTH, QUERY_HEADS * HEAD_WIDTH), MODEL_WIDTH ** -0.5, 0.125, ((0, 4), (1, 2))),
        "key_weight": centred(key_of[4], (MODEL_WIDTH, KEY_VALUE_HEADS * HEAD_WIDTH), MODEL_WIDTH ** -0.5, 0.125, ((0, 4), (1, 2))),
        "value_weight": centred(key_of[5], (MODEL_WIDTH, KEY_VALUE_HEADS * HEAD_WIDTH), MODEL_WIDTH ** -0.5, 0.125, ((0, 4), (1, 2))),
        "w_out": centred(key_of[6], (QUERY_HEADS * HEAD_WIDTH, MODEL_WIDTH), (max(1, 2 * MODEL_WIDTH // SEQUENCE_LENGTH)) ** -0.5, 3.0, ((0, 2), (1, 4))),
        "mlp_gain": jnp.clip(1.0 + 0.18 * jax.random.normal(key_of[7], (MODEL_WIDTH,), jnp.float32), 0.099609375, 1.8984375).astype(jnp.bfloat16),
        "w_gate": centred(key_of[8], (MODEL_WIDTH, FF), MODEL_WIDTH ** -0.5, 0.125, ((0, 4), (1, 2))),
        "w_up": centred(key_of[9], (MODEL_WIDTH, FF), MODEL_WIDTH ** -0.5, 0.125, ((0, 4), (1, 2))),
        "w_down": centred(key_of[10], (FF, MODEL_WIDTH), FF ** -0.5, 0.0625, ((0, 2), (1, 4))),
        "out_grad": centred(key_of[11], (SEQS, SEQUENCE_LENGTH, MODEL_WIDTH), 1.0, 6.0, ((0, 4), (1, 4), (2, 2))),
    }


@jax.custom_vjp
def low(v):
    return lax.optimization_barrier(v.astype(jnp.bfloat16)).astype(jnp.float32)

@jax.custom_vjp
def low_back(v):
    return v

def low_keep(v):
    return (low(v), None)

def low_pass(kept, grad):
    return (grad,)

def back_keep(v):
    return (v, None)

def back_low(kept, grad):
    return (low(grad),)
low.defvjp(low_keep, low_pass)
low_back.defvjp(back_keep, back_low)
EPS = 1e-05
NEG = -1e+30
HIGH = lax.Precision.HIGHEST

def rope_freqs(head_size):
    half_size = head_size // 2
    index = jnp.arange(half_size, dtype=jnp.float32)
    base_freq = jnp.exp(-(2.0 * index / head_size) * math.log(500000.0))
    wavelen = 2.0 * math.pi / base_freq
    smooth = (8192.0 / wavelen - 1.0) / 3.0
    blended = (1.0 - smooth) * base_freq / 32.0 + smooth * base_freq
    return jnp.where(wavelen > 8192.0, base_freq / 32.0, jnp.where(wavelen < 2048.0, base_freq, blended))

def apply_rotary(values, cosine_table, sine_table):
    half_size = values.shape[-1] // 2
    first = values[..., :half_size]
    second = values[..., half_size:]
    return jnp.concatenate([first * cosine_table - second * sine_table, second * cosine_table + first * sine_table], -1)

def matrix_product(left, right):
    return jnp.dot(left, right, precision=HIGH, preferred_element_type=jnp.float32)

def positions(span_order):
    slot_index = jnp.arange(SEQUENCE_LENGTH, dtype=jnp.int32)
    owner_dev = slot_index // TOK_DEV
    inside = slot_index % TOK_DEV
    span_ids = span_order.reshape(-1)[owner_dev * 2 + inside // SPAN]
    return span_ids * SPAN + inside % SPAN

def head_attend(allowed, item):
    query_one, key_one, value_one = item
    scores = low_back(jnp.dot(query_one, key_one.T, precision=HIGH, preferred_element_type=jnp.float32) * (1.0 / math.sqrt(HEAD_WIDTH)))
    scores = jnp.where(allowed, scores, NEG)
    top_score = lax.optimization_barrier(jnp.max(scores, -1, keepdims=True))
    expo = jnp.exp(scores - top_score)
    weights = expo / lax.optimization_barrier(jnp.sum(expo, -1, keepdims=True))
    return jnp.dot(low(weights), value_one, precision=HIGH, preferred_element_type=jnp.float32)

def layer(cosine_table, sine_table, allowed, resid_in, gain_one, query_w, key_matrix, value_matrix, out_w, gain_two, gate_w, up_w, down_w):
    scale_one = lax.rsqrt(lax.optimization_barrier(jnp.mean(resid_in * resid_in, -1, keepdims=True)) + EPS)
    first_normalized = low(resid_in * scale_one * gain_one)
    queries = low(apply_rotary(low_back(matrix_product(first_normalized, query_w)).reshape(SEQUENCE_LENGTH, QUERY_HEADS, HEAD_WIDTH), cosine_table, sine_table))
    rotated_keys = low(apply_rotary(low_back(matrix_product(first_normalized, key_matrix)).reshape(SEQUENCE_LENGTH, KEY_VALUE_HEADS, HEAD_WIDTH), cosine_table, sine_table))
    reduced_values = low(low_back(matrix_product(first_normalized, value_matrix))).reshape(SEQUENCE_LENGTH, KEY_VALUE_HEADS, HEAD_WIDTH)
    query_heads = queries.transpose(1, 0, 2)
    heads_of_key = jnp.repeat(rotated_keys.transpose(1, 0, 2), QUERY_HEADS // KEY_VALUE_HEADS, axis=0)
    heads_of_value = jnp.repeat(reduced_values.transpose(1, 0, 2), QUERY_HEADS // KEY_VALUE_HEADS, axis=0)
    attended = lax.map(jax.checkpoint(partial(head_attend, allowed)), (query_heads, heads_of_key, heads_of_value))
    attended = attended.transpose(1, 0, 2).reshape(SEQUENCE_LENGTH, QUERY_HEADS * HEAD_WIDTH)
    attn_low = low(low_back(attended))
    resid_mid = resid_in + low_back(matrix_product(attn_low, out_w))
    scale_two = lax.rsqrt(lax.optimization_barrier(jnp.mean(resid_mid * resid_mid, -1, keepdims=True)) + EPS)
    normed_two = low(resid_mid * scale_two * gain_two)
    gate_val = low_back(matrix_product(normed_two, gate_w))
    up_val = low_back(matrix_product(normed_two, up_w))
    hidden = low(gate_val * jax.nn.sigmoid(gate_val) * up_val)
    return resid_mid + low_back(matrix_product(hidden, down_w))

def reference(tokens, span_order, attn_gain, w_query, key_weight, value_weight, w_out, mlp_gain, w_gate, w_up, w_down, out_grad):
    pos_int = positions(span_order)
    allowed = pos_int[:, None] >= pos_int[None, :]
    angles = pos_int.astype(jnp.float32)[:, None] * rope_freqs(HEAD_WIDTH)[None, :]
    cosine_table = jnp.cos(angles)[:, None, :]
    sine_table = jnp.sin(angles)[:, None, :]
    params = tuple((weight.astype(jnp.float32) for weight in (attn_gain, w_query, key_weight, value_weight, w_out, mlp_gain, w_gate, w_up, w_down)))
    layer_fn = partial(layer, cosine_table, sine_table, allowed)

    def one_sequence(totals, item):
        seq_in, seq_cot = item
        value_out, pull = jax.vjp(layer_fn, seq_in.astype(jnp.float32), *params)
        grads = pull(seq_cot.astype(jnp.float32))
        totals = tuple((total + grad for total, grad in zip(totals, grads[1:])))
        return (totals, (value_out.astype(jnp.bfloat16), grads[0].astype(jnp.bfloat16)))
    zeros = tuple((jnp.zeros(weight.shape, jnp.float32) for weight in params))
    totals, (outputs, in_grads) = lax.scan(one_sequence, zeros, (tokens, out_grad))
    return (outputs, in_grads, totals[0], totals[1], totals[2], totals[3], totals[4], totals[5], totals[6], totals[7], totals[8])
```

```python
import math

import jax
import jax.numpy as jnp
from jax import lax
from jax.sharding import PartitionSpec as P

HEAD_WIDTH = 64
EPS = 1e-05
NEG = -1e30
BF = jnp.bfloat16
F32 = jnp.float32


def rope_freqs(head_size):
    half_size = head_size // 2
    index = jnp.arange(half_size, dtype=jnp.float32)
    base_freq = jnp.exp(-(2.0 * index / head_size) * math.log(500000.0))
    wavelen = 2.0 * math.pi / base_freq
    smooth = (8192.0 / wavelen - 1.0) / 3.0
    blended = (1.0 - smooth) * base_freq / 32.0 + smooth * base_freq
    return jnp.where(
        wavelen > 8192.0, base_freq / 32.0, jnp.where(wavelen < 2048.0, base_freq, blended)
    )


def apply_rotary(values, cosine_table, sine_table):
    half_size = values.shape[-1] // 2
    first = values[..., :half_size]
    second = values[..., half_size:]
    return jnp.concatenate(
        [first * cosine_table - second * sine_table, second * cosine_table + first * sine_table], -1
    )


def dot(left, right):
    return jnp.dot(left, right, preferred_element_type=F32)


def dot_t(left, right):
    return lax.dot_general(left, right, (((1,), (1,)), ((), ())), preferred_element_type=F32)


def t_dot(left, right):
    return lax.dot_general(left, right, (((0,), (0,)), ((), ())), preferred_element_type=F32)


def pick(blocks, index, axis=0):
    return lax.dynamic_index_in_dim(blocks, index, axis, keepdims=False)


def place(whole, block, starts):
    return lax.dynamic_update_slice(whole, block, starts)


def shards(
    tokens,
    span_order,
    attn_gain,
    w_query,
    key_weight,
    value_weight,
    w_out,
    mlp_gain,
    w_gate,
    w_up,
    w_down,
    out_grad,
):
    planes = lax.axis_size("fsdp")
    contexts = lax.axis_size("context")
    z = lax.axis_index("fsdp")
    c = lax.axis_index("context")
    t = lax.axis_index("tensor")
    outers = contexts // 2
    o, k = c // 2, c % 2

    def swap_t(v):
        return lax.ppermute(v, "tensor", [(0, 1), (1, 0)])

    def swap_k(v):
        return lax.ppermute(v, "context", [(i, i ^ 1) for i in range(contexts)])

    def shift_o(v, by):
        return lax.ppermute(
            v,
            "context",
            [(i, ((i // 2 + by) % outers) * 2 + i % 2) for i in range(contexts)],
        )

    def shift_z(v, by):
        return lax.ppermute(v, "fsdp", [(i, (i + by) % planes) for i in range(planes)])

    def gather_context(piece):
        column = [piece] + [shift_o(piece, by) for by in range(1, outers)]
        other = swap_k(jnp.stack(column))
        found = []
        for by in range(outers):
            home = (o - by + outers) % outers
            found.append((home * 2 + k, column[by]))
            found.append((home * 2 + 1 - k, other[by]))
        return found

    def sum_context(part):
        shape = part.shape
        part = part.reshape(shape[0], outers, 2, *shape[2:])
        got = swap_k(pick(part, 1 - k, 2).astype(BF))
        total = pick(part, k, 2) + got.astype(F32)
        sums = pick(total, o, 1)
        for by in range(1, outers):
            sums = sums + shift_o(pick(total, (o + by) % outers, 1).astype(BF), by).astype(F32)
        return sums

    tok_own, cot_own = tokens[0], out_grad[0]
    rows, own_cols = tok_own.shape
    width = own_cols * 2
    depth = width // planes
    strip = depth // contexts
    units = w_gate.shape[1] // planes
    unit_strip = units // contexts

    def whole_cols(mine, theirs):
        return jnp.concatenate(
            [jnp.where(t == 0, mine, theirs), jnp.where(t == 0, theirs, mine)], -1
        )

    def own_half(v):
        return lax.dynamic_slice_in_dim(v, t * own_cols, own_cols, v.ndim - 1)

    def other_half(v):
        return lax.dynamic_slice_in_dim(v, (1 - t) * own_cols, own_cols, v.ndim - 1)

    resid_in = whole_cols(tok_own, swap_t(tok_own)).astype(F32)
    own_in = tok_own.astype(F32)

    query_cols = w_query.shape[1]
    kv_cols = key_weight.shape[1]
    qkv_own = jnp.concatenate([w_query, key_weight, value_weight], 1)
    qkv_strip = lax.dynamic_slice_in_dim(qkv_own, c * strip, strip, 0)
    out_rows = w_out.shape[0]
    out_strip_rows = out_rows // contexts
    out_strip = lax.dynamic_slice_in_dim(w_out, c * out_strip_rows, out_strip_rows, 0)
    gains_own = jnp.stack([attn_gain, mlp_gain])
    gains = place(jnp.zeros((2, width), BF), gains_own, (0, z * depth))
    qkv_w = place(jnp.zeros((width, qkv_own.shape[1]), BF), qkv_own, (z * depth, 0))
    out_w = place(jnp.zeros((out_rows, width), BF), w_out, (0, z * depth))
    for by in range(1, planes):
        home = (z - by + planes) % planes
        gains = place(gains, shift_z(gains_own, by), (0, home * depth))
        for index, piece in gather_context(shift_z(qkv_strip, by)):
            qkv_w = place(qkv_w, piece, (home * depth + index * strip, 0))
    for by in range(1, planes):
        home = (z - by + planes) % planes
        for index, piece in gather_context(shift_z(out_strip, by)):
            out_w = place(out_w, piece, (index * out_strip_rows, home * depth))
    gain_one, gain_two = gains[0].astype(F32), gains[1].astype(F32)

    cot_blocks = []
    for by in range(planes):
        piece = cot_own if by == 0 else shift_z(cot_own, by)
        cot_blocks.append(whole_cols(piece, swap_t(piece)))

    def unit_cols(v, plane):
        return lax.dynamic_slice_in_dim(v, plane * units, units, 1)

    gate_up = jnp.concatenate([unit_cols(w_gate, z), unit_cols(w_up, z)], 1)
    gate_up_w = place(jnp.zeros((width, 2 * units), BF), gate_up, (z * depth, 0))
    down_w = place(
        jnp.zeros((units, width), BF),
        lax.dynamic_slice_in_dim(w_down, z * units, units, 0),
        (0, z * depth),
    )
    gate_strip = lax.dynamic_slice_in_dim(w_gate, c * strip, strip, 0)
    up_strip = lax.dynamic_slice_in_dim(w_up, c * strip, strip, 0)
    for by in range(1, planes):
        goal = (z + by) % planes
        home = (z - by + planes) % planes
        piece = jnp.concatenate([unit_cols(gate_strip, goal), unit_cols(up_strip, goal)], 1)
        for index, found in gather_context(shift_z(piece, by)):
            gate_up_w = place(gate_up_w, found, (home * depth + index * strip, 0))
    for by in range(1, planes):
        goal = (z + by) % planes
        home = (z - by + planes) % planes
        piece = lax.dynamic_slice_in_dim(w_down, goal * units + c * unit_strip, unit_strip, 0)
        for index, found in gather_context(shift_z(piece, by)):
            down_w = place(down_w, found, (index * unit_strip, home * depth))

    heads_q = query_cols // HEAD_WIDTH
    heads_kv = kv_cols // HEAD_WIDTH
    group_size = heads_q // heads_kv
    half_rows = rows // 2
    scale_one = lax.rsqrt(jnp.mean(resid_in * resid_in, -1, keepdims=True) + EPS)
    first_normalized = (resid_in * scale_one * gain_one).astype(BF)
    qkv_lin = dot(first_normalized, qkv_w)

    slot = jnp.arange(rows, dtype=jnp.int32)

    def positions(index):
        spans = pick(span_order, index)
        return spans[slot // half_rows] * half_rows + slot % half_rows

    pos_mine = positions(c)
    angles = pos_mine.astype(F32)[:, None] * rope_freqs(HEAD_WIDTH)[None, :]
    cosine_table = jnp.cos(angles)[:, None, :]
    sine_table = jnp.sin(angles)[:, None, :]
    factor = 1.0 / math.sqrt(HEAD_WIDTH)
    qk_rot = apply_rotary(
        qkv_lin[:, : query_cols + kv_cols].reshape(rows, heads_q + heads_kv, HEAD_WIDTH),
        cosine_table,
        sine_table,
    ).astype(BF)
    query_rot = qk_rot[:, :heads_q]
    key_value = jnp.concatenate(
        [
            qk_rot[:, heads_q:].reshape(rows, kv_cols),
            qkv_lin[:, query_cols + kv_cols :].astype(BF),
        ],
        1,
    )
    found = gather_context(key_value)
    kv_all = jnp.concatenate([piece for _, piece in found], 0)
    pos_all = jnp.concatenate([positions(index) for index, _ in found], 0)
    seq_len = rows * contexts
    allowed = pos_mine[:, None] >= pos_all[None, :]
    query_heads = query_rot.reshape(rows, heads_kv, group_size, HEAD_WIDTH).transpose(1, 2, 0, 3)
    heads_of_key = kv_all[:, :kv_cols].reshape(seq_len, heads_kv, HEAD_WIDTH).transpose(1, 0, 2)
    heads_of_value = kv_all[:, kv_cols:].reshape(seq_len, heads_kv, HEAD_WIDTH).transpose(1, 0, 2)

    def scores_of(query_block, key_block):
        raw_scores = (
            jnp.einsum("gtd,ld->gtl", query_block, key_block, preferred_element_type=F32) * factor
        )
        return jnp.where(allowed[None], raw_scores, NEG)

    def attend(item):
        query_block, key_block, value_block = item
        scores = scores_of(query_block, key_block)
        top_score = jnp.max(scores, -1, keepdims=True)
        expo = jnp.exp(scores - top_score)
        total = jnp.sum(expo, -1, keepdims=True)
        weights = expo / total
        attended = jnp.einsum(
            "gtl,ld->gtd", weights.astype(BF), value_block, preferred_element_type=F32
        )
        return (attended, top_score + jnp.log(total))

    attended, log_sums = lax.map(attend, (query_heads, heads_of_key, heads_of_value))
    attn_low = attended.transpose(2, 0, 1, 3).reshape(rows, query_cols).astype(BF)
    attn_part = dot(attn_low, out_w)
    mid_own = own_in + own_half(attn_part) + swap_t(other_half(attn_part).astype(BF)).astype(F32)

    def row_total(v):
        part = jnp.sum(v, -1)
        return (part + swap_t(part))[:, None]

    gain_one_own, gain_two_own = own_half(gain_one), own_half(gain_two)
    scale_two = lax.rsqrt(row_total(mid_own * mid_own) / width + EPS)
    normal_two = mid_own * scale_two
    normed_own = (normal_two * gain_two_own).astype(BF)

    normed_blocks, hidden_blocks, unit_grad_blocks = [], [], []
    mlp_sum = None
    normed_grad = None
    for by in range(planes):
        piece = normed_own if by == 0 else shift_z(normed_own, by)
        normed = whole_cols(piece, swap_t(piece))
        cot = cot_blocks[by]
        gate_up_val = dot(normed, gate_up_w)
        gate_val, up_val = gate_up_val[:, :units], gate_up_val[:, units:]
        sigmoid_gate = jax.nn.sigmoid(gate_val)
        hidden = (gate_val * sigmoid_gate * up_val).astype(BF)
        hidden_grad = dot_t(cot, down_w)
        gate_grad = hidden_grad * up_val * sigmoid_gate * (1.0 + gate_val * (1.0 - sigmoid_gate))
        up_grad = hidden_grad * gate_val * sigmoid_gate
        unit_grad = jnp.concatenate([gate_grad.astype(BF), up_grad.astype(BF)], 1)
        normed_part = dot_t(unit_grad, gate_up_w)
        mlp_part = dot(hidden, down_w)
        grad_own = own_half(normed_part) + swap_t(other_half(normed_part).astype(BF)).astype(F32)
        mlp_own = own_half(mlp_part) + swap_t(other_half(mlp_part).astype(BF)).astype(F32)
        if by == 0:
            normed_grad, mlp_sum = grad_own, mlp_own
        else:
            normed_grad = normed_grad + shift_z(grad_own.astype(BF), planes - by).astype(F32)
            mlp_sum = mlp_sum + shift_z(mlp_own.astype(BF), planes - by).astype(F32)
        normed_blocks.append(normed)
        hidden_blocks.append(hidden)
        unit_grad_blocks.append(unit_grad)
    result = (mid_own + mlp_sum).astype(BF)

    normed_all = jnp.concatenate(normed_blocks, 0)
    hidden_all = jnp.concatenate(hidden_blocks, 0)
    unit_grad_all = jnp.concatenate(unit_grad_blocks, 0)
    cot_all = jnp.concatenate(cot_blocks, 0)
    gate_up_grad = t_dot(normed_all, unit_grad_all)
    down_grad = t_dot(hidden_all, cot_all)

    gate_up_sum = sum_context(gate_up_grad.reshape(planes, contexts, strip, 2 * units)).astype(BF)
    gate_strips = jnp.zeros((2, strip, planes * units), BF)
    for by in range(planes):
        home = (z - by + planes) % planes
        block = pick(gate_up_sum, (z + by) % planes)
        piece = block if by == 0 else shift_z(block, by)
        piece = jnp.stack([piece[:, :units], piece[:, units:]])
        gate_strips = place(gate_strips, piece, (0, 0, home * units))
    gate_out = jnp.zeros((depth, planes * units), F32)
    up_out = jnp.zeros((depth, planes * units), F32)
    for index, piece in gather_context(gate_strips):
        gate_out = place(gate_out, piece[0].astype(F32), (index * strip, 0))
        up_out = place(up_out, piece[1].astype(F32), (index * strip, 0))

    down_parts = down_grad.reshape(1, contexts, unit_strip, width)
    down_sum = sum_context(down_parts)[0].astype(BF)
    down_strips = jnp.zeros((planes, unit_strip, depth), BF)
    for by in range(planes):
        home = (z - by + planes) % planes
        block = lax.dynamic_slice_in_dim(down_sum, ((z + by) % planes) * depth, depth, 1)
        piece = block if by == 0 else shift_z(block, by)
        down_strips = place(down_strips, piece[None], (home, 0, 0))
    down_out = jnp.zeros((planes, contexts, unit_strip, depth), F32)
    for index, piece in gather_context(down_strips):
        down_out = place(down_out, piece[:, None].astype(F32), (0, index, 0, 0))
    down_out = down_out.reshape(planes * units, depth)

    def norm_backward(grad_out, normal, scale_row, gain):
        scaled = grad_out * gain
        gain_grad = jnp.sum(grad_out * normal, 0)
        inner = row_total(scaled * normal) / width
        return (gain_grad, scale_row * (scaled - normal * inner))

    gain_two_grad, mid_from_norm = norm_backward(normed_grad, normal_two, scale_two, gain_two_own)
    mid_grad = cot_own.astype(F32) + mid_from_norm
    mid_grad_own = mid_grad.astype(BF)
    mid_grad_low = whole_cols(mid_grad_own, swap_t(mid_grad_own))

    out_w_grad = t_dot(attn_low, mid_grad_low)
    attn_grad_heads = (
        dot_t(mid_grad_low, out_w)
        .astype(BF)
        .reshape(rows, heads_kv, group_size, HEAD_WIDTH)
        .transpose(1, 2, 0, 3)
    )

    def attend_back(item):
        query_block, key_block, value_block, grad_block, log_block = item
        scores = scores_of(query_block, key_block)
        weights = jnp.exp(scores - log_block)
        weight_grad = jnp.einsum(
            "gtd,ld->gtl", grad_block, value_block, preferred_element_type=F32
        )
        value_grad = jnp.einsum(
            "gtl,gtd->ld", weights.astype(BF), grad_block, preferred_element_type=F32
        )
        inner = jnp.sum(weights * weight_grad, -1, keepdims=True)
        score_grad = (weights * (weight_grad - inner)).astype(BF)
        query_grad = (
            jnp.einsum("gtl,ld->gtd", score_grad, key_block, preferred_element_type=F32) * factor
        )
        key_grad = (
            jnp.einsum("gtl,gtd->ld", score_grad, query_block, preferred_element_type=F32) * factor
        )
        return (query_grad, key_grad, value_grad)

    query_grad, key_grad, value_grad = lax.map(
        attend_back, (query_heads, heads_of_key, heads_of_value, attn_grad_heads, log_sums)
    )
    kv_grad = jnp.concatenate(
        [
            key_grad.transpose(1, 0, 2).reshape(seq_len, kv_cols),
            value_grad.transpose(1, 0, 2).reshape(seq_len, kv_cols),
        ],
        1,
    ).reshape(outers, 2, rows, 2 * kv_cols)
    kv_core = kv_grad[:, 0] + swap_k(kv_grad[:, 1].astype(BF)).astype(F32)
    kv_grad_own = kv_core[0]
    for by in range(1, outers):
        kv_grad_own = kv_grad_own + shift_o(kv_core[by].astype(BF), outers - by).astype(F32)
    qk_grad = jnp.concatenate(
        [
            query_grad.transpose(2, 0, 1, 3).reshape(rows, query_cols),
            kv_grad_own[:, :kv_cols],
        ],
        1,
    ).reshape(rows, heads_q + heads_kv, HEAD_WIDTH)
    qk_grad = apply_rotary(qk_grad, cosine_table, -sine_table)
    qkv_grad = jnp.concatenate(
        [qk_grad.reshape(rows, query_cols + kv_cols), kv_grad_own[:, kv_cols:]], 1
    ).astype(BF)
    qkv_w_grad = t_dot(first_normalized, qkv_grad)
    normed_one_part = dot_t(qkv_grad, qkv_w)
    normed_one_grad = own_half(normed_one_part) + swap_t(
        other_half(normed_one_part).astype(BF)
    ).astype(F32)
    gain_one_grad, in_from_norm = norm_backward(
        normed_one_grad, own_in * scale_one, scale_one, gain_one_own
    )
    input_result = (mid_grad + in_from_norm).astype(BF)

    def sum_planes(parts):
        total = pick(parts, z)
        for by in range(1, planes):
            total = total + shift_z(pick(parts, (z + by) % planes).astype(BF), by).astype(F32)
        return total

    out_sum = sum_context(out_w_grad.reshape(1, contexts, out_strip_rows, width))[0]
    out_sum = sum_planes(out_sum.reshape(out_strip_rows, planes, depth).transpose(1, 0, 2))
    out_out = jnp.zeros((out_rows, depth), F32)
    for index, piece in gather_context(out_sum.astype(BF)):
        out_out = place(out_out, piece.astype(F32), (index * out_strip_rows, 0))

    qkv_sum = sum_context(qkv_w_grad.reshape(planes, contexts, strip, -1))
    qkv_sum = sum_planes(qkv_sum)
    qkv_out = jnp.zeros((depth, qkv_own.shape[1]), F32)
    for index, piece in gather_context(qkv_sum.astype(BF)):
        qkv_out = place(qkv_out, piece.astype(F32), (index * strip, 0))

    gain_grads = lax.psum(jnp.stack([gain_one_grad, gain_two_grad]), ("fsdp", "context"))
    gain_all = whole_cols(gain_grads, swap_t(gain_grads))
    gain_out = lax.dynamic_slice_in_dim(gain_all, z * depth, depth, 1)
    return (
        result[None],
        input_result[None],
        gain_out[0],
        qkv_out[:, :query_cols],
        qkv_out[:, query_cols : query_cols + kv_cols],
        qkv_out[:, query_cols + kv_cols :],
        out_out,
        gain_out[1],
        gate_out,
        up_out,
        down_out,
    )


def solution(mesh):
    weight = P("fsdp", "tensor")
    turned = P("tensor", "fsdp")
    block = P("fsdp", "context", "tensor")
    gain = P("fsdp")
    return jax.shard_map(
        shards,
        mesh=mesh,
        in_specs=(
            block, P(), gain, weight, weight, weight, turned, gain, weight, weight, turned, block,
        ),
        out_specs=(
            block, block, gain, weight, weight, weight, turned, gain, weight, weight, turned,
        ),
        check_vma=False,
    )
```

```python
import math

import jax
import jax.numpy as jnp
from jax import lax
from jax.experimental import pallas as pl
from jax.experimental.pallas import tpu as pltpu
from jax.sharding import PartitionSpec as P

HEAD_WIDTH = 64
EPS = 1e-05
NEG = -1e30
BF = jnp.bfloat16
F32 = jnp.float32
LANES = 128
GAIN_ROWS = 16
FACTOR = 1.0 / math.sqrt(HEAD_WIDTH)
VMEM_LIMIT = 60 * 2**20
MESH = pl.DeviceIdType.MESH


def rope_freqs(head_size):
    half_size = head_size // 2
    index = jnp.arange(half_size, dtype=jnp.float32)
    base_freq = jnp.exp(-(2.0 * index / head_size) * math.log(500000.0))
    wavelen = 2.0 * math.pi / base_freq
    smooth = (8192.0 / wavelen - 1.0) / 3.0
    blended = (1.0 - smooth) * base_freq / 32.0 + smooth * base_freq
    return jnp.where(
        wavelen > 8192.0, base_freq / 32.0, jnp.where(wavelen < 2048.0, base_freq, blended)
    )


def apply_rotary(values, cosine_table, sine_table):
    half_size = values.shape[-1] // 2
    first = values[..., :half_size]
    second = values[..., half_size:]
    return jnp.concatenate(
        [first * cosine_table - second * sine_table, second * cosine_table + first * sine_table], -1
    )


def dot(left, right):
    return jnp.dot(left, right, preferred_element_type=F32)


def dot_t(left, right):
    return lax.dot_general(left, right, (((1,), (1,)), ((), ())), preferred_element_type=F32)


def t_dot(left, right):
    return lax.dot_general(left, right, (((0,), (0,)), ((), ())), preferred_element_type=F32)


def pick(blocks, index, axis=0):
    return lax.dynamic_index_in_dim(blocks, index, axis, keepdims=False)


def place(whole, block, starts):
    return lax.dynamic_update_slice(whole, block, starts)


def build_front(planes, contexts, rows, width, query_cols, kv_cols, units):
    outers = contexts // 2
    half = width // 2
    depth = width // planes
    strip = depth // contexts
    out_strip = query_cols // contexts
    unit_strip = units // contexts
    seq_len = rows * contexts
    n_q, n_kv = query_cols // LANES, kv_cols // LANES
    heads = query_cols // HEAD_WIDTH
    group = query_cols // kv_cols
    qkv_cols = query_cols + 2 * kv_cols
    QKV, OUT, GATE, UP, DOWN, COT, NORM, GAIN = range(8)

    def kernel(
        tok, cot, gains_own, qkv_own, out_own, gate_own, up_own, down_own, cosine, sine, pos_q, pos_k,
        gate_w, up_w, down_w, cot_all, norm_all, qkv_w, out_w, gains, q_pad, kv_all, attn, log_sum,
        mid_own, normed_one, tok_all,
        lin, heads_out, send_half, recv_half, norm_own, sq_send, sq_recv,
        z_send, z_recv, y_send, y_recv, k_send, k_recv, x_send, x_recv, own_sem,
    ):
        z = lax.axis_index("fsdp")
        c = lax.axis_index("context")
        t = lax.axis_index("tensor")
        o, k = c // 2, c % 2

        def at_z(p):
            return (p, c, t)

        def at_o(other):
            return (z, other * 2 + k, t)

        at_k = (z, o * 2 + 1 - k, t)
        at_x = (z, c, 1 - t)

        def copy(src, dst, send_sem, recv_sem, device):
            return pltpu.make_async_remote_copy(
                src_ref=src, dst_ref=dst, send_sem=send_sem, recv_sem=recv_sem,
                device_id=device, device_id_type=MESH,
            )

        barrier = pltpu.get_barrier_semaphore()
        peers = [at_z(lax.rem(z + s, planes)) for s in range(1, planes)]
        peers += [at_o(lax.rem(o + s, outers)) for s in range(1, outers)] + [at_k, at_x]
        for peer in peers:
            pl.semaphore_signal(barrier, inc=1, device_id=peer, device_id_type=MESH)
        pl.semaphore_wait(barrier, len(peers))

        order = []
        for i in range(planes - 1):
            p = jnp.int32(0)
            for plane in range(planes):
                far = sorted((abs(q - plane), q) for q in range(planes) if q != plane)
                p = p + jnp.where(z == plane, far[i][1], 0)
            order.append(p)

        def slot(item, p, q):
            if item == QKV:
                return qkv_w.at[pl.ds(p * depth + q * strip, strip), :]
            if item == OUT:
                return out_w.at[pl.ds(q * out_strip, out_strip), pl.ds(p * depth, depth)]
            if item == GATE:
                return gate_w.at[pl.ds(p * depth + q * strip, strip), :]
            if item == UP:
                return up_w.at[pl.ds(p * depth + q * strip, strip), :]
            if item == DOWN:
                return down_w.at[pl.ds(q * unit_strip, unit_strip), pl.ds(p * depth, depth)]
            if item == COT:
                return cot_all.at[p, :, pl.ds(t * half, half)]
            return norm_all.at[p, :, pl.ds(t * half, half)]

        def z_copy(item, p, src, goal, way):
            return copy(src, slot(item, p, c), z_send.at[item, p, way], z_recv.at[item, p], at_z(goal))

        def z_wait(item, p):
            z_copy(item, p, slot(item, p, c), z, 0).wait_recv()

        def spread(item, src):
            @pl.when(z + 1 < planes)
            def _():
                z_copy(item, z, src, z + 1, 0).start()

            @pl.when(z > 0)
            def _():
                z_copy(item, z, src, z - 1, 1).start()

        def spread_done(item, src):
            @pl.when(z + 1 < planes)
            def _():
                z_copy(item, z, src, z + 1, 0).wait_send()

            @pl.when(z > 0)
            def _():
                z_copy(item, z, src, z - 1, 1).wait_send()

        def passes_on(p):
            return ((p < z) & (z + 1 < planes)) | ((p > z) & (z > 0))

        def onward(p):
            return jnp.where(p < z, z + 1, z - 1)

        def forward(item, p):
            @pl.when(passes_on(p))
            def _():
                z_copy(item, p, slot(item, p, c), onward(p), 0).start()

        def forward_done(item, p):
            @pl.when(passes_on(p))
            def _():
                z_copy(item, p, slot(item, p, c), onward(p), 0).wait_send()

        def y_copy(item, p, by):
            here = slot(item, p, c)
            return copy(here, here, y_send.at[item, p, by], y_recv.at[item, p, by], at_o(lax.rem(o + by, outers)))

        def y_wait(item, p, by):
            there = slot(item, p, lax.rem(o - by + outers, outers) * 2 + k)
            copy(there, there, y_send.at[item, p, by], y_recv.at[item, p, by], at_k).wait_recv()

        def k_copy(item, p, by):
            here = slot(item, p, lax.rem(o - by + outers, outers) * 2 + k)
            return copy(here, here, k_send.at[item, p, by], k_recv.at[item, p, by], at_k)

        def k_wait(item, p, by):
            there = slot(item, p, lax.rem(o - by + outers, outers) * 2 + 1 - k)
            copy(there, there, k_send.at[item, p, by], k_recv.at[item, p, by], at_k).wait_recv()

        def share(item, p):
            for by in range(1, outers):
                y_copy(item, p, by).start()
            k_copy(item, p, 0).start()

        def share_on(item, p):
            for by in range(1, outers):
                y_wait(item, p, by)
                k_copy(item, p, by).start()

        def shared(item, p):
            for by in range(outers):
                k_wait(item, p, by)

        def share_done(item, p):
            for by in range(1, outers):
                y_copy(item, p, by).wait_send()
            for by in range(outers):
                k_copy(item, p, by).wait_send()

        def x_copy(i, src, dst):
            return copy(src, dst, x_send.at[i], x_recv.at[i], at_x)

        tok_cols = pl.ds(t * half, half)
        tok_copy = x_copy(0, tok, tok_all.at[:, tok_cols])
        tok_copy.start()
        gain_copies = [
            copy(
                gains_own, gains.at[:, pl.ds(z * depth, depth)], z_send.at[GAIN, lax.rem(z + s, planes), 0],
                z_recv.at[GAIN, z], at_z(lax.rem(z + s, planes)),
            )
            for s in range(1, planes)
        ]
        for one in gain_copies:
            one.start()
        qkv_src = qkv_own.at[pl.ds(c * strip, strip), :]
        out_src = out_own.at[pl.ds(c * out_strip, out_strip), :]
        spread(QKV, qkv_src)
        own_copies = [
            pltpu.make_async_copy(qkv_own, qkv_w.at[pl.ds(z * depth, depth), :], own_sem.at[0]),
            pltpu.make_async_copy(out_own, out_w.at[:, pl.ds(z * depth, depth)], own_sem.at[1]),
            pltpu.make_async_copy(
                gate_own.at[:, pl.ds(z * units, units)], gate_w.at[pl.ds(z * depth, depth), :], own_sem.at[2]
            ),
            pltpu.make_async_copy(
                up_own.at[:, pl.ds(z * units, units)], up_w.at[pl.ds(z * depth, depth), :], own_sem.at[3]
            ),
            pltpu.make_async_copy(
                down_own.at[pl.ds(z * units, units), :], down_w.at[:, pl.ds(z * depth, depth)], own_sem.at[4]
            ),
            pltpu.make_async_copy(cot, slot(COT, z, c), own_sem.at[5]),
        ]
        for one in own_copies:
            one.start()
        gains[:, pl.ds(z * depth, depth)] = gains_own[...]
        tok_all[:, tok_cols] = tok[...]

        tok_copy.wait()
        for s in range(1, planes):
            p = lax.rem(z + s, planes)
            there = gains.at[:, pl.ds(p * depth, depth)]
            copy(there, there, z_send.at[GAIN, p, 0], z_recv.at[GAIN, p], at_k).wait_recv()
        x = tok_all[...].astype(F32)
        scale = lax.rsqrt(jnp.mean(x * x, -1, keepdims=True) + EPS)
        normed_one[...] = (x * scale * gains[0:1, :].astype(F32)).astype(BF)

        for p in order:
            z_wait(QKV, p)
            forward(QKV, p)
            share(QKV, p)

        spread(OUT, out_src)
        sends = []
        for s in range(1, planes):
            goal = lax.rem(z + s, planes)
            cols = pl.ds(goal * units, units)
            sends += [
                z_copy(GATE, z, gate_own.at[pl.ds(c * strip, strip), cols], goal, s - 1),
                z_copy(UP, z, up_own.at[pl.ds(c * strip, strip), cols], goal, s - 1),
                z_copy(
                    DOWN, z, down_own.at[pl.ds(goal * units + c * unit_strip, unit_strip), :], goal, s - 1
                ),
            ]
        for one in sends:
            one.start()
        spread(COT, cot)
        cot_copy = x_copy(1 + z, cot, slot(COT, z, c))
        cot_copy.start()

        for p in order:
            share_on(QKV, p)
        for p in order:
            shared(QKV, p)
        own_copies[0].wait()

        n_tile = 2 * LANES

        @pl.loop(0, qkv_cols // n_tile)
        def _(i):
            cols = pl.ds(pl.multiple_of(i * n_tile, n_tile), n_tile)
            found = jnp.dot(normed_one[...], qkv_w[:, cols], preferred_element_type=F32)
            lin[2 * i] = found[:, :LANES]
            lin[2 * i + 1] = found[:, LANES:]

        lane = lax.broadcasted_iota(jnp.int32, (rows, LANES), 1)
        first = lax.rem(lane, HEAD_WIDTH) < HEAD_WIDTH // 2
        low = lane < HEAD_WIDTH

        def rotated(u):
            partner = jnp.where(
                first, pltpu.roll(u, LANES - HEAD_WIDTH // 2, 1), pltpu.roll(u, HEAD_WIDTH // 2, 1)
            )
            return u * cosine[...] + partner * sine[...]

        for i in range(n_kv):
            kv_all[c, i] = rotated(lin[n_q + i]).astype(BF)
            kv_all[c, n_kv + i] = lin[n_q + n_kv + i].astype(BF)

        def kv_slot(q):
            return kv_all.at[q]

        kv_sends = [
            copy(kv_slot(c), kv_slot(c), y_send.at[COT, 0, by], y_recv.at[COT, 0, by], at_o(lax.rem(o + by, outers)))
            for by in range(1, outers)
        ]
        kv_sends.append(copy(kv_slot(c), kv_slot(c), k_send.at[COT, 0, 0], k_recv.at[COT, 0, 0], at_k))
        for one in kv_sends:
            one.start()

        @pl.loop(0, n_q)
        def _(j):
            u = rotated(lin[j]).astype(BF).astype(F32) * FACTOR
            side = lax.rem((2 * j) // group, 2)
            lo = jnp.where(low, u, 0.0)
            hi = jnp.where(low, 0.0, u)
            q_pad[2 * j] = jnp.where(side == 0, lo, pltpu.roll(lo, HEAD_WIDTH, 1)).astype(BF)
            q_pad[2 * j + 1] = jnp.where(side == 1, hi, pltpu.roll(hi, HEAD_WIDTH, 1)).astype(BF)

        for by in range(1, outers):
            q = lax.rem(o - by + outers, outers) * 2 + k
            copy(kv_slot(q), kv_slot(q), y_send.at[COT, 0, by], y_recv.at[COT, 0, by], at_k).wait_recv()
            one = copy(kv_slot(q), kv_slot(q), k_send.at[COT, 0, by], k_recv.at[COT, 0, by], at_k)
            one.start()
            kv_sends.append(one)
        for by in range(outers):
            q = lax.rem(o - by + outers, outers) * 2 + 1 - k
            copy(kv_slot(q), kv_slot(q), k_send.at[COT, 0, by], k_recv.at[COT, 0, by], at_k).wait_recv()

        for p in order:
            z_wait(OUT, p)
            forward(OUT, p)
            share(OUT, p)

        def attend(first_head, last_head):
            @pl.loop(first_head, last_head)
            def _(h):
                pair = h // (2 * group)
                keys = kv_all[:, pair].reshape(seq_len, LANES)
                values = kv_all[:, n_kv + pair].reshape(seq_len, LANES)
                scores = dot_t(keys, q_pad[h])
                scores = jnp.where(pos_q[0:1, :] >= pos_k[...], scores, NEG)
                top = jnp.max(scores, 0, keepdims=True)
                expo = jnp.exp(scores - top)
                total = jnp.sum(expo, 0, keepdims=True)
                weights = (expo * (1.0 / total)).astype(BF)
                heads_out[h] = t_dot(values, weights).T
                log_sum[pl.ds(h, 1), :] = top + jnp.log(total)

        attend(0, heads // 2)
        for p in order:
            share_on(OUT, p)
        for p in order:
            z_wait(COT, p)
            forward(COT, p)
            x_copy(1 + p, slot(COT, p, c), slot(COT, p, c)).start()
        attend(heads // 2, heads)

        for j in range(n_q):
            side = (2 * j) // group % 2
            lo, hi = heads_out[2 * j], heads_out[2 * j + 1]
            if side == 0:
                hi = pltpu.roll(hi, HEAD_WIDTH, 1)
            else:
                lo = pltpu.roll(lo, HEAD_WIDTH, 1)
            attn[:, j * LANES : (j + 1) * LANES] = jnp.where(low, lo, hi).astype(BF)

        for p in order:
            shared(OUT, p)
        own_copies[1].wait()

        n_out = half // n_tile

        @pl.loop(0, n_out)
        def _(i):
            cols = pl.ds(pl.multiple_of((1 - t) * half + i * n_tile, n_tile), n_tile)
            here = pl.ds(pl.multiple_of(i * n_tile, n_tile), n_tile)
            send_half[:, here] = jnp.dot(attn[...], out_w[:, cols], preferred_element_type=F32).astype(BF)

        half_copy = x_copy(1 + planes, send_half, recv_half)
        half_copy.start()

        @pl.loop(0, n_out)
        def _(i):
            cols = pl.ds(pl.multiple_of(t * half + i * n_tile, n_tile), n_tile)
            here = pl.ds(pl.multiple_of(i * n_tile, n_tile), n_tile)
            part = jnp.dot(attn[...], out_w[:, cols], preferred_element_type=F32)
            mid_own[:, here] = tok[:, here].astype(F32) + part

        half_copy.wait_recv()
        mid = mid_own[...] + recv_half[...].astype(F32)
        mid_own[...] = mid
        squares = jnp.sum(mid * mid, -1, keepdims=True)
        sq_send[...] = jnp.broadcast_to(squares, (rows, LANES))
        sq_copy = x_copy(2 + planes, sq_send, sq_recv)
        sq_copy.start()
        sq_copy.wait_recv()
        scale_two = lax.rsqrt((squares + sq_recv[:, 0:1]) * (1.0 / width) + EPS)
        gain_two = gains[1:2, pl.ds(pl.multiple_of(t * half, half), half)].astype(F32)
        norm_own[...] = (mid_own[...] * scale_two * gain_two).astype(BF)

        spread(NORM, norm_own)
        norm_copy = x_copy(3 + planes + z, norm_own, slot(NORM, z, c))
        norm_copy.start()
        norm_keep = pltpu.make_async_copy(norm_own, slot(NORM, z, c), own_sem.at[6])
        norm_keep.start()
        items = (GATE, UP, DOWN)
        for s in range(1, planes):
            p = lax.rem(z + planes - s, planes)
            for item in items:
                z_wait(item, p)
                share(item, p)
        for i, p in enumerate(order):
            z_wait(NORM, p)
            forward(NORM, p)
            x_copy(3 + planes + p, slot(NORM, p, c), slot(NORM, p, c)).start()
            for item in items:
                share_on(item, lax.rem(z + planes - 1 - i, planes))

        for s in range(1, planes):
            p = lax.rem(z + s, planes)
            for item in items:
                shared(item, p)
        for p in [z] + order:
            for base, item in ((1, COT), (3 + planes, NORM)):
                there = (cot_all if item == COT else norm_all).at[p, :, pl.ds((1 - t) * half, half)]
                copy(there, there, x_send.at[base + p], x_recv.at[base + p], at_x).wait_recv()
        for one in own_copies[2:]:
            one.wait()
        norm_keep.wait()
        tok_copy_out = [half_copy, sq_copy, cot_copy, norm_copy]
        for one in gain_copies + sends + kv_sends + tok_copy_out:
            one.wait_send()
        spread_done(QKV, qkv_src)
        spread_done(OUT, out_src)
        spread_done(COT, cot)
        spread_done(NORM, norm_own)
        for p in order:
            for item in (QKV, OUT, COT, NORM):
                forward_done(item, p)
            for item in (QKV, OUT, GATE, UP, DOWN):
                share_done(item, p)
            x_copy(1 + p, slot(COT, p, c), slot(COT, p, c)).wait_send()
            x_copy(3 + planes + p, slot(NORM, p, c), slot(NORM, p, c)).wait_send()

    hbm = pl.BlockSpec(memory_space=pl.ANY)
    vmem = pl.BlockSpec(memory_space=pltpu.VMEM)
    dma = pltpu.SemaphoreType.DMA
    shape = jax.ShapeDtypeStruct
    return pl.pallas_call(
        kernel,
        name="front",
        out_shape=(
            shape((width, units), BF),
            shape((width, units), BF),
            shape((units, width), BF),
            shape((planes, rows, width), BF),
            shape((planes, rows, width), BF),
            shape((width, qkv_cols), BF),
            shape((query_cols, width), BF),
            shape((GAIN_ROWS, width), BF),
            shape((heads, rows, LANES), BF),
            shape((contexts, 2 * n_kv, rows, LANES), BF),
            shape((rows, query_cols), BF),
            shape((heads, rows), F32),
            shape((rows, half), F32),
            shape((rows, width), BF),
            shape((rows, width), BF),
        ),
        in_specs=[vmem, hbm, vmem, hbm, hbm, hbm, hbm, hbm, vmem, vmem, vmem, vmem],
        out_specs=(hbm,) * 5 + (vmem,) * 10,
        scratch_shapes=[
            pltpu.VMEM((qkv_cols // LANES, rows, LANES), F32),
            pltpu.VMEM((heads, rows, LANES), F32),
            pltpu.VMEM((rows, half), BF),
            pltpu.VMEM((rows, half), BF),
            pltpu.VMEM((rows, half), BF),
            pltpu.VMEM((rows, LANES), F32),
            pltpu.VMEM((rows, LANES), F32),
            dma((8, planes, planes)),
            dma((8, planes)),
            dma((6, planes, max(outers, 2))),
            dma((6, planes, max(outers, 2))),
            dma((6, planes, max(outers, 2))),
            dma((6, planes, max(outers, 2))),
            dma((3 + 2 * planes,)),
            dma((3 + 2 * planes,)),
            dma((8,)),
        ],
        compiler_params=pltpu.CompilerParams(
            collective_id=0, has_side_effects=True, vmem_limit_bytes=VMEM_LIMIT
        ),
        cost_estimate=pl.CostEstimate(flops=8 * 10**9, bytes_accessed=80 * 10**6, transcendentals=4 * 10**6),
    )


def build_attend_back(contexts, rows, query_cols, kv_cols):
    seq_len = rows * contexts
    n_q, n_kv = query_cols // LANES, kv_cols // LANES
    heads = query_cols // HEAD_WIDTH
    group = query_cols // kv_cols

    def kernel(
        q_pad, kv_all, attn_grad, log_sum, cosine, sine, pos_q, pos_k, query_grad, kv_grad,
        grad_pad, query_out, key_sum, value_sum,
    ):
        lane = lax.broadcasted_iota(jnp.int32, (rows, LANES), 1)
        first = lax.rem(lane, HEAD_WIDTH) < HEAD_WIDTH // 2
        low = lane < HEAD_WIDTH
        for j in range(n_q):
            u = attn_grad[:, j * LANES : (j + 1) * LANES].astype(F32)
            side = (2 * j) // group % 2
            lo = jnp.where(low, u, 0.0)
            hi = jnp.where(low, 0.0, u)
            if side == 0:
                hi = pltpu.roll(hi, HEAD_WIDTH, 1)
            else:
                lo = pltpu.roll(lo, HEAD_WIDTH, 1)
            grad_pad[2 * j] = lo.astype(BF)
            grad_pad[2 * j + 1] = hi.astype(BF)
        key_sum[...] = jnp.zeros_like(key_sum)
        value_sum[...] = jnp.zeros_like(value_sum)

        @pl.loop(0, heads)
        def _(h):
            pair = h // (2 * group)
            keys = kv_all[:, pair].reshape(seq_len, LANES)
            values = kv_all[:, n_kv + pair].reshape(seq_len, LANES)
            scores = dot_t(keys, q_pad[h])
            scores = jnp.where(pos_q[0:1, :] >= pos_k[...], scores, NEG)
            weights = jnp.exp(scores - log_sum[pl.ds(h, 1), :])
            weight_grad = dot_t(values, grad_pad[h])
            inner = jnp.sum(weights * weight_grad, 0, keepdims=True)
            score_grad = (weights * (weight_grad - inner)).astype(BF)
            value_sum[pair] += jnp.dot(weights.astype(BF), grad_pad[h], preferred_element_type=F32)
            key_sum[pair] += jnp.dot(score_grad, q_pad[h], preferred_element_type=F32)
            query_out[h] = t_dot(keys, score_grad).T

        for j in range(n_q):
            side = (2 * j) // group % 2
            lo, hi = query_out[2 * j], query_out[2 * j + 1]
            if side == 0:
                hi = pltpu.roll(hi, HEAD_WIDTH, 1)
            else:
                lo = pltpu.roll(lo, HEAD_WIDTH, 1)
            u = jnp.where(low, lo, hi) * FACTOR
            partner = jnp.where(
                first, pltpu.roll(u, LANES - HEAD_WIDTH // 2, 1), pltpu.roll(u, HEAD_WIDTH // 2, 1)
            )
            turned = u * cosine[...] - partner * sine[...]
            query_grad[:, j * LANES : (j + 1) * LANES] = turned.astype(BF)
        for i in range(n_kv):
            kv_grad[:, i] = key_sum[i].astype(BF).reshape(contexts, rows, LANES)
            kv_grad[:, n_kv + i] = value_sum[i].astype(BF).reshape(contexts, rows, LANES)

    vmem = pl.BlockSpec(memory_space=pltpu.VMEM)
    return pl.pallas_call(
        kernel,
        name="attend_back",
        out_shape=(
            jax.ShapeDtypeStruct((rows, query_cols), BF),
            jax.ShapeDtypeStruct((contexts, 2 * n_kv, rows, LANES), BF),
        ),
        in_specs=[vmem] * 8,
        out_specs=(vmem, vmem),
        scratch_shapes=[
            pltpu.VMEM((heads, rows, LANES), BF),
            pltpu.VMEM((heads, rows, LANES), F32),
            pltpu.VMEM((n_kv, seq_len, LANES), F32),
            pltpu.VMEM((n_kv, seq_len, LANES), F32),
        ],
        compiler_params=pltpu.CompilerParams(vmem_limit_bytes=VMEM_LIMIT),
        cost_estimate=pl.CostEstimate(
            flops=10 * heads * rows * seq_len * LANES, bytes_accessed=8 * 10**6,
            transcendentals=heads * rows * seq_len,
        ),
    )


def shards(
    tokens,
    span_order,
    attn_gain,
    w_query,
    key_weight,
    value_weight,
    w_out,
    mlp_gain,
    w_gate,
    w_up,
    w_down,
    out_grad,
):
    planes = lax.axis_size("fsdp")
    contexts = lax.axis_size("context")
    z = lax.axis_index("fsdp")
    c = lax.axis_index("context")
    t = lax.axis_index("tensor")
    outers = contexts // 2
    o, k = c // 2, c % 2

    def swap_t(v):
        return lax.ppermute(v, "tensor", [(0, 1), (1, 0)])

    def swap_k(v):
        return lax.ppermute(v, "context", [(i, i ^ 1) for i in range(contexts)])

    def shift_o(v, by):
        return lax.ppermute(
            v,
            "context",
            [(i, ((i // 2 + by) % outers) * 2 + i % 2) for i in range(contexts)],
        )

    def shift_z(v, by):
        return lax.ppermute(v, "fsdp", [(i, (i + by) % planes) for i in range(planes)])

    def gather_context(piece):
        column = [piece] + [shift_o(piece, by) for by in range(1, outers)]
        other = swap_k(jnp.stack(column))
        found = []
        for by in range(outers):
            home = (o - by + outers) % outers
            found.append((home * 2 + k, column[by]))
            found.append((home * 2 + 1 - k, other[by]))
        return found

    def sum_context(part):
        shape = part.shape
        part = part.reshape(shape[0], outers, 2, *shape[2:])
        got = swap_k(pick(part, 1 - k, 2).astype(BF))
        total = pick(part, k, 2) + got.astype(F32)
        sums = pick(total, o, 1)
        for by in range(1, outers):
            sums = sums + shift_o(pick(total, (o + by) % outers, 1).astype(BF), by).astype(F32)
        return sums

    tok_own, cot_own = tokens[0], out_grad[0]
    rows, own_cols = tok_own.shape
    width = own_cols * 2
    depth = width // planes
    strip = depth // contexts
    units = w_gate.shape[1] // planes
    unit_strip = units // contexts

    def whole_cols(mine, theirs):
        return jnp.concatenate(
            [jnp.where(t == 0, mine, theirs), jnp.where(t == 0, theirs, mine)], -1
        )

    def own_half(v):
        return lax.dynamic_slice_in_dim(v, t * own_cols, own_cols, v.ndim - 1)

    def other_half(v):
        return lax.dynamic_slice_in_dim(v, (1 - t) * own_cols, own_cols, v.ndim - 1)

    query_cols = w_query.shape[1]
    kv_cols = key_weight.shape[1]
    half_rows = rows // 2
    slot = jnp.arange(rows, dtype=jnp.int32)

    def positions(index):
        spans = pick(span_order, index)
        return spans[slot // half_rows] * half_rows + slot % half_rows

    pos_mine = positions(c)
    pos_q = jnp.broadcast_to(pos_mine[None, :], (8, rows))
    pos_k = jnp.concatenate([positions(i) for i in range(contexts)])[:, None]
    angles = pos_mine.astype(F32)[:, None] * rope_freqs(HEAD_WIDTH)[None, :]
    cosine, sine = jnp.cos(angles), jnp.sin(angles)
    cosine_table = jnp.concatenate([cosine] * 4, 1)
    sine_table = jnp.concatenate([-sine, sine] * 2, 1)

    own_in = tok_own.astype(F32)
    qkv_own = jnp.concatenate([w_query, key_weight, value_weight], 1)
    gains_own = jnp.concatenate(
        [attn_gain[None], mlp_gain[None], jnp.zeros((GAIN_ROWS - 2, depth), BF)], 0
    )
    front = build_front(planes, contexts, rows, width, query_cols, kv_cols, units)
    (
        gate_w, up_w, down_w, cot_all, norm_all, qkv_w, out_w, gains, q_pad, kv_all, attn_low, log_sum,
        mid_own, first_normalized, resid_low,
    ) = front(
        tok_own, cot_own, gains_own, qkv_own, w_out, w_gate, w_up, w_down, cosine_table, sine_table,
        pos_q, pos_k,
    )
    gain_one, gain_two = gains[0].astype(F32), gains[1].astype(F32)
    resid_in = resid_low.astype(F32)
    scale_one = lax.rsqrt(jnp.mean(resid_in * resid_in, -1, keepdims=True) + EPS)

    def row_total(v):
        part = jnp.sum(v, -1)
        return (part + swap_t(part))[:, None]

    gain_one_own, gain_two_own = own_half(gain_one), own_half(gain_two)
    scale_two = lax.rsqrt(row_total(mid_own * mid_own) / width + EPS)
    normal_two = mid_own * scale_two

    normed_blocks, cot_blocks, hidden_blocks, unit_grad_blocks = [], [], [], []
    mlp_sum = None
    normed_grad = None
    for by in range(planes):
        home = (z - by + planes) % planes
        normed = pick(norm_all, home)
        cot = pick(cot_all, home)
        gate_val, up_val = dot(normed, gate_w), dot(normed, up_w)
        sigmoid_gate = jax.nn.sigmoid(gate_val)
        hidden = (gate_val * sigmoid_gate * up_val).astype(BF)
        hidden_grad = dot_t(cot, down_w)
        gate_grad = hidden_grad * up_val * sigmoid_gate * (1.0 + gate_val * (1.0 - sigmoid_gate))
        up_grad = hidden_grad * gate_val * sigmoid_gate
        gate_grad, up_grad = gate_grad.astype(BF), up_grad.astype(BF)
        unit_grad = jnp.concatenate([gate_grad, up_grad], 1)
        normed_part = dot_t(gate_grad, gate_w) + dot_t(up_grad, up_w)
        mlp_part = dot(hidden, down_w)
        grad_own = own_half(normed_part) + swap_t(other_half(normed_part).astype(BF)).astype(F32)
        mlp_own = own_half(mlp_part) + swap_t(other_half(mlp_part).astype(BF)).astype(F32)
        if by == 0:
            normed_grad, mlp_sum = grad_own, mlp_own
        else:
            normed_grad = normed_grad + shift_z(grad_own.astype(BF), planes - by).astype(F32)
            mlp_sum = mlp_sum + shift_z(mlp_own.astype(BF), planes - by).astype(F32)
        normed_blocks.append(normed)
        cot_blocks.append(cot)
        hidden_blocks.append(hidden)
        unit_grad_blocks.append(unit_grad)
    result = (mid_own + mlp_sum).astype(BF)

    normed_all = jnp.concatenate(normed_blocks, 0)
    hidden_all = jnp.concatenate(hidden_blocks, 0)
    unit_grad_all = jnp.concatenate(unit_grad_blocks, 0)
    cot_all = jnp.concatenate(cot_blocks, 0)
    gate_up_grad = t_dot(normed_all, unit_grad_all)
    down_grad = t_dot(hidden_all, cot_all)

    gate_up_sum = sum_context(gate_up_grad.reshape(planes, contexts, strip, 2 * units)).astype(BF)
    gate_strips = jnp.zeros((2, strip, planes * units), BF)
    for by in range(planes):
        home = (z - by + planes) % planes
        block = pick(gate_up_sum, (z + by) % planes)
        piece = block if by == 0 else shift_z(block, by)
        piece = jnp.stack([piece[:, :units], piece[:, units:]])
        gate_strips = place(gate_strips, piece, (0, 0, home * units))
    gate_out = jnp.zeros((depth, planes * units), F32)
    up_out = jnp.zeros((depth, planes * units), F32)
    for index, piece in gather_context(gate_strips):
        gate_out = place(gate_out, piece[0].astype(F32), (index * strip, 0))
        up_out = place(up_out, piece[1].astype(F32), (index * strip, 0))

    down_parts = down_grad.reshape(1, contexts, unit_strip, width)
    down_sum = sum_context(down_parts)[0].astype(BF)
    down_strips = jnp.zeros((planes, unit_strip, depth), BF)
    for by in range(planes):
        home = (z - by + planes) % planes
        block = lax.dynamic_slice_in_dim(down_sum, ((z + by) % planes) * depth, depth, 1)
        piece = block if by == 0 else shift_z(block, by)
        down_strips = place(down_strips, piece[None], (home, 0, 0))
    down_out = jnp.zeros((planes, contexts, unit_strip, depth), F32)
    for index, piece in gather_context(down_strips):
        down_out = place(down_out, piece[:, None].astype(F32), (0, index, 0, 0))
    down_out = down_out.reshape(planes * units, depth)

    def norm_backward(grad_out, normal, scale_row, gain):
        scaled = grad_out * gain
        gain_grad = jnp.sum(grad_out * normal, 0)
        inner = row_total(scaled * normal) / width
        return (gain_grad, scale_row * (scaled - normal * inner))

    gain_two_grad, mid_from_norm = norm_backward(normed_grad, normal_two, scale_two, gain_two_own)
    mid_grad = cot_own.astype(F32) + mid_from_norm
    mid_grad_own = mid_grad.astype(BF)
    mid_grad_low = whole_cols(mid_grad_own, swap_t(mid_grad_own))

    out_w_grad = t_dot(attn_low, mid_grad_low)
    attn_grad = dot_t(mid_grad_low, out_w).astype(BF)
    query_grad, kv_grad = build_attend_back(contexts, rows, query_cols, kv_cols)(
        q_pad, kv_all, attn_grad, log_sum, cosine_table, sine_table, pos_q, pos_k
    )
    kv_sum = sum_context(kv_grad[None].astype(F32))[0]
    n_kv = kv_cols // LANES
    key_grad = apply_rotary(
        kv_sum[:n_kv].reshape(n_kv, rows, 2, HEAD_WIDTH), cosine[:, None, :], -sine[:, None, :]
    )
    kv_tiles = jnp.concatenate([key_grad.reshape(n_kv, rows, LANES), kv_sum[n_kv:]], 0)
    qkv_grad = jnp.concatenate(
        [query_grad, kv_tiles.transpose(1, 0, 2).reshape(rows, 2 * kv_cols).astype(BF)], 1
    )
    qkv_w_grad = t_dot(first_normalized, qkv_grad)
    normed_one_part = dot_t(qkv_grad, qkv_w)
    normed_one_grad = own_half(normed_one_part) + swap_t(
        other_half(normed_one_part).astype(BF)
    ).astype(F32)
    gain_one_grad, in_from_norm = norm_backward(
        normed_one_grad, own_in * scale_one, scale_one, gain_one_own
    )
    input_result = (mid_grad + in_from_norm).astype(BF)

    def sum_planes(parts):
        total = pick(parts, z)
        for by in range(1, planes):
            total = total + shift_z(pick(parts, (z + by) % planes).astype(BF), by).astype(F32)
        return total

    out_rows = w_out.shape[0]
    out_strip_rows = out_rows // contexts
    out_sum = sum_context(out_w_grad.reshape(1, contexts, out_strip_rows, width))[0]
    out_sum = sum_planes(out_sum.reshape(out_strip_rows, planes, depth).transpose(1, 0, 2))
    out_out = jnp.zeros((out_rows, depth), F32)
    for index, piece in gather_context(out_sum.astype(BF)):
        out_out = place(out_out, piece.astype(F32), (index * out_strip_rows, 0))

    qkv_sum = sum_context(qkv_w_grad.reshape(planes, contexts, strip, -1))
    qkv_sum = sum_planes(qkv_sum)
    qkv_out = jnp.zeros((depth, qkv_own.shape[1]), F32)
    for index, piece in gather_context(qkv_sum.astype(BF)):
        qkv_out = place(qkv_out, piece.astype(F32), (index * strip, 0))

    gain_grads = lax.psum(jnp.stack([gain_one_grad, gain_two_grad]), ("fsdp", "context"))
    gain_all = whole_cols(gain_grads, swap_t(gain_grads))
    gain_out = lax.dynamic_slice_in_dim(gain_all, z * depth, depth, 1)
    return (
        result[None],
        input_result[None],
        gain_out[0],
        qkv_out[:, :query_cols],
        qkv_out[:, query_cols : query_cols + kv_cols],
        qkv_out[:, query_cols + kv_cols :],
        out_out,
        gain_out[1],
        gate_out,
        up_out,
        down_out,
    )


def solution(mesh):
    weight = P("fsdp", "tensor")
    turned = P("tensor", "fsdp")
    block = P("fsdp", "context", "tensor")
    gain = P("fsdp")
    return jax.shard_map(
        shards,
        mesh=mesh,
        in_specs=(
            block, P(), gain, weight, weight, weight, turned, gain, weight, weight, turned, block,
        ),
        out_specs=(
            block, block, gain, weight, weight, weight, turned, gain, weight, weight, turned,
        ),
        check_vma=False,
    )
```

```python
import math

import jax
import jax.numpy as jnp
from jax import lax
from jax.experimental import pallas as pl
from jax.experimental.pallas import tpu as pltpu
from jax.sharding import PartitionSpec as P

HEAD_WIDTH = 64
EPS = 1e-05
NEG = -1e30
BF = jnp.bfloat16
F32 = jnp.float32
LANES = 128
TILE = 256
GAIN_ROWS = 16
FACTOR = 1.0 / math.sqrt(HEAD_WIDTH)
VMEM_LIMIT = 62 * 2**20
MESH = pl.DeviceIdType.MESH


def rope_freqs(head_size):
    half_size = head_size // 2
    index = jnp.arange(half_size, dtype=jnp.float32)
    base_freq = jnp.exp(-(2.0 * index / head_size) * math.log(500000.0))
    wavelen = 2.0 * math.pi / base_freq
    smooth = (8192.0 / wavelen - 1.0) / 3.0
    blended = (1.0 - smooth) * base_freq / 32.0 + smooth * base_freq
    return jnp.where(
        wavelen > 8192.0, base_freq / 32.0, jnp.where(wavelen < 2048.0, base_freq, blended)
    )


def dot_t(left, right):
    return lax.dot_general(left, right, (((1,), (1,)), ((), ())), preferred_element_type=F32)


def t_dot(left, right):
    return lax.dot_general(left, right, (((0,), (0,)), ((), ())), preferred_element_type=F32)


def build_front(planes, contexts, rows, width, query_cols, kv_cols, units):
    outers = contexts // 2
    half = width // 2
    depth = width // planes
    strip = depth // contexts
    out_strip = query_cols // contexts
    unit_strip = units // contexts
    seq_len = rows * contexts
    n_q, n_kv = query_cols // LANES, kv_cols // LANES
    heads = query_cols // HEAD_WIDTH
    group = query_cols // kv_cols
    qkv_cols = query_cols + 2 * kv_cols
    QKV, OUT, GATE, UP, DOWN, COT, NORM, GAIN = range(8)

    def kernel(
        tok, cot, gains_own, qkv_own, out_own, gate_own, up_own, down_own, cosine, sine, pos_q, pos_k,
        gate_w, up_w, down_w, cot_all, norm_all, qkv_w, out_w, gains, q_pad, kv_all, attn, log_sum,
        mid_own, normed_one, tok_all, scales,
        lin, heads_out, send_half, recv_half, norm_own, sq_send, sq_recv,
        z_send, z_recv, y_send, y_recv, k_send, k_recv, x_send, x_recv, own_sem,
    ):
        z = lax.axis_index("fsdp")
        c = lax.axis_index("context")
        t = lax.axis_index("tensor")
        o, k = c // 2, c % 2

        def at_z(p):
            return (p, c, t)

        def at_o(other):
            return (z, other * 2 + k, t)

        at_k = (z, o * 2 + 1 - k, t)
        at_x = (z, c, 1 - t)

        def copy(src, dst, send_sem, recv_sem, device):
            return pltpu.make_async_remote_copy(
                src_ref=src, dst_ref=dst, send_sem=send_sem, recv_sem=recv_sem,
                device_id=device, device_id_type=MESH,
            )

        barrier = pltpu.get_barrier_semaphore()
        peers = [at_z(lax.rem(z + s, planes)) for s in range(1, planes)]
        peers += [at_o(lax.rem(o + s, outers)) for s in range(1, outers)] + [at_k, at_x]
        for peer in peers:
            pl.semaphore_signal(barrier, inc=1, device_id=peer, device_id_type=MESH)
        pl.semaphore_wait(barrier, len(peers))

        order = []
        for i in range(planes - 1):
            p = jnp.int32(0)
            for plane in range(planes):
                far = sorted((abs(q - plane), q) for q in range(planes) if q != plane)
                p = p + jnp.where(z == plane, far[i][1], 0)
            order.append(p)

        def slot(item, p, q):
            if item == QKV:
                return qkv_w.at[pl.ds(p * depth + q * strip, strip), :]
            if item == OUT:
                return out_w.at[pl.ds(q * out_strip, out_strip), pl.ds(p * depth, depth)]
            if item == GATE:
                return gate_w.at[pl.ds(p * depth + q * strip, strip), :]
            if item == UP:
                return up_w.at[pl.ds(p * depth + q * strip, strip), :]
            if item == DOWN:
                return down_w.at[pl.ds(q * unit_strip, unit_strip), pl.ds(p * depth, depth)]
            if item == COT:
                return cot_all.at[p, :, pl.ds(t * half, half)]
            return norm_all.at[p, :, pl.ds(t * half, half)]

        def z_copy(item, p, src, goal, way):
            return copy(src, slot(item, p, c), z_send.at[item, p, way], z_recv.at[item, p], at_z(goal))

        def z_wait(item, p):
            z_copy(item, p, slot(item, p, c), z, 0).wait_recv()

        def spread(item, src):
            @pl.when(z + 1 < planes)
            def _():
                z_copy(item, z, src, z + 1, 0).start()

            @pl.when(z > 0)
            def _():
                z_copy(item, z, src, z - 1, 1).start()

        def spread_done(item, src):
            @pl.when(z + 1 < planes)
            def _():
                z_copy(item, z, src, z + 1, 0).wait_send()

            @pl.when(z > 0)
            def _():
                z_copy(item, z, src, z - 1, 1).wait_send()

        def passes_on(p):
            return ((p < z) & (z + 1 < planes)) | ((p > z) & (z > 0))

        def onward(p):
            return jnp.where(p < z, z + 1, z - 1)

        def forward(item, p):
            @pl.when(passes_on(p))
            def _():
                z_copy(item, p, slot(item, p, c), onward(p), 0).start()

        def forward_done(item, p):
            @pl.when(passes_on(p))
            def _():
                z_copy(item, p, slot(item, p, c), onward(p), 0).wait_send()

        def y_copy(item, p, by):
            here = slot(item, p, c)
            return copy(here, here, y_send.at[item, p, by], y_recv.at[item, p, by], at_o(lax.rem(o + by, outers)))

        def y_wait(item, p, by):
            there = slot(item, p, lax.rem(o - by + outers, outers) * 2 + k)
            copy(there, there, y_send.at[item, p, by], y_recv.at[item, p, by], at_k).wait_recv()

        def k_copy(item, p, by):
            here = slot(item, p, lax.rem(o - by + outers, outers) * 2 + k)
            return copy(here, here, k_send.at[item, p, by], k_recv.at[item, p, by], at_k)

        def k_wait(item, p, by):
            there = slot(item, p, lax.rem(o - by + outers, outers) * 2 + 1 - k)
            copy(there, there, k_send.at[item, p, by], k_recv.at[item, p, by], at_k).wait_recv()

        def share(item, p):
            for by in range(1, outers):
                y_copy(item, p, by).start()
            k_copy(item, p, 0).start()

        def share_on(item, p):
            for by in range(1, outers):
                y_wait(item, p, by)
                k_copy(item, p, by).start()

        def shared(item, p):
            for by in range(outers):
                k_wait(item, p, by)

        def share_done(item, p):
            for by in range(1, outers):
                y_copy(item, p, by).wait_send()
            for by in range(outers):
                k_copy(item, p, by).wait_send()

        def x_copy(i, src, dst):
            return copy(src, dst, x_send.at[i], x_recv.at[i], at_x)

        tok_cols = pl.ds(t * half, half)
        tok_copy = x_copy(0, tok, tok_all.at[:, tok_cols])
        tok_copy.start()
        gain_copies = [
            copy(
                gains_own, gains.at[:, pl.ds(z * depth, depth)], z_send.at[GAIN, lax.rem(z + s, planes), 0],
                z_recv.at[GAIN, z], at_z(lax.rem(z + s, planes)),
            )
            for s in range(1, planes)
        ]
        for one in gain_copies:
            one.start()
        qkv_src = qkv_own.at[pl.ds(c * strip, strip), :]
        out_src = out_own.at[pl.ds(c * out_strip, out_strip), :]
        spread(QKV, qkv_src)
        own_copies = [
            pltpu.make_async_copy(qkv_own, qkv_w.at[pl.ds(z * depth, depth), :], own_sem.at[0]),
            pltpu.make_async_copy(out_own, out_w.at[:, pl.ds(z * depth, depth)], own_sem.at[1]),
            pltpu.make_async_copy(
                gate_own.at[:, pl.ds(z * units, units)], gate_w.at[pl.ds(z * depth, depth), :], own_sem.at[2]
            ),
            pltpu.make_async_copy(
                up_own.at[:, pl.ds(z * units, units)], up_w.at[pl.ds(z * depth, depth), :], own_sem.at[3]
            ),
            pltpu.make_async_copy(
                down_own.at[pl.ds(z * units, units), :], down_w.at[:, pl.ds(z * depth, depth)], own_sem.at[4]
            ),
            pltpu.make_async_copy(cot, slot(COT, z, c), own_sem.at[5]),
        ]
        for one in own_copies:
            one.start()
        gains[:, pl.ds(z * depth, depth)] = gains_own[...]
        tok_all[:, tok_cols] = tok[...]

        tok_copy.wait()
        for s in range(1, planes):
            p = lax.rem(z + s, planes)
            there = gains.at[:, pl.ds(p * depth, depth)]
            copy(there, there, z_send.at[GAIN, p, 0], z_recv.at[GAIN, p], at_k).wait_recv()
        x = tok_all[...].astype(F32)
        scale = lax.rsqrt(jnp.mean(x * x, -1, keepdims=True) + EPS)
        scales[0] = jnp.broadcast_to(scale, (rows, LANES))
        normed_one[...] = (x * scale * gains[0:1, :].astype(F32)).astype(BF)

        for p in order:
            z_wait(QKV, p)
            forward(QKV, p)
            share(QKV, p)

        spread(OUT, out_src)
        sends = []
        for s in range(1, planes):
            goal = lax.rem(z + s, planes)
            cols = pl.ds(goal * units, units)
            sends += [
                z_copy(GATE, z, gate_own.at[pl.ds(c * strip, strip), cols], goal, s - 1),
                z_copy(UP, z, up_own.at[pl.ds(c * strip, strip), cols], goal, s - 1),
                z_copy(
                    DOWN, z, down_own.at[pl.ds(goal * units + c * unit_strip, unit_strip), :], goal, s - 1
                ),
            ]
        for one in sends:
            one.start()
        spread(COT, cot)
        cot_copy = x_copy(1 + z, cot, slot(COT, z, c))
        cot_copy.start()

        for p in order:
            share_on(QKV, p)
        for p in order:
            shared(QKV, p)
        own_copies[0].wait()

        n_tile = 2 * LANES

        @pl.loop(0, qkv_cols // n_tile)
        def _(i):
            cols = pl.ds(pl.multiple_of(i * n_tile, n_tile), n_tile)
            found = jnp.dot(normed_one[...], qkv_w[:, cols], preferred_element_type=F32)
            lin[2 * i] = found[:, :LANES]
            lin[2 * i + 1] = found[:, LANES:]

        lane = lax.broadcasted_iota(jnp.int32, (rows, LANES), 1)
        first = lax.rem(lane, HEAD_WIDTH) < HEAD_WIDTH // 2
        low = lane < HEAD_WIDTH

        def rotated(u):
            partner = jnp.where(
                first, pltpu.roll(u, LANES - HEAD_WIDTH // 2, 1), pltpu.roll(u, HEAD_WIDTH // 2, 1)
            )
            return u * cosine[...] + partner * sine[...]

        for i in range(n_kv):
            kv_all[c, i] = rotated(lin[n_q + i]).astype(BF)
            kv_all[c, n_kv + i] = lin[n_q + n_kv + i].astype(BF)

        def kv_slot(q):
            return kv_all.at[q]

        kv_sends = [
            copy(kv_slot(c), kv_slot(c), y_send.at[COT, 0, by], y_recv.at[COT, 0, by], at_o(lax.rem(o + by, outers)))
            for by in range(1, outers)
        ]
        kv_sends.append(copy(kv_slot(c), kv_slot(c), k_send.at[COT, 0, 0], k_recv.at[COT, 0, 0], at_k))
        for one in kv_sends:
            one.start()

        @pl.loop(0, n_q)
        def _(j):
            u = rotated(lin[j]).astype(BF).astype(F32) * FACTOR
            side = lax.rem((2 * j) // group, 2)
            lo = jnp.where(low, u, 0.0)
            hi = jnp.where(low, 0.0, u)
            q_pad[2 * j] = jnp.where(side == 0, lo, pltpu.roll(lo, HEAD_WIDTH, 1)).astype(BF)
            q_pad[2 * j + 1] = jnp.where(side == 1, hi, pltpu.roll(hi, HEAD_WIDTH, 1)).astype(BF)

        for by in range(1, outers):
            q = lax.rem(o - by + outers, outers) * 2 + k
            copy(kv_slot(q), kv_slot(q), y_send.at[COT, 0, by], y_recv.at[COT, 0, by], at_k).wait_recv()
            one = copy(kv_slot(q), kv_slot(q), k_send.at[COT, 0, by], k_recv.at[COT, 0, by], at_k)
            one.start()
            kv_sends.append(one)
        for by in range(outers):
            q = lax.rem(o - by + outers, outers) * 2 + 1 - k
            copy(kv_slot(q), kv_slot(q), k_send.at[COT, 0, by], k_recv.at[COT, 0, by], at_k).wait_recv()

        for p in order:
            z_wait(OUT, p)
            forward(OUT, p)
            share(OUT, p)

        def attend(first_head, last_head):
            @pl.loop(first_head, last_head)
            def _(h):
                pair = h // (2 * group)
                keys = kv_all[:, pair].reshape(seq_len, LANES)
                values = kv_all[:, n_kv + pair].reshape(seq_len, LANES)
                scores = dot_t(keys, q_pad[h])
                scores = jnp.where(pos_q[0:1, :] >= pos_k[...], scores, NEG)
                top = jnp.max(scores, 0, keepdims=True)
                expo = jnp.exp(scores - top)
                total = jnp.sum(expo, 0, keepdims=True)
                weights = (expo * (1.0 / total)).astype(BF)
                heads_out[h] = t_dot(values, weights).T
                log_sum[pl.ds(h, 1), :] = top + jnp.log(total)

        attend(0, heads // 2)
        for p in order:
            share_on(OUT, p)
        for p in order:
            z_wait(COT, p)
            forward(COT, p)
            x_copy(1 + p, slot(COT, p, c), slot(COT, p, c)).start()
        attend(heads // 2, heads)

        for j in range(n_q):
            side = (2 * j) // group % 2
            lo, hi = heads_out[2 * j], heads_out[2 * j + 1]
            if side == 0:
                hi = pltpu.roll(hi, HEAD_WIDTH, 1)
            else:
                lo = pltpu.roll(lo, HEAD_WIDTH, 1)
            attn[:, j * LANES : (j + 1) * LANES] = jnp.where(low, lo, hi).astype(BF)

        for p in order:
            shared(OUT, p)
        own_copies[1].wait()

        n_out = half // n_tile

        @pl.loop(0, n_out)
        def _(i):
            cols = pl.ds(pl.multiple_of((1 - t) * half + i * n_tile, n_tile), n_tile)
            here = pl.ds(pl.multiple_of(i * n_tile, n_tile), n_tile)
            send_half[:, here] = jnp.dot(attn[...], out_w[:, cols], preferred_element_type=F32).astype(BF)

        half_copy = x_copy(1 + planes, send_half, recv_half)
        half_copy.start()

        @pl.loop(0, n_out)
        def _(i):
            cols = pl.ds(pl.multiple_of(t * half + i * n_tile, n_tile), n_tile)
            here = pl.ds(pl.multiple_of(i * n_tile, n_tile), n_tile)
            part = jnp.dot(attn[...], out_w[:, cols], preferred_element_type=F32)
            mid_own[:, here] = tok[:, here].astype(F32) + part

        half_copy.wait_recv()
        mid = mid_own[...] + recv_half[...].astype(F32)
        mid_own[...] = mid
        squares = jnp.sum(mid * mid, -1, keepdims=True)
        sq_send[...] = jnp.broadcast_to(squares, (rows, LANES))
        sq_copy = x_copy(2 + planes, sq_send, sq_recv)
        sq_copy.start()
        sq_copy.wait_recv()
        scale_two = lax.rsqrt((squares + sq_recv[:, 0:1]) * (1.0 / width) + EPS)
        scales[1] = jnp.broadcast_to(scale_two, (rows, LANES))
        gain_two = gains[1:2, pl.ds(pl.multiple_of(t * half, half), half)].astype(F32)
        norm_own[...] = (mid_own[...] * scale_two * gain_two).astype(BF)

        spread(NORM, norm_own)
        norm_copy = x_copy(3 + planes + z, norm_own, slot(NORM, z, c))
        norm_copy.start()
        norm_keep = pltpu.make_async_copy(norm_own, slot(NORM, z, c), own_sem.at[6])
        norm_keep.start()
        items = (GATE, UP, DOWN)
        for s in range(1, planes):
            p = lax.rem(z + planes - s, planes)
            for item in items:
                z_wait(item, p)
                share(item, p)
        for i, p in enumerate(order):
            z_wait(NORM, p)
            forward(NORM, p)
            x_copy(3 + planes + p, slot(NORM, p, c), slot(NORM, p, c)).start()
            for item in items:
                share_on(item, lax.rem(z + planes - 1 - i, planes))

        for s in range(1, planes):
            p = lax.rem(z + s, planes)
            for item in items:
                shared(item, p)
        for p in [z] + order:
            for base, item in ((1, COT), (3 + planes, NORM)):
                there = (cot_all if item == COT else norm_all).at[p, :, pl.ds((1 - t) * half, half)]
                copy(there, there, x_send.at[base + p], x_recv.at[base + p], at_x).wait_recv()
        for one in own_copies[2:]:
            one.wait()
        norm_keep.wait()
        tok_copy_out = [half_copy, sq_copy, cot_copy, norm_copy]
        for one in gain_copies + sends + kv_sends + tok_copy_out:
            one.wait_send()
        spread_done(QKV, qkv_src)
        spread_done(OUT, out_src)
        spread_done(COT, cot)
        spread_done(NORM, norm_own)
        for p in order:
            for item in (QKV, OUT, COT, NORM):
                forward_done(item, p)
            for item in (QKV, OUT, GATE, UP, DOWN):
                share_done(item, p)
            x_copy(1 + p, slot(COT, p, c), slot(COT, p, c)).wait_send()
            x_copy(3 + planes + p, slot(NORM, p, c), slot(NORM, p, c)).wait_send()

    hbm = pl.BlockSpec(memory_space=pl.ANY)
    vmem = pl.BlockSpec(memory_space=pltpu.VMEM)
    dma = pltpu.SemaphoreType.DMA
    shape = jax.ShapeDtypeStruct
    return pl.pallas_call(
        kernel,
        name="front",
        out_shape=(
            shape((width, units), BF),
            shape((width, units), BF),
            shape((units, width), BF),
            shape((planes, rows, width), BF),
            shape((planes, rows, width), BF),
            shape((width, qkv_cols), BF),
            shape((query_cols, width), BF),
            shape((GAIN_ROWS, width), BF),
            shape((heads, rows, LANES), BF),
            shape((contexts, 2 * n_kv, rows, LANES), BF),
            shape((rows, query_cols), BF),
            shape((heads, rows), F32),
            shape((rows, half), F32),
            shape((rows, width), BF),
            shape((rows, width), BF),
            shape((2, rows, LANES), F32),
        ),
        in_specs=[vmem, hbm, vmem, hbm, hbm, hbm, hbm, hbm, vmem, vmem, vmem, vmem],
        out_specs=(hbm,) * 5 + (vmem,) * 11,
        scratch_shapes=[
            pltpu.VMEM((qkv_cols // LANES, rows, LANES), F32),
            pltpu.VMEM((heads, rows, LANES), F32),
            pltpu.VMEM((rows, half), BF),
            pltpu.VMEM((rows, half), BF),
            pltpu.VMEM((rows, half), BF),
            pltpu.VMEM((rows, LANES), F32),
            pltpu.VMEM((rows, LANES), F32),
            dma((8, planes, planes)),
            dma((8, planes)),
            dma((6, planes, max(outers, 2))),
            dma((6, planes, max(outers, 2))),
            dma((6, planes, max(outers, 2))),
            dma((6, planes, max(outers, 2))),
            dma((3 + 2 * planes,)),
            dma((3 + 2 * planes,)),
            dma((8,)),
        ],
        compiler_params=pltpu.CompilerParams(
            collective_id=0, has_side_effects=True, vmem_limit_bytes=VMEM_LIMIT
        ),
        cost_estimate=pl.CostEstimate(flops=8 * 10**9, bytes_accessed=80 * 10**6, transcendentals=4 * 10**6),
    )


def add_strips(total, terms, chunk):
    lead, size, _ = total.shape
    steps = size // chunk

    @pl.loop(0, lead * steps)
    def _(i):
        a, r = i // steps, pl.ds(pl.multiple_of(lax.rem(i, steps) * chunk, chunk), chunk)
        found = terms[0][a, r, :].astype(F32)
        for term in terms[1:]:
            found = found + term[a, r, :].astype(F32)
        total[a, r, :] = found.astype(BF)


class Ring:
    def __init__(self, planes, contexts):
        self.planes, self.outers = planes, contexts // 2
        self.z = z = lax.axis_index("fsdp")
        self.c = c = lax.axis_index("context")
        self.t = t = lax.axis_index("tensor")
        self.o, self.k = c // 2, c % 2
        self.at_k = (z, self.o * 2 + 1 - self.k, t)
        self.at_x = (z, c, 1 - t)

    def at_z(self, p):
        return (p, self.c, self.t)

    def at_o(self, other):
        return (self.z, other * 2 + self.k, self.t)

    def after(self, by):
        return lax.rem(self.o + by, self.outers)

    def before(self, by):
        return lax.rem(self.o - by + self.outers, self.outers)

    def plane(self, by):
        return lax.rem(self.z + by, self.planes)

    def greet(self):
        barrier = pltpu.get_barrier_semaphore()
        peers = [self.at_z(self.plane(s)) for s in range(1, self.planes)]
        peers += [self.at_o(self.after(s)) for s in range(1, self.outers)] + [self.at_k, self.at_x]
        for peer in peers:
            pl.semaphore_signal(barrier, inc=1, device_id=peer, device_id_type=MESH)
        pl.semaphore_wait(barrier, len(peers))

    def by_distance(self):
        order = []
        for i in range(self.planes - 1):
            p = jnp.int32(0)
            for plane in range(self.planes):
                far = sorted((abs(q - plane), q) for q in range(self.planes) if q != plane)
                p = p + jnp.where(self.z == plane, far[i][1], 0)
            order.append(p)
        return order


def copy_to(src, dst, send_sem, recv_sem, device):
    return pltpu.make_async_remote_copy(
        src_ref=src, dst_ref=dst, send_sem=send_sem, recv_sem=recv_sem, device_id=device, device_id_type=MESH
    )


class Reduction:
    def __init__(self, ring, item, part, core_in, outer_out, outer_in, strip_sum, sems):
        self.ring, self.item, self.part = ring, item, part
        self.core_in, self.outer_out, self.outer_in, self.strip_sum = core_in, outer_out, outer_in, strip_sum
        self.k_send, self.k_recv, self.y_send, self.y_recv = sems
        self.chunk = 32 if strip_sum.shape[2] > 1024 else 64
        self.chunk = min(self.chunk, strip_sum.shape[1])

    def core_copy(self, other):
        g = self.ring
        return copy_to(
            self.part.at[:, other * 2 + 1 - g.k], self.core_in.at[other],
            self.k_send.at[self.item, other], self.k_recv.at[self.item, other], g.at_k,
        )

    def to_core(self):
        for other in range(self.ring.outers):
            self.core_copy(other).start()

    def outer_copy(self, by):
        g = self.ring
        return copy_to(
            self.outer_out.at[by - 1], self.outer_in.at[by - 1],
            self.y_send.at[self.item, by], self.y_recv.at[self.item, by], g.at_o(g.after(by)),
        )

    def from_core(self):
        g = self.ring
        for other in range(g.outers):
            self.core_copy(other).wait_recv()
        for by in range(1, g.outers):
            goal = g.after(by)
            add_strips(
                self.outer_out.at[by - 1], [self.part.at[:, goal * 2 + g.k], self.core_in.at[goal]], self.chunk
            )
            self.outer_copy(by).start()
        add_strips(self.strip_sum, [self.part.at[:, g.c], self.core_in.at[g.o]], self.chunk)

    def core_done(self):
        for other in range(self.ring.outers):
            self.core_copy(other).wait_send()

    def from_outer(self):
        for by in range(1, self.ring.outers):
            self.outer_copy(by).wait_recv()
        terms = [self.strip_sum] + [self.outer_in.at[by - 1] for by in range(1, self.ring.outers)]
        if len(terms) > 1:
            add_strips(self.strip_sum, terms, self.chunk)

    def outer_done(self):
        for by in range(1, self.ring.outers):
            self.outer_copy(by).wait_send()


def rotate_tile(u, cosine, sine, first):
    partner = jnp.where(
        first, pltpu.roll(u, LANES - HEAD_WIDTH // 2, 1), pltpu.roll(u, HEAD_WIDTH // 2, 1)
    )
    return u * cosine + partner * sine


def store_part(part, i, tile):
    size = part.shape[2]
    per = part.shape[1] * size // TILE
    for r in range(TILE // size):
        part[i // per, lax.rem(i, per) * (TILE // size) + r] = tile[r * size : (r + 1) * size].astype(BF)


def build_back(planes, contexts, rows, width, query_cols, kv_cols, units):
    outers = contexts // 2
    half = width // 2
    depth = width // planes
    strip = depth // contexts
    unit_strip = units // contexts
    seq_len = rows * contexts
    n_q, n_kv = query_cols // LANES, kv_cols // LANES
    heads = query_cols // HEAD_WIDTH
    group = query_cols // kv_cols
    qkv_cols = query_cols + 2 * kv_cols
    DOWN, GATE, UP, KV = range(4)
    lots = max(outers - 1, 1)

    def kernel(
        gate_hbm, up_hbm, down_hbm, norm_hbm, cot_hbm, qkv_hbm, out_hbm, q_hbm, kv_hbm, mid_hbm, tok_hbm,
        gains, cosine, sine, pos_q, pos_k, log_sum, scales,
        result, input_grad, gate_strip, up_strip, down_strip, mid_full, qkv_grad, gain_rows,
        norm_x_in, mlp_x_in, norm_z_in, mlp_z_in, norm_x_out, mlp_x_out, norm_sum, mlp_sum,
        row_core_in, col_core_in, row_outer_in, col_outer_in, row_outer_out, col_outer_out, row_sum, col_sum,
        kv_core_in, kv_outer_in, sq_out, sq_in, first_x_out, first_x_in,
        x_send, x_recv, z_send, z_recv, k_send, k_recv, y_send, y_recv, grad_send, grad_recv, load_sem, credit,
    ):
        ring = Ring(planes, contexts)
        z, c, t, k, o = ring.z, ring.c, ring.t, ring.k, ring.o
        order = ring.by_distance()
        blocks = order[::-1] + [z]
        ring.greet()
        own_cols = pl.multiple_of(t * half, half)
        other_cols = pl.multiple_of((1 - t) * half, half)
        n_half = half // TILE

        def x_copy(i, src, dst):
            return copy_to(src, dst, x_send.at[i], x_recv.at[i], ring.at_x)

        NORM, MLP, MID, SQ_TWO, FIRST, SQ_ONE = 0, planes, 2 * planes, 2 * planes + 1, 2 * planes + 2, 2 * planes + 3

        def norm_x(i):
            return x_copy(NORM + i, norm_x_out.at[i % 2], norm_x_in.at[blocks[i]])

        def mlp_x(p):
            return x_copy(MLP + p, mlp_x_out.at[p], mlp_x_in.at[p])

        def back_from(p, here):
            return lax.rem(p - here + planes, planes) - 1

        def norm_z(p):
            return copy_to(
                norm_sum.at[p], norm_z_in.at[back_from(z, p)], z_send.at[0, p], z_recv.at[0, z], ring.at_z(p)
            )

        def mlp_z(p):
            return copy_to(
                mlp_sum.at[p], mlp_z_in.at[back_from(z, p)], z_send.at[1, p], z_recv.at[1, z], ring.at_z(p)
            )

        def z_wait(i, dst, p):
            there = dst.at[back_from(p, z)]
            copy_to(there, there, z_send.at[i, p], z_recv.at[i, p], ring.at_k).wait_recv()

        def add_block(total, other, p):
            n = rows // 64

            @pl.loop(0, n)
            def _(i):
                r = pl.ds(pl.multiple_of(i * 64, 64), 64)
                total[p, r, :] = (total[p, r, :].astype(F32) + other[p, r, :].astype(F32)).astype(BF)

        def norm_on(i):
            norm_x(i).wait_recv()
            add_block(norm_sum, norm_x_in, blocks[i])

        def mlp_on(p):
            mlp_x(p).wait_recv()
            add_block(mlp_sum, mlp_x_in, p)

        sems = (k_send, k_recv, y_send, y_recv)

        def feed_forward(norm, cot, hid, gate_grad, up_grad):
            def load(i, src, dst):
                one = pltpu.make_async_copy(src, dst, load_sem.at[i])
                one.start()
                return one

            loads = [
                (load(2 * i, norm_hbm.at[p], norm.at[p]), load(2 * i + 1, cot_hbm.at[p], cot.at[p]))
                for i, p in enumerate(blocks)
            ]

            def with_weights(gate_w, up_w, down_w):
                weights = [
                    load(2 * planes, gate_hbm, gate_w),
                    load(2 * planes + 1, up_hbm, up_w),
                    load(2 * planes + 2, down_hbm, down_w),
                ]
                for one in weights:
                    one.wait()
                for i, p in enumerate(blocks):
                    loads[i][0].wait()
                    loads[i][1].wait()

                    @pl.loop(0, units // TILE)
                    def _(j):
                        cols = pl.ds(pl.multiple_of(j * TILE, TILE), TILE)
                        gate = jnp.dot(norm[p], gate_w[:, cols], preferred_element_type=F32)
                        up = jnp.dot(norm[p], up_w[:, cols], preferred_element_type=F32)
                        grad = dot_t(cot[p], down_w[cols, :])
                        sig = jax.nn.sigmoid(gate)
                        act = gate * sig
                        hid[p, :, cols] = (act * up).astype(BF)
                        gate_grad[p, :, cols] = (grad * up * sig * (1.0 + gate * (1.0 - sig))).astype(BF)
                        up_grad[p, :, cols] = (grad * act).astype(BF)

                    def norm_tile(at):
                        r = pl.ds(pl.multiple_of(at, TILE), TILE)
                        return dot_t(gate_grad[p], gate_w[r, :]) + dot_t(up_grad[p], up_w[r, :])

                    def mlp_tile(at):
                        r = pl.ds(pl.multiple_of(at, TILE), TILE)
                        return jnp.dot(hid[p], down_w[:, r], preferred_element_type=F32)

                    def halves(tile_of, out, total, start):
                        @pl.loop(0, n_half)
                        def _(j):
                            here = pl.ds(pl.multiple_of(j * TILE, TILE), TILE)
                            out[:, here] = tile_of(other_cols + j * TILE).astype(BF)

                        start()

                        @pl.loop(0, n_half)
                        def _(j):
                            here = pl.ds(pl.multiple_of(j * TILE, TILE), TILE)
                            total[p, :, here] = tile_of(own_cols + j * TILE).astype(BF)

                    if i > 1:
                        norm_x(i - 2).wait_send()
                    halves(norm_tile, norm_x_out.at[i % 2], norm_sum, lambda: norm_x(i).start())
                    if i > 0:
                        norm_on(i - 1)
                        norm_z(blocks[i - 1]).start()
                    halves(mlp_tile, mlp_x_out.at[p], mlp_sum, lambda: None)

            pl.run_scoped(
                with_weights,
                pltpu.VMEM((width, units), BF), pltpu.VMEM((width, units), BF), pltpu.VMEM((units, width), BF),
            )

            def with_parts(row_part, col_part):
                down = Reduction(
                    ring, DOWN, col_part, col_core_in, col_outer_out, col_outer_in, col_sum, sems
                )
                gate = Reduction(
                    ring, GATE, row_part, row_core_in, row_outer_out.at[0], row_outer_in.at[0], row_sum.at[0], sems
                )
                up = Reduction(
                    ring, UP, row_part, row_core_in, row_outer_out.at[1], row_outer_in.at[1], row_sum.at[1], sems
                )

                def product(part, left, right):
                    total = planes * rows

                    @pl.loop(0, left.shape[2] // TILE)
                    def _(i):
                        cols = pl.ds(pl.multiple_of(i * TILE, TILE), TILE)
                        tile = t_dot(left[:, :, cols].reshape(total, TILE), right[...].reshape(total, right.shape[2]))
                        store_part(part, i, tile)

                product(col_part, hid, cot)
                down.to_core()
                norm_on(planes - 1)
                product(row_part, norm, gate_grad)
                gate.to_core()
                down.from_core()
                gate.from_core()
                gate.core_done()
                pl.semaphore_signal(credit, inc=1, device_id=ring.at_k, device_id_type=MESH)
                product(row_part, norm, up_grad)
                pl.semaphore_wait(credit, 1)
                up.to_core()
                up.from_core()
                up.core_done()
                down.core_done()

            pl.run_scoped(
                with_parts,
                pltpu.VMEM((planes, contexts, strip, units), BF), pltpu.VMEM((1, contexts, unit_strip, width), BF),
            )

        block_bf = pltpu.VMEM((planes, rows, width), BF)
        unit_bf = pltpu.VMEM((planes, rows, units), BF)
        pl.run_scoped(feed_forward, block_bf, block_bf, unit_bf, unit_bf, unit_bf)

        down = Reduction(ring, DOWN, None, None, col_outer_out, col_outer_in, col_sum, sems)
        gate = Reduction(ring, GATE, None, None, row_outer_out.at[0], row_outer_in.at[0], row_sum.at[0], sems)
        up = Reduction(ring, UP, None, None, row_outer_out.at[1], row_outer_in.at[1], row_sum.at[1], sems)

        def strip_src(item, goal):
            if item == DOWN:
                return col_sum.at[0, :, pl.ds(pl.multiple_of(goal * depth, depth), depth)]
            return row_sum.at[0 if item == GATE else 1, goal]

        def strip_dst(item, home):
            if item == DOWN:
                return down_strip.at[home]
            return (gate_strip if item == GATE else up_strip).at[:, pl.ds(pl.multiple_of(home * units, units), units)]

        def strip_copy(item, s):
            goal = ring.plane(s)
            return copy_to(
                strip_src(item, goal), strip_dst(item, z), grad_send.at[item, s], grad_recv.at[item, z], ring.at_z(goal)
            )

        def strip_keep(item):
            return pltpu.make_async_copy(strip_src(item, z), strip_dst(item, z), grad_send.at[item, 0])

        def to_planes(item, reduction):
            reduction.from_outer()
            for s in range(1, planes):
                strip_copy(item, s).start()
            strip_keep(item).start()

        def attention(mid, mid_grad, q_pad, kv_all, tok, grad_pad, query_out, key_sum, value_sum, kv_grad, kv_out):
            loads = [
                pltpu.make_async_copy(mid_hbm, mid, load_sem.at[0]),
                pltpu.make_async_copy(tok_hbm.at[:, pl.ds(own_cols, half)], tok, load_sem.at[1]),
                pltpu.make_async_copy(q_hbm, q_pad, load_sem.at[2]),
                pltpu.make_async_copy(kv_hbm, kv_all, load_sem.at[3]),
                pltpu.make_async_copy(cot_hbm.at[z, :, pl.ds(own_cols, half)], first_x_out, load_sem.at[4]),
            ]
            for one in loads:
                one.start()
            for one in loads:
                one.wait()
            key_sum[...] = jnp.zeros_like(key_sum)
            value_sum[...] = jnp.zeros_like(value_sum)
            gain_rows[...] = jnp.zeros_like(gain_rows)

            def norm_back(grad, normal, scale, gain, gain_row, i):
                scaled = grad * gain
                gain_rows[gain_row : gain_row + 1, :] = jnp.sum(grad * normal, 0, keepdims=True)
                mine = jnp.sum(scaled * normal, -1, keepdims=True)
                sq_out[i] = jnp.broadcast_to(mine, (rows, LANES))
                swap = x_copy(SQ_TWO if i == 0 else SQ_ONE, sq_out.at[i], sq_in.at[i])
                swap.start()
                swap.wait()
                inner = (mine + sq_in[i][:, 0:1]) * (1.0 / width)
                return scale * (scaled - normal * inner)

            for p in order:
                z_wait(0, norm_z_in, p)
            grad = norm_sum[z].astype(F32)
            for p in order:
                grad = grad + norm_z_in[back_from(p, z)].astype(F32)
            scale_two = scales[1][:, 0:1]
            gain_two = gains[1:2, pl.ds(own_cols, half)].astype(F32)
            back = norm_back(grad, mid[...] * scale_two, scale_two, gain_two, 1, 0)
            mid_grad[...] = first_x_out[...].astype(F32) + back
            mine = mid_full.at[:, pl.ds(own_cols, half)]
            mid_full[:, pl.ds(own_cols, half)] = mid_grad[...].astype(BF)
            mid_swap = x_copy(MID, mine, mine)
            mid_swap.start()
            for p in blocks:
                mlp_x(p).start()
            to_planes(DOWN, down)
            mid_swap.wait_recv()

            lane = lax.broadcasted_iota(jnp.int32, (rows, LANES), 1)
            first = lax.rem(lane, HEAD_WIDTH) < HEAD_WIDTH // 2
            low = lane < HEAD_WIDTH

            def with_out(out_w):
                one = pltpu.make_async_copy(out_hbm, out_w, load_sem.at[0])
                one.start()
                one.wait()

                @pl.loop(0, query_cols // TILE)
                def _(i):
                    r = pl.ds(pl.multiple_of(i * TILE, TILE), TILE)
                    found = dot_t(mid_full[...], out_w[r, :])
                    for half_tile in range(TILE // LANES):
                        j = i * (TILE // LANES) + half_tile
                        u = found[:, half_tile * LANES : (half_tile + 1) * LANES]
                        u = u.astype(BF).astype(F32)
                        side = lax.rem((2 * j) // group, 2)
                        lo = jnp.where(low, u, 0.0)
                        hi = jnp.where(low, 0.0, u)
                        grad_pad[2 * j] = jnp.where(side == 0, lo, pltpu.roll(lo, HEAD_WIDTH, 1)).astype(BF)
                        grad_pad[2 * j + 1] = jnp.where(side == 1, hi, pltpu.roll(hi, HEAD_WIDTH, 1)).astype(BF)

            pl.run_scoped(with_out, pltpu.VMEM((query_cols, width), BF))

            def attend_back(first_head, last_head):
                @pl.loop(first_head, last_head)
                def _(h):
                    pair = h // (2 * group)
                    keys = kv_all[:, pair].reshape(seq_len, LANES)
                    values = kv_all[:, n_kv + pair].reshape(seq_len, LANES)
                    scores = dot_t(keys, q_pad[h])
                    scores = jnp.where(pos_q[0:1, :] >= pos_k[...], scores, NEG)
                    weights = jnp.exp(scores - log_sum[pl.ds(h, 1), :])
                    weight_grad = dot_t(values, grad_pad[h])
                    inner = jnp.sum(weights * weight_grad, 0, keepdims=True)
                    score_grad = (weights * (weight_grad - inner)).astype(BF)
                    value_sum[pair] += jnp.dot(weights.astype(BF), grad_pad[h], preferred_element_type=F32)
                    key_sum[pair] += jnp.dot(score_grad, q_pad[h], preferred_element_type=F32)
                    query_out[h] = t_dot(keys, score_grad).T

            attend_back(0, heads // 2)
            mlp_on(blocks[0])
            mlp_z(blocks[0]).start()
            attend_back(heads // 2, heads)
            for i in range(n_kv):
                kv_grad[:, i] = key_sum[i].astype(BF).reshape(contexts, rows, LANES)
                kv_grad[:, n_kv + i] = value_sum[i].astype(BF).reshape(contexts, rows, LANES)

            def kv_core(other):
                return copy_to(
                    kv_grad.at[other * 2 + 1 - k], kv_core_in.at[other], k_send.at[KV, other], k_recv.at[KV, other],
                    ring.at_k,
                )

            def kv_outer(by):
                return copy_to(
                    kv_out.at[by - 1], kv_outer_in.at[by - 1], y_send.at[KV, by], y_recv.at[KV, by],
                    ring.at_o(ring.after(by)),
                )

            for other in range(outers):
                kv_core(other).start()
            to_planes(GATE, gate)
            for j in range(n_q):
                side = (2 * j) // group % 2
                lo, hi = query_out[2 * j], query_out[2 * j + 1]
                if side == 0:
                    hi = pltpu.roll(hi, HEAD_WIDTH, 1)
                else:
                    lo = pltpu.roll(lo, HEAD_WIDTH, 1)
                u = jnp.where(low, lo, hi) * FACTOR
                qkv_grad[:, j * LANES : (j + 1) * LANES] = rotate_tile(u, cosine[...], -sine[...], first).astype(BF)
            for other in range(outers):
                kv_core(other).wait_recv()
            for by in range(1, outers):
                goal = ring.after(by)
                kv_out[by - 1] = (
                    kv_grad[goal * 2 + k].astype(F32) + kv_core_in[goal].astype(F32)
                ).astype(BF)
                kv_outer(by).start()
            kv_sum = kv_grad[c].astype(F32) + kv_core_in[o].astype(F32)
            for by in range(1, outers):
                kv_outer(by).wait_recv()
                kv_sum = kv_sum + kv_outer_in[by - 1].astype(F32)
            for i in range(n_kv):
                at = query_cols + i * LANES
                qkv_grad[:, at : at + LANES] = rotate_tile(kv_sum[i], cosine[...], -sine[...], first).astype(BF)
                qkv_grad[:, at + kv_cols : at + kv_cols + LANES] = kv_sum[n_kv + i].astype(BF)
            for other in range(outers):
                kv_core(other).wait_send()
            for by in range(1, outers):
                kv_outer(by).wait_send()

            first_swap = x_copy(FIRST, first_x_out, first_x_in)

            def with_qkv(qkv_w, own):
                one = pltpu.make_async_copy(qkv_hbm, qkv_w, load_sem.at[0])
                one.start()
                one.wait()

                def tile_of(at):
                    return dot_t(qkv_grad[...], qkv_w[pl.ds(pl.multiple_of(at, TILE), TILE), :])

                @pl.loop(0, n_half)
                def _(j):
                    here = pl.ds(pl.multiple_of(j * TILE, TILE), TILE)
                    first_x_out[:, here] = tile_of(other_cols + j * TILE).astype(BF)

                first_swap.start()

                @pl.loop(0, n_half)
                def _(j):
                    here = pl.ds(pl.multiple_of(j * TILE, TILE), TILE)
                    own[:, here] = tile_of(own_cols + j * TILE)

                for p in blocks[1:]:
                    mlp_on(p)
                    if p is not z:
                        mlp_z(p).start()
                first_swap.wait()
                scale_one = scales[0][:, 0:1]
                gain_one = gains[0:1, pl.ds(own_cols, half)].astype(F32)
                back = norm_back(
                    own[...] + first_x_in[...].astype(F32), tok[...].astype(F32) * scale_one, scale_one, gain_one, 0, 1
                )
                input_grad[...] = (mid_grad[...] + back).astype(BF)

            pl.run_scoped(with_qkv, pltpu.VMEM((width, qkv_cols), BF), pltpu.VMEM((rows, half), F32))
            to_planes(UP, up)
            mid_swap.wait_send()
            total = mid[...] + mlp_sum[z].astype(F32)
            for p in order:
                z_wait(1, mlp_z_in, p)
                total = total + mlp_z_in[back_from(p, z)].astype(F32)
            result[...] = total.astype(BF)

        tile_f32 = pltpu.VMEM((rows, half), F32)
        pl.run_scoped(
            attention,
            tile_f32,
            tile_f32,
            pltpu.VMEM((heads, rows, LANES), BF),
            pltpu.VMEM((contexts, 2 * n_kv, rows, LANES), BF),
            pltpu.VMEM((rows, half), BF),
            pltpu.VMEM((heads, rows, LANES), BF),
            pltpu.VMEM((heads, rows, LANES), F32),
            pltpu.VMEM((n_kv, seq_len, LANES), F32),
            pltpu.VMEM((n_kv, seq_len, LANES), F32),
            pltpu.VMEM((contexts, 2 * n_kv, rows, LANES), BF),
            pltpu.VMEM((lots, 2 * n_kv, rows, LANES), BF),
        )

        for item in (DOWN, GATE, UP):
            for s in range(1, planes):
                p = ring.plane(s)
                there = strip_dst(item, p)
                copy_to(there, there, grad_send.at[item, s], grad_recv.at[item, p], ring.at_k).wait_recv()
                strip_copy(item, s).wait_send()
            strip_keep(item).wait()
        for reduction in (down, gate, up):
            reduction.outer_done()
        for i in range(max(planes - 2, 0), planes):
            norm_x(i).wait_send()
        for p in blocks:
            mlp_x(p).wait_send()
        for p in order:
            norm_z(p).wait_send()
            mlp_z(p).wait_send()

    hbm = pl.BlockSpec(memory_space=pl.ANY)
    vmem = pl.BlockSpec(memory_space=pltpu.VMEM)
    dma = pltpu.SemaphoreType.DMA
    shape = jax.ShapeDtypeStruct
    acts = pltpu.VMEM((planes, rows, half), BF)
    arrivals = pltpu.VMEM((planes - 1, rows, half), BF)
    return pl.pallas_call(
        kernel,
        name="back",
        out_shape=(
            shape((rows, half), BF),
            shape((rows, half), BF),
            shape((strip, planes * units), BF),
            shape((strip, planes * units), BF),
            shape((planes, unit_strip, depth), BF),
            shape((rows, width), BF),
            shape((rows, qkv_cols), BF),
            shape((8, half), F32),
        ),
        in_specs=[hbm] * 11 + [vmem] * 7,
        out_specs=(vmem, vmem, hbm, hbm, hbm, vmem, vmem, vmem),
        scratch_shapes=[acts, acts, arrivals, arrivals, pltpu.VMEM((2, rows, half), BF), acts, acts, acts]
        + [
            pltpu.VMEM((outers, planes, strip, units), BF),
            pltpu.VMEM((outers, 1, unit_strip, width), BF),
            pltpu.VMEM((2, lots, planes, strip, units), BF),
            pltpu.VMEM((lots, 1, unit_strip, width), BF),
            pltpu.VMEM((2, lots, planes, strip, units), BF),
            pltpu.VMEM((lots, 1, unit_strip, width), BF),
            pltpu.VMEM((2, planes, strip, units), BF),
            pltpu.VMEM((1, unit_strip, width), BF),
            pltpu.VMEM((outers, 2 * n_kv, rows, LANES), BF),
            pltpu.VMEM((lots, 2 * n_kv, rows, LANES), BF),
            pltpu.VMEM((2, rows, LANES), F32),
            pltpu.VMEM((2, rows, LANES), F32),
            pltpu.VMEM((rows, half), BF),
            pltpu.VMEM((rows, half), BF),
            dma((2 * planes + 4,)),
            dma((2 * planes + 4,)),
            dma((2, planes)),
            dma((2, planes)),
            dma((4, outers)),
            dma((4, outers)),
            dma((4, max(outers, 2))),
            dma((4, max(outers, 2))),
            dma((3, planes)),
            dma((3, planes)),
            dma((2 * planes + 3,)),
            pltpu.SemaphoreType.REGULAR,
        ],
        compiler_params=pltpu.CompilerParams(
            collective_id=1, has_side_effects=True, vmem_limit_bytes=VMEM_LIMIT
        ),
        cost_estimate=pl.CostEstimate(flops=50 * 10**9, bytes_accessed=80 * 10**6, transcendentals=8 * 10**6),
    )


def build_grads(planes, contexts, rows, width, query_cols, kv_cols, units):
    outers = contexts // 2
    half = width // 2
    depth = width // planes
    strip = depth // contexts
    out_strip = query_cols // contexts
    unit_strip = units // contexts
    qkv_cols = query_cols + 2 * kv_cols
    lots = max(outers - 1, 1)
    per_half = planes // 2
    DOWN, GATE, UP, OUT, QKV = range(5)

    def kernel(
        attn, mid_full, normed_one, qkv_grad, gain_rows, gate_strip, up_strip, down_strip,
        gate_out, up_out, down_out, out_out, qkv_out, gain_out,
        out_part, qkv_part, out_core, qkv_core, out_outer_out, qkv_outer_out, out_outer_in, qkv_outer_in,
        out_sum, qkv_sum, out_z, qkv_z, gain_z, gain_y, gain_k, gain_now,
        k_send, k_recv, y_send, y_recv, z_send, z_recv, sk_send, sk_recv, sy_send, sy_recv, gain_send, gain_recv,
        own_sem,
    ):
        ring = Ring(planes, contexts)
        z, c, t, k, o = ring.z, ring.c, ring.t, ring.k, ring.o
        order = ring.by_distance()
        ring.greet()

        def slot(item, q):
            if item == DOWN:
                return down_out.at[:, q]
            if item == OUT:
                return out_out.at[pl.ds(q * out_strip, out_strip), :]
            whole = {GATE: gate_out, UP: up_out, QKV: qkv_out}[item]
            return whole.at[pl.ds(q * strip, strip), :]

        def own_strip(item):
            return {DOWN: down_strip, GATE: gate_strip, UP: up_strip}.get(item, None)

        def source(item):
            found = own_strip(item)
            return slot(item, c) if found is None else found

        def y_copy(item, by):
            return copy_to(
                source(item), slot(item, c), sy_send.at[item, by], sy_recv.at[item, by], ring.at_o(ring.after(by))
            )

        def k_copy(item, by):
            q = ring.before(by) * 2 + k
            src = source(item) if by == 0 else slot(item, q)
            return copy_to(src, slot(item, q), sk_send.at[item, by], sk_recv.at[item, by], ring.at_k)

        def share(item):
            for by in range(1, outers):
                y_copy(item, by).start()
            k_copy(item, 0).start()

        def share_on(item):
            for by in range(1, outers):
                there = slot(item, ring.before(by) * 2 + k)
                copy_to(there, there, sy_send.at[item, by], sy_recv.at[item, by], ring.at_k).wait_recv()
                k_copy(item, by).start()

        def shared(item):
            for by in range(outers):
                there = slot(item, ring.before(by) * 2 + 1 - k)
                copy_to(there, there, sk_send.at[item, by], sk_recv.at[item, by], ring.at_k).wait_recv()
            for by in range(1, outers):
                y_copy(item, by).wait_send()
            for by in range(outers):
                k_copy(item, by).wait_send()

        keeps = [
            pltpu.make_async_copy(own_strip(item), slot(item, c), own_sem.at[item]) for item in (DOWN, GATE, UP)
        ]
        share(DOWN)
        for one in keeps:
            one.start()

        takes_part = z // per_half == t

        def gain_plane(j):
            return t * per_half + j

        def gain_copy(j):
            return copy_to(
                gain_rows.at[:, pl.ds(j * depth, depth)], gain_z.at[z], gain_send.at[j], gain_recv.at[z],
                ring.at_z(gain_plane(j)),
            )

        for j in range(per_half):

            @pl.when(gain_plane(j) != z)
            def _(j=j):
                gain_copy(j).start()

        gain_x = copy_to(
            gain_out, gain_out, gain_send.at[per_half], gain_recv.at[planes], ring.at_x
        )

        def gain_outer(by):
            return copy_to(
                gain_now.at[0], gain_y.at[by - 1], gain_send.at[per_half + by], gain_recv.at[planes + by],
                ring.at_o(ring.after(by)),
            )

        gain_core = copy_to(
            gain_now.at[1], gain_k, gain_send.at[per_half + outers], gain_recv.at[planes + outers], ring.at_k
        )

        def product(part, left, right):
            @pl.loop(0, left.shape[1] // TILE)
            def _(i):
                cols = pl.ds(pl.multiple_of(i * TILE, TILE), TILE)
                store_part(part, i, t_dot(left[:, cols], right[...]))

        sems = (k_send, k_recv, y_send, y_recv)
        out = Reduction(ring, 0, out_part, out_core, out_outer_out, out_outer_in, out_sum, sems)
        qkv = Reduction(ring, 1, qkv_part, qkv_core, qkv_outer_out, qkv_outer_in, qkv_sum, sems)
        product(out_part, attn, mid_full)
        out.to_core()
        product(qkv_part, normed_one, qkv_grad)
        qkv.to_core()
        out.from_core()

        @pl.when(takes_part)
        def _():
            mine = lax.rem(z, per_half) * depth
            total = gain_rows[:, pl.ds(pl.multiple_of(mine, depth), depth)]
            for s in range(1, planes):
                p = ring.plane(s)
                copy_to(gain_z.at[p], gain_z.at[p], gain_send.at[0], gain_recv.at[p], ring.at_k).wait_recv()
                total = total + gain_z[p]
            gain_now[0] = total
            for by in range(1, outers):
                gain_outer(by).start()

        qkv.from_core()
        share(GATE)
        share(UP)

        @pl.when(takes_part)
        def _():
            total = gain_now[0]
            for by in range(1, outers):
                gain_outer(by).wait()
                total = total + gain_y[by - 1]
            gain_now[1] = total
            gain_core.start()

        def piece(item, p):
            if item == OUT:
                return out_sum.at[0, :, pl.ds(pl.multiple_of(p * depth, depth), depth)]
            return qkv_sum.at[p]

        def landing(item, p):
            return (out_z if item == OUT else qkv_z).at[p]

        def z_copy(item, s):
            p = ring.plane(s)
            return copy_to(
                piece(item, p), landing(item, z), z_send.at[item - OUT, s], z_recv.at[item - OUT, z], ring.at_z(p)
            )

        def to_planes(item, reduction):
            reduction.from_outer()
            for s in range(1, planes):
                z_copy(item, s).start()

        def from_planes(item):
            for p in order:
                there = landing(item, p)
                copy_to(there, there, z_send.at[item - OUT, 0], z_recv.at[item - OUT, p], ring.at_k).wait_recv()
            size = out_strip if item == OUT else strip
            whole = out_out if item == OUT else qkv_out
            total = piece(item, z)[...].astype(F32)
            for p in order:
                total = total + landing(item, p)[...].astype(F32)
            whole[pl.ds(pl.multiple_of(c * size, size), size), :] = total.astype(BF)
            share(item)

        to_planes(OUT, out)

        @pl.when(takes_part)
        def _():
            gain_core.wait()
            gain_out[...] = gain_now[1] + gain_k[...]
            gain_x.start()

        share_on(DOWN)
        to_planes(QKV, qkv)
        from_planes(OUT)
        from_planes(QKV)
        share_on(GATE)
        share_on(UP)
        share_on(OUT)
        share_on(QKV)
        for one in keeps:
            one.wait()
        for item in range(5):
            shared(item)
        for reduction in (out, qkv):
            reduction.core_done()
            reduction.outer_done()
        for item in (OUT, QKV):
            for s in range(1, planes):
                z_copy(item, s).wait_send()
        for j in range(per_half):

            @pl.when(gain_plane(j) != z)
            def _(j=j):
                gain_copy(j).wait_send()

        @pl.when(takes_part)
        def _():
            gain_x.wait_send()

        @pl.when(jnp.logical_not(takes_part))
        def _():
            gain_x.wait_recv()

    hbm = pl.BlockSpec(memory_space=pl.ANY)
    vmem = pl.BlockSpec(memory_space=pltpu.VMEM)
    dma = pltpu.SemaphoreType.DMA
    shape = jax.ShapeDtypeStruct
    return pl.pallas_call(
        kernel,
        name="grads",
        out_shape=(
            shape((depth, planes * units), BF),
            shape((depth, planes * units), BF),
            shape((planes, contexts, unit_strip, depth), BF),
            shape((query_cols, depth), BF),
            shape((depth, qkv_cols), BF),
            shape((8, depth), F32),
        ),
        in_specs=[vmem] * 5 + [hbm] * 3,
        out_specs=(hbm, hbm, hbm, vmem, vmem, vmem),
        scratch_shapes=[
            pltpu.VMEM((1, contexts, out_strip, width), BF),
            pltpu.VMEM((planes, contexts, strip, qkv_cols), BF),
            pltpu.VMEM((outers, 1, out_strip, width), BF),
            pltpu.VMEM((outers, planes, strip, qkv_cols), BF),
            pltpu.VMEM((lots, 1, out_strip, width), BF),
            pltpu.VMEM((lots, planes, strip, qkv_cols), BF),
            pltpu.VMEM((lots, 1, out_strip, width), BF),
            pltpu.VMEM((lots, planes, strip, qkv_cols), BF),
            pltpu.VMEM((1, out_strip, width), BF),
            pltpu.VMEM((planes, strip, qkv_cols), BF),
            pltpu.VMEM((planes, out_strip, depth), BF),
            pltpu.VMEM((planes, strip, qkv_cols), BF),
            pltpu.VMEM((planes, 8, depth), F32),
            pltpu.VMEM((lots, 8, depth), F32),
            pltpu.VMEM((8, depth), F32),
            pltpu.VMEM((2, 8, depth), F32),
            dma((2, outers)),
            dma((2, outers)),
            dma((2, max(outers, 2))),
            dma((2, max(outers, 2))),
            dma((2, planes)),
            dma((2, planes)),
            dma((5, outers)),
            dma((5, outers)),
            dma((5, max(outers, 2))),
            dma((5, max(outers, 2))),
            dma((per_half + outers + 1,)),
            dma((planes + outers + 1,)),
            dma((3,)),
        ],
        compiler_params=pltpu.CompilerParams(
            collective_id=2, has_side_effects=True, vmem_limit_bytes=VMEM_LIMIT
        ),
        cost_estimate=pl.CostEstimate(flops=4 * 10**9, bytes_accessed=40 * 10**6, transcendentals=0),
    )


def shards(
    tokens,
    span_order,
    attn_gain,
    w_query,
    key_weight,
    value_weight,
    w_out,
    mlp_gain,
    w_gate,
    w_up,
    w_down,
    out_grad,
):
    planes = lax.axis_size("fsdp")
    contexts = lax.axis_size("context")
    c = lax.axis_index("context")
    tok_own, cot_own = tokens[0], out_grad[0]
    rows, own_cols = tok_own.shape
    width = own_cols * 2
    depth = width // planes
    units = w_gate.shape[1] // planes
    query_cols = w_query.shape[1]
    kv_cols = key_weight.shape[1]
    sizes = (planes, contexts, rows, width, query_cols, kv_cols, units)

    half_rows = rows // 2
    slot = jnp.arange(rows, dtype=jnp.int32)

    def positions(index):
        spans = lax.dynamic_index_in_dim(span_order, index, 0, keepdims=False)
        return jnp.where(slot < half_rows, spans[0], spans[1]) * half_rows + slot % half_rows

    pos_mine = positions(c)
    pos_q = jnp.broadcast_to(pos_mine[None, :], (8, rows))
    pos_k = jnp.concatenate([positions(i) for i in range(contexts)])[:, None]
    angles = pos_mine.astype(F32)[:, None] * rope_freqs(HEAD_WIDTH)[None, :]
    cosine, sine = jnp.cos(angles), jnp.sin(angles)
    cosine_table = jnp.concatenate([cosine] * 4, 1)
    sine_table = jnp.concatenate([-sine, sine] * 2, 1)

    qkv_own = jnp.concatenate([w_query, key_weight, value_weight], 1)
    gains_own = jnp.concatenate(
        [attn_gain[None], mlp_gain[None], jnp.zeros((GAIN_ROWS - 2, depth), BF)], 0
    )
    (
        gate_w, up_w, down_w, cot_all, norm_all, qkv_w, out_w, gains, q_pad, kv_all, attn, log_sum, mid_own,
        normed_one, tok_all, scales,
    ) = build_front(*sizes)(
        tok_own, cot_own, gains_own, qkv_own, w_out, w_gate, w_up, w_down, cosine_table, sine_table, pos_q, pos_k
    )
    result, input_grad, gate_strip, up_strip, down_strip, mid_full, qkv_grad, gain_rows = build_back(*sizes)(
        gate_w, up_w, down_w, norm_all, cot_all, qkv_w, out_w, q_pad, kv_all, mid_own, tok_all, gains,
        cosine_table, sine_table, pos_q, pos_k, log_sum, scales,
    )
    gate_out, up_out, down_out, out_out, qkv_out, gain_out = build_grads(*sizes)(
        attn, mid_full, normed_one, qkv_grad, gain_rows, gate_strip, up_strip, down_strip
    )
    qkv_out = qkv_out.astype(F32)
    return (
        result[None],
        input_grad[None],
        gain_out[0],
        qkv_out[:, :query_cols],
        qkv_out[:, query_cols : query_cols + kv_cols],
        qkv_out[:, query_cols + kv_cols :],
        out_out.astype(F32),
        gain_out[1],
        gate_out.astype(F32),
        up_out.astype(F32),
        down_out.reshape(planes * units, depth).astype(F32),
    )


def solution(mesh):
    weight = P("fsdp", "tensor")
    turned = P("tensor", "fsdp")
    block = P("fsdp", "context", "tensor")
    gain = P("fsdp")
    return jax.shard_map(
        shards,
        mesh=mesh,
        in_specs=(
            block, P(), gain, weight, weight, weight, turned, gain, weight, weight, turned, block,
        ),
        out_specs=(
            block, block, gain, weight, weight, weight, turned, gain, weight, weight, turned,
        ),
        check_vma=False,
    )
```

```python
import math

import jax
import jax.numpy as jnp
from jax import lax
from jax.experimental import pallas as pl
from jax.experimental.pallas import tpu as pltpu
from jax.sharding import PartitionSpec as P

HEAD_WIDTH = 64
EPS = 1e-05
NEG = -1e30
BF = jnp.bfloat16
F32 = jnp.float32
LANES = 128
TILE = 256
WIDE = 512
FACTOR = 1.0 / math.sqrt(HEAD_WIDTH)
VMEM_LIMIT = 62 * 2**20
MESH = pl.DeviceIdType.MESH


def rope_freqs(head_size):
    half_size = head_size // 2
    index = jnp.arange(half_size, dtype=jnp.float32)
    base_freq = jnp.exp(-(2.0 * index / head_size) * math.log(500000.0))
    wavelen = 2.0 * math.pi / base_freq
    smooth = (8192.0 / wavelen - 1.0) / 3.0
    blended = (1.0 - smooth) * base_freq / 32.0 + smooth * base_freq
    return jnp.where(
        wavelen > 8192.0, base_freq / 32.0, jnp.where(wavelen < 2048.0, base_freq, blended)
    )


def dot_t(left, right):
    return lax.dot_general(left, right, (((1,), (1,)), ((), ())), preferred_element_type=F32)


def t_dot(left, right):
    return lax.dot_general(left, right, (((0,), (0,)), ((), ())), preferred_element_type=F32)


def build_front(planes, contexts, rows, width, query_cols, kv_cols, units):
    outers = contexts // 2
    half = width // 2
    depth = width // planes
    strip = depth // contexts
    out_strip = query_cols // contexts
    unit_strip = units // contexts
    seq_len = rows * contexts
    n_q, n_kv = query_cols // LANES, kv_cols // LANES
    heads = query_cols // HEAD_WIDTH
    group = query_cols // kv_cols
    qkv_cols = query_cols + 2 * kv_cols
    QKV, OUT, GATE, UP, DOWN, COT, NORM, GAIN = range(8)

    def kernel(
        tok, cot, gain_one_own, gain_two_own, query_own, key_own, value_own, out_own, gate_own, up_own, down_own,
        spans, freqs,
        gate_w, up_w, down_w, cot_all, norm_all, qkv_hbm, out_hbm, gains, q_pad, kv_all, attn, log_sum,
        mid_own, normed_one, tok_all, scales, cosine, sine, pos_q, pos_k,
        qkv_w, out_w, gains_own, lin, heads_out, send_half, recv_half, norm_own, sq_send, sq_recv,
        z_send, z_recv, y_send, y_recv, k_send, k_recv, x_send, x_recv, own_sem,
    ):
        z = lax.axis_index("fsdp")
        c = lax.axis_index("context")
        t = lax.axis_index("tensor")
        o, k = c // 2, c % 2

        def at_z(p):
            return (p, c, t)

        def at_o(other):
            return (z, other * 2 + k, t)

        at_k = (z, o * 2 + 1 - k, t)
        at_x = (z, c, 1 - t)

        def copy(src, dst, send_sem, recv_sem, device):
            return pltpu.make_async_remote_copy(
                src_ref=src, dst_ref=dst, send_sem=send_sem, recv_sem=recv_sem,
                device_id=device, device_id_type=MESH,
            )

        barrier = pltpu.get_barrier_semaphore()
        peers = [at_z(lax.rem(z + s, planes)) for s in range(1, planes)]
        peers += [at_o(lax.rem(o + s, outers)) for s in range(1, outers)] + [at_k, at_x]
        for peer in peers:
            pl.semaphore_signal(barrier, inc=1, device_id=peer, device_id_type=MESH)
        pl.semaphore_wait(barrier, len(peers))

        order = []
        for i in range(planes - 1):
            p = jnp.int32(0)
            for plane in range(planes):
                far = sorted((abs(q - plane), q) for q in range(planes) if q != plane)
                p = p + jnp.where(z == plane, far[i][1], 0)
            order.append(p)

        def slot(item, p, q):
            if item == QKV:
                return qkv_w.at[pl.ds(p * depth + q * strip, strip), :]
            if item == OUT:
                return out_w.at[pl.ds(q * out_strip, out_strip), pl.ds(p * depth, depth)]
            if item == GATE:
                return gate_w.at[pl.ds(p * depth + q * strip, strip), :]
            if item == UP:
                return up_w.at[pl.ds(p * depth + q * strip, strip), :]
            if item == DOWN:
                return down_w.at[pl.ds(q * unit_strip, unit_strip), pl.ds(p * depth, depth)]
            if item == COT:
                return cot_all.at[p, :, pl.ds(t * half, half)]
            return norm_all.at[p, :, pl.ds(t * half, half)]

        def z_copy(item, p, src, goal, way):
            return copy(src, slot(item, p, c), z_send.at[item, p, way], z_recv.at[item, p], at_z(goal))

        def z_wait(item, p):
            z_copy(item, p, slot(item, p, c), z, 0).wait_recv()

        def spread(item, src):
            @pl.when(z + 1 < planes)
            def _():
                z_copy(item, z, src, z + 1, 0).start()

            @pl.when(z > 0)
            def _():
                z_copy(item, z, src, z - 1, 1).start()

        def spread_done(item, src):
            @pl.when(z + 1 < planes)
            def _():
                z_copy(item, z, src, z + 1, 0).wait_send()

            @pl.when(z > 0)
            def _():
                z_copy(item, z, src, z - 1, 1).wait_send()

        def passes_on(p):
            return ((p < z) & (z + 1 < planes)) | ((p > z) & (z > 0))

        def onward(p):
            return jnp.where(p < z, z + 1, z - 1)

        def forward(item, p):
            @pl.when(passes_on(p))
            def _():
                z_copy(item, p, slot(item, p, c), onward(p), 0).start()

        def forward_done(item, p):
            @pl.when(passes_on(p))
            def _():
                z_copy(item, p, slot(item, p, c), onward(p), 0).wait_send()

        def y_copy(item, p, by):
            here = slot(item, p, c)
            return copy(here, here, y_send.at[item, p, by], y_recv.at[item, p, by], at_o(lax.rem(o + by, outers)))

        def y_wait(item, p, by):
            there = slot(item, p, lax.rem(o - by + outers, outers) * 2 + k)
            copy(there, there, y_send.at[item, p, by], y_recv.at[item, p, by], at_k).wait_recv()

        def k_copy(item, p, by):
            here = slot(item, p, lax.rem(o - by + outers, outers) * 2 + k)
            return copy(here, here, k_send.at[item, p, by], k_recv.at[item, p, by], at_k)

        def k_wait(item, p, by):
            there = slot(item, p, lax.rem(o - by + outers, outers) * 2 + 1 - k)
            copy(there, there, k_send.at[item, p, by], k_recv.at[item, p, by], at_k).wait_recv()

        def share(item, p):
            for by in range(1, outers):
                y_copy(item, p, by).start()
            k_copy(item, p, 0).start()

        def share_on(item, p):
            for by in range(1, outers):
                y_wait(item, p, by)
                k_copy(item, p, by).start()

        def shared(item, p):
            for by in range(outers):
                k_wait(item, p, by)

        def share_done(item, p):
            for by in range(1, outers):
                y_copy(item, p, by).wait_send()
            for by in range(outers):
                k_copy(item, p, by).wait_send()

        def x_copy(i, src, dst):
            return copy(src, dst, x_send.at[i], x_recv.at[i], at_x)

        gains_own[...] = jnp.zeros_like(gains_own)
        gains_own[0:1, :] = gain_one_own[...].astype(F32)
        gains_own[1:2, :] = gain_two_own[...].astype(F32)
        tok_cols = pl.ds(t * half, half)
        tok_copy = x_copy(0, tok, tok_all.at[:, tok_cols])
        tok_copy.start()
        gain_copies = [
            copy(
                gains_own, gains.at[:, pl.ds(z * depth, depth)], z_send.at[GAIN, lax.rem(z + s, planes), 0],
                z_recv.at[GAIN, z], at_z(lax.rem(z + s, planes)),
            )
            for s in range(1, planes)
        ]
        for one in gain_copies:
            one.start()
        home = pl.ds(z * depth, depth)
        own_qkv = [
            pltpu.make_async_copy(query_own, qkv_w.at[home, pl.ds(0, query_cols)], own_sem.at[0]),
            pltpu.make_async_copy(key_own, qkv_w.at[home, pl.ds(query_cols, kv_cols)], own_sem.at[7]),
            pltpu.make_async_copy(value_own, qkv_w.at[home, pl.ds(query_cols + kv_cols, kv_cols)], own_sem.at[8]),
        ]
        for one in own_qkv:
            one.start()
        for one in own_qkv:
            one.wait()
        qkv_src = slot(QKV, z, c)
        out_src = out_own.at[pl.ds(c * out_strip, out_strip), :]
        spread(QKV, qkv_src)
        own_copies = [
            pltpu.make_async_copy(out_own, out_w.at[:, pl.ds(z * depth, depth)], own_sem.at[1]),
            pltpu.make_async_copy(
                gate_own.at[:, pl.ds(z * units, units)], gate_w.at[pl.ds(z * depth, depth), :], own_sem.at[2]
            ),
            pltpu.make_async_copy(
                up_own.at[:, pl.ds(z * units, units)], up_w.at[pl.ds(z * depth, depth), :], own_sem.at[3]
            ),
            pltpu.make_async_copy(
                down_own.at[pl.ds(z * units, units), :], down_w.at[:, pl.ds(z * depth, depth)], own_sem.at[4]
            ),
            pltpu.make_async_copy(cot, slot(COT, z, c), own_sem.at[5]),
        ]
        for one in own_copies:
            one.start()
        gains[:, pl.ds(z * depth, depth)] = gains_own[...]
        tok_all[:, tok_cols] = tok[...]

        def positions(q, shape, axis):
            r = lax.broadcasted_iota(jnp.int32, shape, axis)
            return jnp.where(r < rows // 2, spans[q, 0], spans[q, 1]) * (rows // 2) + lax.rem(r, rows // 2)

        for q in range(contexts):
            pos_k[q * rows : (q + 1) * rows, :] = positions(q, (rows, 1), 0)
        pos_q[...] = positions(c, (8, rows), 1)
        angle = positions(c, (rows, LANES), 0).astype(F32) * freqs[...]
        cosine[...] = jnp.cos(angle)
        side_of = lax.rem(lax.broadcasted_iota(jnp.int32, (rows, LANES), 1), HEAD_WIDTH) < HEAD_WIDTH // 2
        sine[...] = jnp.where(side_of, -jnp.sin(angle), jnp.sin(angle))

        tok_copy.wait()
        for s in range(1, planes):
            p = lax.rem(z + s, planes)
            there = gains.at[:, pl.ds(p * depth, depth)]
            copy(there, there, z_send.at[GAIN, p, 0], z_recv.at[GAIN, p], at_k).wait_recv()
        x = tok_all[...].astype(F32)
        scale = lax.rsqrt(jnp.mean(x * x, -1, keepdims=True) + EPS)
        scales[0] = jnp.broadcast_to(scale, (rows, LANES))
        normed_one[...] = (x * scale * gains[0:1, :].astype(F32)).astype(BF)

        for p in order:
            z_wait(QKV, p)
            forward(QKV, p)
            share(QKV, p)

        spread(OUT, out_src)
        sends = []

        def send_units(item):
            for s in range(1, planes):
                goal = lax.rem(z + s, planes)
                if item == DOWN:
                    src = down_own.at[pl.ds(goal * units + c * unit_strip, unit_strip), :]
                else:
                    own = gate_own if item == GATE else up_own
                    src = own.at[pl.ds(c * strip, strip), pl.ds(goal * units, units)]
                one = z_copy(item, z, src, goal, s - 1)
                one.start()
                sends.append(one)

        def share_units(item):
            for s in range(1, planes):
                p = lax.rem(z + planes - s, planes)
                z_wait(item, p)
                share(item, p)

        items = (GATE, UP, DOWN)
        send_units(GATE)
        for p in order:
            share_on(QKV, p)
            z_wait(OUT, p)
            forward(OUT, p)
            share(OUT, p)
        send_units(UP)
        for p in order:
            shared(QKV, p)
        qkv_keep = pltpu.make_async_copy(qkv_w, qkv_hbm, own_sem.at[0])
        qkv_keep.start()

        n_tile = 2 * LANES

        @pl.loop(0, qkv_cols // n_tile)
        def _(i):
            cols = pl.ds(pl.multiple_of(i * n_tile, n_tile), n_tile)
            found = jnp.dot(normed_one[...], qkv_w[:, cols], preferred_element_type=F32)
            lin[2 * i] = found[:, :LANES]
            lin[2 * i + 1] = found[:, LANES:]

        lane = lax.broadcasted_iota(jnp.int32, (rows, LANES), 1)
        first = lax.rem(lane, HEAD_WIDTH) < HEAD_WIDTH // 2
        low = lane < HEAD_WIDTH

        def rotated(u):
            partner = jnp.where(
                first, pltpu.roll(u, LANES - HEAD_WIDTH // 2, 1), pltpu.roll(u, HEAD_WIDTH // 2, 1)
            )
            return u * cosine[...] + partner * sine[...]

        for i in range(n_kv):
            kv_all[c, i] = rotated(lin[n_q + i]).astype(BF)
            kv_all[c, n_kv + i] = lin[n_q + n_kv + i].astype(BF)

        def kv_slot(q):
            return kv_all.at[q]

        kv_sends = [
            copy(kv_slot(c), kv_slot(c), y_send.at[COT, 0, by], y_recv.at[COT, 0, by], at_o(lax.rem(o + by, outers)))
            for by in range(1, outers)
        ]
        kv_sends.append(copy(kv_slot(c), kv_slot(c), k_send.at[COT, 0, 0], k_recv.at[COT, 0, 0], at_k))
        for one in kv_sends:
            one.start()

        @pl.loop(0, n_q)
        def _(j):
            u = rotated(lin[j]).astype(BF).astype(F32) * FACTOR
            side = lax.rem((2 * j) // group, 2)
            lo = jnp.where(low, u, 0.0)
            hi = jnp.where(low, 0.0, u)
            q_pad[2 * j] = jnp.where(side == 0, lo, pltpu.roll(lo, HEAD_WIDTH, 1)).astype(BF)
            q_pad[2 * j + 1] = jnp.where(side == 1, hi, pltpu.roll(hi, HEAD_WIDTH, 1)).astype(BF)

        for by in range(1, outers):
            q = lax.rem(o - by + outers, outers) * 2 + k
            copy(kv_slot(q), kv_slot(q), y_send.at[COT, 0, by], y_recv.at[COT, 0, by], at_k).wait_recv()
            one = copy(kv_slot(q), kv_slot(q), k_send.at[COT, 0, by], k_recv.at[COT, 0, by], at_k)
            one.start()
            kv_sends.append(one)
        for by in range(outers):
            q = lax.rem(o - by + outers, outers) * 2 + 1 - k
            copy(kv_slot(q), kv_slot(q), k_send.at[COT, 0, by], k_recv.at[COT, 0, by], at_k).wait_recv()

        send_units(DOWN)
        spread(COT, cot)
        cot_copy = x_copy(1 + z, cot, slot(COT, z, c))
        cot_copy.start()

        def attend(first_head, last_head):
            @pl.loop(first_head, last_head)
            def _(h):
                pair = h // (2 * group)
                keys = kv_all[:, pair].reshape(seq_len, LANES)
                values = kv_all[:, n_kv + pair].reshape(seq_len, LANES)
                scores = dot_t(keys, q_pad[h])
                scores = jnp.where(pos_q[0:1, :] >= pos_k[...], scores, NEG)
                top = jnp.max(scores, 0, keepdims=True)
                expo = jnp.exp(scores - top)
                total = jnp.sum(expo, 0, keepdims=True)
                weights = (expo * (1.0 / total)).astype(BF)
                heads_out[h] = t_dot(values, weights).T
                log_sum[pl.ds(h, 1), :] = top + jnp.log(total)

        attend(0, heads // 2)
        for p in order:
            share_on(OUT, p)
        share_units(GATE)
        attend(heads // 2, heads)

        for j in range(n_q):
            side = (2 * j) // group % 2
            lo, hi = heads_out[2 * j], heads_out[2 * j + 1]
            if side == 0:
                hi = pltpu.roll(hi, HEAD_WIDTH, 1)
            else:
                lo = pltpu.roll(lo, HEAD_WIDTH, 1)
            attn[:, j * LANES : (j + 1) * LANES] = jnp.where(low, lo, hi).astype(BF)

        for p in order:
            shared(OUT, p)
        own_copies[0].wait()
        out_keep = pltpu.make_async_copy(out_w, out_hbm, own_sem.at[7])
        out_keep.start()

        n_out = half // n_tile

        @pl.loop(0, n_out)
        def _(i):
            cols = pl.ds(pl.multiple_of((1 - t) * half + i * n_tile, n_tile), n_tile)
            here = pl.ds(pl.multiple_of(i * n_tile, n_tile), n_tile)
            send_half[:, here] = jnp.dot(attn[...], out_w[:, cols], preferred_element_type=F32).astype(BF)

        half_copy = x_copy(1 + planes, send_half, recv_half)
        half_copy.start()

        @pl.loop(0, n_out)
        def _(i):
            cols = pl.ds(pl.multiple_of(t * half + i * n_tile, n_tile), n_tile)
            here = pl.ds(pl.multiple_of(i * n_tile, n_tile), n_tile)
            part = jnp.dot(attn[...], out_w[:, cols], preferred_element_type=F32)
            mid_own[:, here] = tok[:, here].astype(F32) + part

        share_units(UP)
        half_copy.wait_recv()
        mid = mid_own[...] + recv_half[...].astype(F32)
        mid_own[...] = mid
        squares = jnp.sum(mid * mid, -1, keepdims=True)
        sq_send[...] = jnp.broadcast_to(squares, (rows, LANES))
        sq_copy = x_copy(2 + planes, sq_send, sq_recv)
        sq_copy.start()
        sq_copy.wait_recv()
        scale_two = lax.rsqrt((squares + sq_recv[:, 0:1]) * (1.0 / width) + EPS)
        scales[1] = jnp.broadcast_to(scale_two, (rows, LANES))
        gain_two = gains[1:2, pl.ds(pl.multiple_of(t * half, half), half)].astype(F32)
        norm_own[...] = (mid_own[...] * scale_two * gain_two).astype(BF)

        spread(NORM, norm_own)
        norm_copy = x_copy(3 + planes + z, norm_own, slot(NORM, z, c))
        norm_copy.start()
        norm_keep = pltpu.make_async_copy(norm_own, slot(NORM, z, c), own_sem.at[6])
        norm_keep.start()
        share_units(DOWN)
        for i, p in enumerate(order):
            z_wait(NORM, p)
            forward(NORM, p)
            x_copy(3 + planes + p, slot(NORM, p, c), slot(NORM, p, c)).start()
            z_wait(COT, p)
            forward(COT, p)
            x_copy(1 + p, slot(COT, p, c), slot(COT, p, c)).start()
            for item in items:
                share_on(item, lax.rem(z + planes - 1 - i, planes))

        for s in range(1, planes):
            p = lax.rem(z + s, planes)
            for item in items:
                shared(item, p)
        for p in [z] + order:
            for base, item in ((1, COT), (3 + planes, NORM)):
                there = (cot_all if item == COT else norm_all).at[p, :, pl.ds((1 - t) * half, half)]
                copy(there, there, x_send.at[base + p], x_recv.at[base + p], at_x).wait_recv()
        for one in own_copies[1:] + [qkv_keep, out_keep]:
            one.wait()
        norm_keep.wait()
        tok_copy_out = [half_copy, sq_copy, cot_copy, norm_copy]
        for one in gain_copies + sends + kv_sends + tok_copy_out:
            one.wait_send()
        spread_done(QKV, qkv_src)
        spread_done(OUT, out_src)
        spread_done(COT, cot)
        spread_done(NORM, norm_own)
        for p in order:
            for item in (QKV, OUT, COT, NORM):
                forward_done(item, p)
            for item in (QKV, OUT, GATE, UP, DOWN):
                share_done(item, p)
            x_copy(1 + p, slot(COT, p, c), slot(COT, p, c)).wait_send()
            x_copy(3 + planes + p, slot(NORM, p, c), slot(NORM, p, c)).wait_send()

    hbm = pl.BlockSpec(memory_space=pl.ANY)
    vmem = pl.BlockSpec(memory_space=pltpu.VMEM)
    dma = pltpu.SemaphoreType.DMA
    shape = jax.ShapeDtypeStruct
    return pl.pallas_call(
        kernel,
        name="front",
        out_shape=(
            shape((width, units), BF),
            shape((width, units), BF),
            shape((units, width), BF),
            shape((planes, rows, width), BF),
            shape((planes, rows, width), BF),
            shape((width, qkv_cols), BF),
            shape((query_cols, width), BF),
            shape((8, width), F32),
            shape((heads, rows, LANES), BF),
            shape((contexts, 2 * n_kv, rows, LANES), BF),
            shape((rows, query_cols), BF),
            shape((heads, rows), F32),
            shape((rows, half), F32),
            shape((rows, width), BF),
            shape((rows, width), BF),
            shape((2, rows, LANES), F32),
            shape((rows, LANES), F32),
            shape((rows, LANES), F32),
            shape((8, rows), jnp.int32),
            shape((seq_len, 1), jnp.int32),
        ),
        in_specs=[vmem, hbm, vmem, vmem] + [hbm] * 7 + [pl.BlockSpec(memory_space=pltpu.SMEM), vmem],
        out_specs=(hbm,) * 7 + (vmem,) * 13,
        scratch_shapes=[
            pltpu.VMEM((width, qkv_cols), BF),
            pltpu.VMEM((query_cols, width), BF),
            pltpu.VMEM((8, depth), F32),
            pltpu.VMEM((qkv_cols // LANES, rows, LANES), F32),
            pltpu.VMEM((heads, rows, LANES), F32),
            pltpu.VMEM((rows, half), BF),
            pltpu.VMEM((rows, half), BF),
            pltpu.VMEM((rows, half), BF),
            pltpu.VMEM((rows, LANES), F32),
            pltpu.VMEM((rows, LANES), F32),
            dma((8, planes, planes)),
            dma((8, planes)),
            dma((6, planes, max(outers, 2))),
            dma((6, planes, max(outers, 2))),
            dma((6, planes, max(outers, 2))),
            dma((6, planes, max(outers, 2))),
            dma((3 + 2 * planes,)),
            dma((3 + 2 * planes,)),
            dma((9,)),
        ],
        compiler_params=pltpu.CompilerParams(
            collective_id=0, has_side_effects=True, vmem_limit_bytes=VMEM_LIMIT
        ),
        cost_estimate=pl.CostEstimate(flops=8 * 10**9, bytes_accessed=80 * 10**6, transcendentals=4 * 10**6),
    )


def add_strips(total, terms, chunk):
    lead, size, _ = total.shape
    steps = size // chunk

    @pl.loop(0, lead * steps)
    def _(i):
        a, r = i // steps, pl.ds(pl.multiple_of(lax.rem(i, steps) * chunk, chunk), chunk)
        found = terms[0][a, r, :].astype(F32)
        for term in terms[1:]:
            found = found + term[a, r, :].astype(F32)
        total[a, r, :] = found.astype(BF)


class Ring:
    def __init__(self, planes, contexts):
        self.planes, self.outers = planes, contexts // 2
        self.z = z = lax.axis_index("fsdp")
        self.c = c = lax.axis_index("context")
        self.t = t = lax.axis_index("tensor")
        self.o, self.k = c // 2, c % 2
        self.at_k = (z, self.o * 2 + 1 - self.k, t)
        self.at_x = (z, c, 1 - t)

    def at_z(self, p):
        return (p, self.c, self.t)

    def at_o(self, other):
        return (self.z, other * 2 + self.k, self.t)

    def after(self, by):
        return lax.rem(self.o + by, self.outers)

    def before(self, by):
        return lax.rem(self.o - by + self.outers, self.outers)

    def plane(self, by):
        return lax.rem(self.z + by, self.planes)

    def greet(self):
        barrier = pltpu.get_barrier_semaphore()
        peers = [self.at_z(self.plane(s)) for s in range(1, self.planes)]
        peers += [self.at_o(self.after(s)) for s in range(1, self.outers)] + [self.at_k, self.at_x]
        for peer in peers:
            pl.semaphore_signal(barrier, inc=1, device_id=peer, device_id_type=MESH)
        pl.semaphore_wait(barrier, len(peers))

    def by_distance(self):
        order = []
        for i in range(self.planes - 1):
            p = jnp.int32(0)
            for plane in range(self.planes):
                far = sorted((abs(q - plane), q) for q in range(self.planes) if q != plane)
                p = p + jnp.where(self.z == plane, far[i][1], 0)
            order.append(p)
        return order


def copy_to(src, dst, send_sem, recv_sem, device):
    return pltpu.make_async_remote_copy(
        src_ref=src, dst_ref=dst, send_sem=send_sem, recv_sem=recv_sem, device_id=device, device_id_type=MESH
    )


class Reduction:
    def __init__(self, ring, item, part, core_in, outer_out, outer_in, strip_sum, sems):
        self.ring, self.item, self.part = ring, item, part
        self.core_in, self.outer_out, self.outer_in, self.strip_sum = core_in, outer_out, outer_in, strip_sum
        self.k_send, self.k_recv, self.y_send, self.y_recv = sems
        self.chunk = 32 if strip_sum.shape[2] > 1024 else 64
        self.chunk = min(self.chunk, strip_sum.shape[1])

    def core_copy(self, other):
        g = self.ring
        return copy_to(
            self.part.at[:, other * 2 + 1 - g.k], self.core_in.at[other],
            self.k_send.at[self.item, other], self.k_recv.at[self.item, other], g.at_k,
        )

    def to_core(self):
        for other in range(self.ring.outers):
            self.core_copy(other).start()

    def outer_copy(self, by):
        g = self.ring
        return copy_to(
            self.outer_out.at[by - 1], self.outer_in.at[by - 1],
            self.y_send.at[self.item, by], self.y_recv.at[self.item, by], g.at_o(g.after(by)),
        )

    def from_core(self):
        g = self.ring
        for other in range(g.outers):
            self.core_copy(other).wait_recv()
        for by in range(1, g.outers):
            goal = g.after(by)
            add_strips(
                self.outer_out.at[by - 1], [self.part.at[:, goal * 2 + g.k], self.core_in.at[goal]], self.chunk
            )
            self.outer_copy(by).start()
        add_strips(self.strip_sum, [self.part.at[:, g.c], self.core_in.at[g.o]], self.chunk)

    def core_done(self):
        for other in range(self.ring.outers):
            self.core_copy(other).wait_send()

    def from_outer(self):
        for by in range(1, self.ring.outers):
            self.outer_copy(by).wait_recv()
        terms = [self.strip_sum] + [self.outer_in.at[by - 1] for by in range(1, self.ring.outers)]
        if len(terms) > 1:
            add_strips(self.strip_sum, terms, self.chunk)

    def outer_done(self):
        for by in range(1, self.ring.outers):
            self.outer_copy(by).wait_send()


class Share:
    def __init__(self, ring, item, slot, sems, source=None):
        self.ring, self.item, self.slot = ring, item, slot
        self.source = slot(ring.c) if source is None else source
        self.y_send, self.y_recv, self.k_send, self.k_recv = sems

    def outer_copy(self, by):
        g = self.ring
        return copy_to(
            self.source, self.slot(g.c), self.y_send.at[self.item, by], self.y_recv.at[self.item, by],
            g.at_o(g.after(by)),
        )

    def core_copy(self, by):
        g = self.ring
        there = self.slot(g.before(by) * 2 + g.k)
        return copy_to(
            self.source if by == 0 else there, there, self.k_send.at[self.item, by], self.k_recv.at[self.item, by],
            g.at_k,
        )

    def start(self):
        for by in range(1, self.ring.outers):
            self.outer_copy(by).start()
        self.core_copy(0).start()

    def pass_on(self):
        g = self.ring
        for by in range(1, g.outers):
            there = self.slot(g.before(by) * 2 + g.k)
            copy_to(there, there, self.y_send.at[self.item, by], self.y_recv.at[self.item, by], g.at_k).wait_recv()
            self.core_copy(by).start()

    def finish(self):
        g = self.ring
        for by in range(g.outers):
            there = self.slot(g.before(by) * 2 + 1 - g.k)
            copy_to(there, there, self.k_send.at[self.item, by], self.k_recv.at[self.item, by], g.at_k).wait_recv()
        for by in range(1, g.outers):
            self.outer_copy(by).wait_send()
        for by in range(g.outers):
            self.core_copy(by).wait_send()


def rotate_tile(u, cosine, sine, first):
    partner = jnp.where(
        first, pltpu.roll(u, LANES - HEAD_WIDTH // 2, 1), pltpu.roll(u, HEAD_WIDTH // 2, 1)
    )
    return u * cosine + partner * sine


def store_part(part, i, tile):
    size = part.shape[2]
    per = part.shape[1] * size // TILE
    for r in range(TILE // size):
        part[i // per, lax.rem(i, per) * (TILE // size) + r] = tile[r * size : (r + 1) * size].astype(BF)


def build_back(planes, contexts, rows, width, query_cols, kv_cols, units):
    outers = contexts // 2
    half = width // 2
    depth = width // planes
    strip = depth // contexts
    unit_strip = units // contexts
    seq_len = rows * contexts
    n_q, n_kv = query_cols // LANES, kv_cols // LANES
    heads = query_cols // HEAD_WIDTH
    group = query_cols // kv_cols
    qkv_cols = query_cols + 2 * kv_cols
    DOWN, GATE, UP, KV = range(4)
    lots = max(outers - 1, 1)

    def kernel(
        gate_hbm, up_hbm, down_hbm, norm_hbm, cot_hbm, qkv_hbm, out_hbm, q_hbm, kv_hbm, mid_hbm, tok_hbm,
        gains, cosine, sine, pos_q, pos_k, log_sum, scales,
        input_grad, gate_out, up_strip, down_out, mid_full, qkv_grad, gain_rows, mlp_part,
        norm_x_in, norm_z_in, norm_x_out, norm_sum, mlp_stage,
        row_core_in, col_core_in, row_outer_in, col_outer_in, row_outer_out, col_outer_out, row_sum, col_sum,
        kv_core_in, kv_outer_in, sq_out, sq_in, first_x_out, first_x_in,
        x_send, x_recv, z_send, z_recv, k_send, k_recv, y_send, y_recv, grad_send, grad_recv, sy_send, sy_recv, sk_send,
        sk_recv, load_sem, stage_sem, credit,
    ):
        ring = Ring(planes, contexts)
        z, c, t, k, o = ring.z, ring.c, ring.t, ring.k, ring.o
        order = ring.by_distance()
        blocks = order[::-1] + [z]
        ring.greet()
        own_cols = pl.multiple_of(t * half, half)
        other_cols = pl.multiple_of((1 - t) * half, half)
        n_half = half // WIDE

        def x_copy(i, src, dst):
            return copy_to(src, dst, x_send.at[i], x_recv.at[i], ring.at_x)

        NORM, MID, SQ_TWO, FIRST, SQ_ONE = 0, planes, planes + 1, planes + 2, planes + 3

        def norm_x(i):
            return x_copy(NORM + i, norm_x_out.at[i % 2], norm_x_in.at[blocks[i]])

        def back_from(p, here):
            return lax.rem(p - here + planes, planes) - 1

        def norm_z(p):
            return copy_to(
                norm_sum.at[p], norm_z_in.at[back_from(z, p)], z_send.at[0, p], z_recv.at[0, z], ring.at_z(p)
            )

        def norm_z_wait(p):
            there = norm_z_in.at[back_from(p, z)]
            copy_to(there, there, z_send.at[0, p], z_recv.at[0, p], ring.at_k).wait_recv()

        def add_block(total, other, p):
            n = rows // 64

            @pl.loop(0, n)
            def _(i):
                r = pl.ds(pl.multiple_of(i * 64, 64), 64)
                total[p, r, :] = (total[p, r, :].astype(F32) + other[p, r, :].astype(F32)).astype(BF)

        def norm_on(i):
            norm_x(i).wait_recv()
            add_block(norm_sum, norm_x_in, blocks[i])

        sems = (k_send, k_recv, y_send, y_recv)

        def feed_forward(norm, cot, hid, gate_grad, up_grad):
            def load(i, src, dst):
                one = pltpu.make_async_copy(src, dst, load_sem.at[i])
                one.start()
                return one

            loads = [
                (load(2 * i, norm_hbm.at[p], norm.at[p]), load(2 * i + 1, cot_hbm.at[p], cot.at[p]))
                for i, p in enumerate(blocks)
            ]

            def product(part, left, right):
                total = planes * rows

                @pl.loop(0, left.shape[2] // TILE)
                def _(i):
                    cols = pl.ds(pl.multiple_of(i * TILE, TILE), TILE)
                    tile = t_dot(left[:, :, cols].reshape(total, TILE), right[...].reshape(total, right.shape[2]))
                    store_part(part, i, tile)

            def with_weights(gate_w, up_w, down_w, col_part):
                weights = [
                    load(2 * planes, gate_hbm, gate_w),
                    load(2 * planes + 1, up_hbm, up_w),
                    load(2 * planes + 2, down_hbm, down_w),
                ]
                for one in weights:
                    one.wait()
                def forward_block(i):
                    p = blocks[i]
                    loads[i][0].wait()
                    loads[i][1].wait()

                    @pl.loop(0, units // TILE)
                    def _(j):
                        cols = pl.ds(pl.multiple_of(j * TILE, TILE), TILE)
                        gate = jnp.dot(norm[p], gate_w[:, cols], preferred_element_type=F32)
                        up = jnp.dot(norm[p], up_w[:, cols], preferred_element_type=F32)
                        grad = dot_t(cot[p], down_w[cols, :])
                        sig = jax.nn.sigmoid(gate)
                        act = gate * sig
                        hid[p, :, cols] = (act * up).astype(BF)
                        gate_grad[p, :, cols] = (grad * up * sig * (1.0 + gate * (1.0 - sig))).astype(BF)
                        up_grad[p, :, cols] = (grad * act).astype(BF)

                def norm_block(i):
                    p = blocks[i]

                    def tile_of(at):
                        r = pl.ds(pl.multiple_of(at, WIDE), WIDE)
                        return dot_t(gate_grad[p], gate_w[r, :]) + dot_t(up_grad[p], up_w[r, :])

                    if i > 1:
                        norm_x(i - 2).wait_send()

                    @pl.loop(0, n_half)
                    def _(j):
                        here = pl.ds(pl.multiple_of(j * WIDE, WIDE), WIDE)
                        norm_x_out[i % 2, :, here] = tile_of(other_cols + j * WIDE).astype(BF)

                    norm_x(i).start()

                    @pl.loop(0, n_half)
                    def _(j):
                        here = pl.ds(pl.multiple_of(j * WIDE, WIDE), WIDE)
                        norm_sum[p, :, here] = tile_of(own_cols + j * WIDE).astype(BF)

                    if i > 0:
                        norm_on(i - 1)
                        norm_z(blocks[i - 1]).start()

                down = Reduction(
                    ring, DOWN, col_part, col_core_in, col_outer_out, col_outer_in, col_sum, sems
                )
                for i in range(planes):
                    forward_block(i)
                    norm_block(i)
                product(col_part, hid, cot)
                down.to_core()

                def stage_copy(i):
                    return pltpu.make_async_copy(mlp_stage.at[i % 2], mlp_part.at[blocks[i]], stage_sem.at[i % 2])

                for i, p in enumerate(blocks):
                    if i > 1:
                        stage_copy(i - 2).wait()

                    @pl.loop(0, width // WIDE)
                    def _(j):
                        r = pl.ds(pl.multiple_of(j * WIDE, WIDE), WIDE)
                        mlp_stage[i % 2, :, r] = jnp.dot(hid[p], down_w[:, r], preferred_element_type=F32).astype(BF)

                    stage_copy(i).start()
                    if i == 0:
                        down.from_core()
                for i in range(max(planes - 2, 0), planes):
                    stage_copy(i).wait()
                down.core_done()

            pl.run_scoped(
                with_weights,
                pltpu.VMEM((width, units), BF), pltpu.VMEM((width, units), BF), pltpu.VMEM((units, width), BF),
                pltpu.VMEM((1, contexts, unit_strip, width), BF),
            )

            def with_parts(row_part):
                gate = Reduction(
                    ring, GATE, row_part, row_core_in, row_outer_out.at[0], row_outer_in.at[0], row_sum.at[0], sems
                )
                up = Reduction(
                    ring, UP, row_part, row_core_in, row_outer_out.at[1], row_outer_in.at[1], row_sum.at[1], sems
                )
                product(row_part, norm, gate_grad)
                gate.to_core()
                norm_on(planes - 1)
                gate.from_core()
                gate.core_done()
                pl.semaphore_signal(credit, inc=1, device_id=ring.at_k, device_id_type=MESH)
                product(row_part, norm, up_grad)
                pl.semaphore_wait(credit, 1)
                up.to_core()
                up.from_core()
                up.core_done()

            pl.run_scoped(with_parts, pltpu.VMEM((planes, contexts, strip, units), BF))

        block_bf = pltpu.VMEM((planes, rows, width), BF)
        unit_bf = pltpu.VMEM((planes, rows, units), BF)
        pl.run_scoped(feed_forward, block_bf, block_bf, unit_bf, unit_bf, unit_bf)

        down = Reduction(ring, DOWN, None, None, col_outer_out, col_outer_in, col_sum, sems)
        gate = Reduction(ring, GATE, None, None, row_outer_out.at[0], row_outer_in.at[0], row_sum.at[0], sems)
        up = Reduction(ring, UP, None, None, row_outer_out.at[1], row_outer_in.at[1], row_sum.at[1], sems)

        def strip_src(item, goal):
            if item == DOWN:
                return col_sum.at[0, :, pl.ds(pl.multiple_of(goal * depth, depth), depth)]
            return row_sum.at[0 if item == GATE else 1, goal]

        def strip_dst(item, home):
            if item == DOWN:
                return down_out.at[home, c]
            cols = pl.ds(pl.multiple_of(home * units, units), units)
            if item == GATE:
                return gate_out.at[pl.ds(pl.multiple_of(c * strip, strip), strip), cols]
            return up_strip.at[:, cols]

        def strip_copy(item, s):
            goal = ring.plane(s)
            return copy_to(
                strip_src(item, goal), strip_dst(item, z), grad_send.at[item, s], grad_recv.at[item, z], ring.at_z(goal)
            )

        def strip_keep(item):
            return pltpu.make_async_copy(strip_src(item, z), strip_dst(item, z), grad_send.at[item, 0])

        def to_planes(item, reduction):
            reduction.from_outer()
            for s in range(1, planes):
                strip_copy(item, s).start()
            strip_keep(item).start()

        def from_planes(item):
            for s in range(1, planes):
                p = ring.plane(s)
                there = strip_dst(item, p)
                copy_to(there, there, grad_send.at[item, s], grad_recv.at[item, p], ring.at_k).wait_recv()
            strip_keep(item).wait()

        share_sems = (sy_send, sy_recv, sk_send, sk_recv)
        down_share = Share(ring, 0, lambda q: down_out.at[:, q], share_sems)
        gate_share = Share(ring, 1, lambda q: gate_out.at[pl.ds(pl.multiple_of(q * strip, strip), strip), :], share_sems)

        def attention(mid_grad, q_pad, kv_all, tok, grad_pad, query_out, key_sum, value_sum, kv_grad, kv_out):
            loads = [
                pltpu.make_async_copy(mid_hbm, mid_grad, load_sem.at[0]),
                pltpu.make_async_copy(tok_hbm.at[:, pl.ds(own_cols, half)], tok, load_sem.at[1]),
                pltpu.make_async_copy(q_hbm, q_pad, load_sem.at[2]),
                pltpu.make_async_copy(kv_hbm, kv_all, load_sem.at[3]),
                pltpu.make_async_copy(cot_hbm.at[z, :, pl.ds(own_cols, half)], first_x_out, load_sem.at[4]),
            ]
            for one in loads:
                one.start()
            for one in loads:
                one.wait()
            key_sum[...] = jnp.zeros_like(key_sum)
            value_sum[...] = jnp.zeros_like(value_sum)
            gain_rows[...] = jnp.zeros_like(gain_rows)

            def norm_back(grad, normal, scale, gain, gain_row, i):
                scaled = grad * gain
                gain_rows[gain_row : gain_row + 1, :] = jnp.sum(grad * normal, 0, keepdims=True)
                mine = jnp.sum(scaled * normal, -1, keepdims=True)
                sq_out[i] = jnp.broadcast_to(mine, (rows, LANES))
                swap = x_copy(SQ_TWO if i == 0 else SQ_ONE, sq_out.at[i], sq_in.at[i])
                swap.start()
                swap.wait()
                inner = (mine + sq_in[i][:, 0:1]) * (1.0 / width)
                return scale * (scaled - normal * inner)

            for p in order:
                norm_z_wait(p)
            grad = norm_sum[z].astype(F32)
            for p in order:
                grad = grad + norm_z_in[back_from(p, z)].astype(F32)
            scale_two = scales[1][:, 0:1]
            gain_two = gains[1:2, pl.ds(own_cols, half)].astype(F32)
            back = norm_back(grad, mid_grad[...] * scale_two, scale_two, gain_two, 1, 0)
            mid_grad[...] = first_x_out[...].astype(F32) + back
            mine = mid_full.at[:, pl.ds(own_cols, half)]
            mid_full[:, pl.ds(own_cols, half)] = mid_grad[...].astype(BF)
            mid_swap = x_copy(MID, mine, mine)
            mid_swap.start()
            to_planes(DOWN, down)
            mid_swap.wait_recv()

            lane = lax.broadcasted_iota(jnp.int32, (rows, LANES), 1)
            first = lax.rem(lane, HEAD_WIDTH) < HEAD_WIDTH // 2
            low = lane < HEAD_WIDTH

            def with_out(out_w):
                one = pltpu.make_async_copy(out_hbm, out_w, load_sem.at[0])
                one.start()
                one.wait()

                @pl.loop(0, query_cols // TILE)
                def _(i):
                    r = pl.ds(pl.multiple_of(i * TILE, TILE), TILE)
                    found = dot_t(mid_full[...], out_w[r, :])
                    for half_tile in range(TILE // LANES):
                        j = i * (TILE // LANES) + half_tile
                        u = found[:, half_tile * LANES : (half_tile + 1) * LANES]
                        u = u.astype(BF).astype(F32)
                        side = lax.rem((2 * j) // group, 2)
                        lo = jnp.where(low, u, 0.0)
                        hi = jnp.where(low, 0.0, u)
                        grad_pad[2 * j] = jnp.where(side == 0, lo, pltpu.roll(lo, HEAD_WIDTH, 1)).astype(BF)
                        grad_pad[2 * j + 1] = jnp.where(side == 1, hi, pltpu.roll(hi, HEAD_WIDTH, 1)).astype(BF)

            pl.run_scoped(with_out, pltpu.VMEM((query_cols, width), BF))

            def attend_back(first_head, last_head):
                @pl.loop(first_head, last_head)
                def _(h):
                    pair = h // (2 * group)
                    keys = kv_all[:, pair].reshape(seq_len, LANES)
                    values = kv_all[:, n_kv + pair].reshape(seq_len, LANES)
                    scores = dot_t(keys, q_pad[h])
                    scores = jnp.where(pos_q[0:1, :] >= pos_k[...], scores, NEG)
                    weights = jnp.exp(scores - log_sum[pl.ds(h, 1), :])
                    weight_grad = dot_t(values, grad_pad[h])
                    inner = jnp.sum(weights * weight_grad, 0, keepdims=True)
                    score_grad = (weights * (weight_grad - inner)).astype(BF)
                    value_sum[pair] += jnp.dot(weights.astype(BF), grad_pad[h], preferred_element_type=F32)
                    key_sum[pair] += jnp.dot(score_grad, q_pad[h], preferred_element_type=F32)
                    query_out[h] = t_dot(keys, score_grad).T

            attend_back(0, heads // 2)
            to_planes(GATE, gate)
            from_planes(DOWN)
            down_share.start()
            attend_back(heads // 2, heads)
            for i in range(n_kv):
                kv_grad[:, i] = key_sum[i].astype(BF).reshape(contexts, rows, LANES)
                kv_grad[:, n_kv + i] = value_sum[i].astype(BF).reshape(contexts, rows, LANES)

            def kv_core(other):
                return copy_to(
                    kv_grad.at[other * 2 + 1 - k], kv_core_in.at[other], k_send.at[KV, other], k_recv.at[KV, other],
                    ring.at_k,
                )

            def kv_outer(by):
                return copy_to(
                    kv_out.at[by - 1], kv_outer_in.at[by - 1], y_send.at[KV, by], y_recv.at[KV, by],
                    ring.at_o(ring.after(by)),
                )

            for other in range(outers):
                kv_core(other).start()
            for j in range(n_q):
                side = (2 * j) // group % 2
                lo, hi = query_out[2 * j], query_out[2 * j + 1]
                if side == 0:
                    hi = pltpu.roll(hi, HEAD_WIDTH, 1)
                else:
                    lo = pltpu.roll(lo, HEAD_WIDTH, 1)
                u = jnp.where(low, lo, hi) * FACTOR
                qkv_grad[:, j * LANES : (j + 1) * LANES] = rotate_tile(u, cosine[...], -sine[...], first).astype(BF)
            to_planes(UP, up)
            for other in range(outers):
                kv_core(other).wait_recv()
            for by in range(1, outers):
                goal = ring.after(by)
                kv_out[by - 1] = (
                    kv_grad[goal * 2 + k].astype(F32) + kv_core_in[goal].astype(F32)
                ).astype(BF)
                kv_outer(by).start()
            kv_sum = kv_grad[c].astype(F32) + kv_core_in[o].astype(F32)
            for by in range(1, outers):
                kv_outer(by).wait_recv()
                kv_sum = kv_sum + kv_outer_in[by - 1].astype(F32)
            for i in range(n_kv):
                at = query_cols + i * LANES
                qkv_grad[:, at : at + LANES] = rotate_tile(kv_sum[i], cosine[...], -sine[...], first).astype(BF)
                qkv_grad[:, at + kv_cols : at + kv_cols + LANES] = kv_sum[n_kv + i].astype(BF)
            for other in range(outers):
                kv_core(other).wait_send()
            for by in range(1, outers):
                kv_outer(by).wait_send()

            first_swap = x_copy(FIRST, first_x_out, first_x_in)

            def with_qkv(qkv_w, own):
                one = pltpu.make_async_copy(qkv_hbm, qkv_w, load_sem.at[0])
                one.start()
                one.wait()

                def tile_of(at):
                    return dot_t(qkv_grad[...], qkv_w[pl.ds(pl.multiple_of(at, WIDE), WIDE), :])

                @pl.loop(0, n_half)
                def _(j):
                    here = pl.ds(pl.multiple_of(j * WIDE, WIDE), WIDE)
                    first_x_out[:, here] = tile_of(other_cols + j * WIDE).astype(BF)

                first_swap.start()

                @pl.loop(0, n_half)
                def _(j):
                    here = pl.ds(pl.multiple_of(j * WIDE, WIDE), WIDE)
                    own[:, here] = tile_of(own_cols + j * WIDE)

                from_planes(GATE)
                gate_share.start()
                first_swap.wait()
                scale_one = scales[0][:, 0:1]
                gain_one = gains[0:1, pl.ds(own_cols, half)].astype(F32)
                back = norm_back(
                    own[...] + first_x_in[...].astype(F32), tok[...].astype(F32) * scale_one, scale_one, gain_one, 0, 1
                )
                input_grad[...] = (mid_grad[...] + back).astype(BF)

            pl.run_scoped(with_qkv, pltpu.VMEM((width, qkv_cols), BF), pltpu.VMEM((rows, half), F32))
            mid_swap.wait_send()

        tile_f32 = pltpu.VMEM((rows, half), F32)
        pl.run_scoped(
            attention,
            tile_f32,
            pltpu.VMEM((heads, rows, LANES), BF),
            pltpu.VMEM((contexts, 2 * n_kv, rows, LANES), BF),
            pltpu.VMEM((rows, half), BF),
            pltpu.VMEM((heads, rows, LANES), BF),
            pltpu.VMEM((heads, rows, LANES), F32),
            pltpu.VMEM((n_kv, seq_len, LANES), F32),
            pltpu.VMEM((n_kv, seq_len, LANES), F32),
            pltpu.VMEM((contexts, 2 * n_kv, rows, LANES), BF),
            pltpu.VMEM((lots, 2 * n_kv, rows, LANES), BF),
        )

        down_share.pass_on()
        gate_share.pass_on()
        from_planes(UP)
        down_share.finish()
        gate_share.finish()
        for item in (DOWN, GATE, UP):
            for s in range(1, planes):
                strip_copy(item, s).wait_send()
        for reduction in (down, gate, up):
            reduction.outer_done()
        for i in range(max(planes - 2, 0), planes):
            norm_x(i).wait_send()
        for p in order:
            norm_z(p).wait_send()

    hbm = pl.BlockSpec(memory_space=pl.ANY)
    vmem = pl.BlockSpec(memory_space=pltpu.VMEM)
    dma = pltpu.SemaphoreType.DMA
    shape = jax.ShapeDtypeStruct
    acts = pltpu.VMEM((planes, rows, half), BF)
    arrivals = pltpu.VMEM((planes - 1, rows, half), BF)
    return pl.pallas_call(
        kernel,
        name="back",
        out_shape=(
            shape((rows, half), BF),
            shape((depth, planes * units), BF),
            shape((strip, planes * units), BF),
            shape((planes, contexts, unit_strip, depth), BF),
            shape((rows, width), BF),
            shape((rows, qkv_cols), BF),
            shape((8, half), F32),
            shape((planes, rows, width), BF),
        ),
        in_specs=[hbm] * 11 + [vmem] * 7,
        out_specs=(vmem, hbm, hbm, hbm, vmem, vmem, vmem, hbm),
        scratch_shapes=[acts, arrivals, pltpu.VMEM((2, rows, half), BF), acts, pltpu.VMEM((2, rows, width), BF)]
        + [
            pltpu.VMEM((outers, planes, strip, units), BF),
            pltpu.VMEM((outers, 1, unit_strip, width), BF),
            pltpu.VMEM((2, lots, planes, strip, units), BF),
            pltpu.VMEM((lots, 1, unit_strip, width), BF),
            pltpu.VMEM((2, lots, planes, strip, units), BF),
            pltpu.VMEM((lots, 1, unit_strip, width), BF),
            pltpu.VMEM((2, planes, strip, units), BF),
            pltpu.VMEM((1, unit_strip, width), BF),
            pltpu.VMEM((outers, 2 * n_kv, rows, LANES), BF),
            pltpu.VMEM((lots, 2 * n_kv, rows, LANES), BF),
            pltpu.VMEM((2, rows, LANES), F32),
            pltpu.VMEM((2, rows, LANES), F32),
            pltpu.VMEM((rows, half), BF),
            pltpu.VMEM((rows, half), BF),
            dma((planes + 4,)),
            dma((planes + 4,)),
            dma((1, planes)),
            dma((1, planes)),
            dma((4, outers)),
            dma((4, outers)),
            dma((4, max(outers, 2))),
            dma((4, max(outers, 2))),
            dma((3, planes)),
            dma((3, planes)),
            dma((2, max(outers, 2))),
            dma((2, max(outers, 2))),
            dma((2, outers)),
            dma((2, outers)),
            dma((2 * planes + 3,)),
            dma((2,)),
            pltpu.SemaphoreType.REGULAR,
        ],
        compiler_params=pltpu.CompilerParams(
            collective_id=1, has_side_effects=True, vmem_limit_bytes=VMEM_LIMIT
        ),
        cost_estimate=pl.CostEstimate(flops=50 * 10**9, bytes_accessed=80 * 10**6, transcendentals=8 * 10**6),
    )


def build_grads(planes, contexts, rows, width, query_cols, kv_cols, units):
    outers = contexts // 2
    half = width // 2
    depth = width // planes
    strip = depth // contexts
    out_strip = query_cols // contexts
    unit_strip = units // contexts
    qkv_cols = query_cols + 2 * kv_cols
    lots = max(outers - 1, 1)
    per_half = planes // 2
    OUT, QKV, UP = range(3)

    def kernel(
        attn, mid_full, normed_one, qkv_grad, gain_rows, mid_own, up_strip, mlp_part,
        up_out, out_out, qkv_out, gain_out, result,
        out_part, qkv_part, out_core, qkv_core, out_outer_out, qkv_outer_out, out_outer_in, qkv_outer_in,
        out_sum, qkv_sum, out_z, qkv_z, gain_z, gain_y, gain_k, gain_now, mlp_x_in, mlp_z_in, mlp_sum,
        k_send, k_recv, y_send, y_recv, z_send, z_recv, sk_send, sk_recv, sy_send, sy_recv, gain_send, gain_recv,
        mx_send, mx_recv, mz_send, mz_recv, own_sem,
    ):
        ring = Ring(planes, contexts)
        z, c, t, k, o = ring.z, ring.c, ring.t, ring.k, ring.o
        order = ring.by_distance()
        ring.greet()

        def rows_of(whole, size):
            return lambda q: whole.at[pl.ds(pl.multiple_of(q * size, size), size), :]

        share_sems = (sy_send, sy_recv, sk_send, sk_recv)
        up_share = Share(ring, UP, rows_of(up_out, strip), share_sems, up_strip)
        out_share = Share(ring, OUT, rows_of(out_out, out_strip), share_sems)
        qkv_share = Share(ring, QKV, rows_of(qkv_out, strip), share_sems)
        keep = pltpu.make_async_copy(up_strip, rows_of(up_out, strip)(c), own_sem.at[0])
        keep.start()

        own_cols = pl.multiple_of(t * half, half)
        other_cols = pl.multiple_of((1 - t) * half, half)
        blocks = order[::-1] + [z]

        def mlp_x(p):
            return copy_to(
                mlp_part.at[p, :, pl.ds(other_cols, half)], mlp_x_in.at[p], mx_send.at[p], mx_recv.at[p], ring.at_x
            )

        def mlp_z(p):
            return copy_to(
                mlp_sum.at[p], mlp_z_in.at[lax.rem(z - p + planes, planes) - 1], mz_send.at[p], mz_recv.at[z],
                ring.at_z(p),
            )

        mlp_load = pltpu.make_async_copy(mlp_part.at[:, :, pl.ds(own_cols, half)], mlp_sum, own_sem.at[1])
        for p in blocks:
            mlp_x(p).start()
        mlp_load.start()

        def mlp_on(p):
            mlp_x(p).wait_recv()

            @pl.loop(0, rows // 64)
            def _(i):
                r = pl.ds(pl.multiple_of(i * 64, 64), 64)
                mlp_sum[p, r, :] = (mlp_sum[p, r, :].astype(F32) + mlp_x_in[p, r, :].astype(F32)).astype(BF)

        takes_part = z // per_half == t

        def gain_plane(j):
            return t * per_half + j

        def gain_copy(j):
            return copy_to(
                gain_rows.at[:, pl.ds(j * depth, depth)], gain_z.at[z], gain_send.at[j], gain_recv.at[z],
                ring.at_z(gain_plane(j)),
            )

        for j in range(per_half):

            @pl.when(gain_plane(j) != z)
            def _(j=j):
                gain_copy(j).start()

        gain_x = copy_to(
            gain_out, gain_out, gain_send.at[per_half], gain_recv.at[planes], ring.at_x
        )

        def gain_outer(by):
            return copy_to(
                gain_now.at[0], gain_y.at[by - 1], gain_send.at[per_half + by], gain_recv.at[planes + by],
                ring.at_o(ring.after(by)),
            )

        gain_core = copy_to(
            gain_now.at[1], gain_k, gain_send.at[per_half + outers], gain_recv.at[planes + outers], ring.at_k
        )

        def product(part, left, right):
            @pl.loop(0, left.shape[1] // TILE)
            def _(i):
                cols = pl.ds(pl.multiple_of(i * TILE, TILE), TILE)
                store_part(part, i, t_dot(left[:, cols], right[...]))

        sems = (k_send, k_recv, y_send, y_recv)
        out = Reduction(ring, 0, out_part, out_core, out_outer_out, out_outer_in, out_sum, sems)
        qkv = Reduction(ring, 1, qkv_part, qkv_core, qkv_outer_out, qkv_outer_in, qkv_sum, sems)
        product(qkv_part, normed_one, qkv_grad)
        qkv.to_core()
        product(out_part, attn, mid_full)
        qkv.from_core()
        out.to_core()

        @pl.when(takes_part)
        def _():
            mine = lax.rem(z, per_half) * depth
            total = gain_rows[:, pl.ds(pl.multiple_of(mine, depth), depth)]
            for s in range(1, planes):
                p = ring.plane(s)
                copy_to(gain_z.at[p], gain_z.at[p], gain_send.at[0], gain_recv.at[p], ring.at_k).wait_recv()
                total = total + gain_z[p]
            gain_now[0] = total
            for by in range(1, outers):
                gain_outer(by).start()

        out.from_core()
        mlp_load.wait()
        for p in blocks[:-1]:
            mlp_on(p)
            mlp_z(p).start()

        @pl.when(takes_part)
        def _():
            total = gain_now[0]
            for by in range(1, outers):
                gain_outer(by).wait()
                total = total + gain_y[by - 1]
            gain_now[1] = total
            gain_core.start()

        def piece(item, p):
            if item == OUT:
                return out_sum.at[0, :, pl.ds(pl.multiple_of(p * depth, depth), depth)]
            return qkv_sum.at[p]

        def landing(item, p):
            return (out_z if item == OUT else qkv_z).at[p]

        def z_copy(item, s):
            p = ring.plane(s)
            return copy_to(
                piece(item, p), landing(item, z), z_send.at[item, s], z_recv.at[item, z], ring.at_z(p)
            )

        def to_planes(item, reduction):
            reduction.from_outer()
            for s in range(1, planes):
                z_copy(item, s).start()

        def from_planes(item):
            for p in order:
                there = landing(item, p)
                copy_to(there, there, z_send.at[item, 0], z_recv.at[item, p], ring.at_k).wait_recv()
            size = out_strip if item == OUT else strip
            whole = out_out if item == OUT else qkv_out
            total = piece(item, z)[...].astype(F32)
            for p in order:
                total = total + landing(item, p)[...].astype(F32)
            whole[pl.ds(pl.multiple_of(c * size, size), size), :] = total.astype(BF)
            (out_share if item == OUT else qkv_share).start()

        to_planes(QKV, qkv)

        @pl.when(takes_part)
        def _():
            gain_core.wait()
            gain_out[...] = gain_now[1] + gain_k[...]
            gain_x.start()

        to_planes(OUT, out)
        up_share.start()
        from_planes(QKV)
        mlp_on(z)
        from_planes(OUT)
        total = mid_own[...] + mlp_sum[z].astype(F32)
        for p in order:
            there = mlp_z_in.at[lax.rem(p - z + planes, planes) - 1]
            copy_to(there, there, mz_send.at[p], mz_recv.at[p], ring.at_k).wait_recv()
            total = total + there[...].astype(F32)
        result[...] = total.astype(BF)
        for one in (up_share, out_share, qkv_share):
            one.pass_on()
        keep.wait()
        for one in (up_share, out_share, qkv_share):
            one.finish()
        for p in blocks:
            mlp_x(p).wait_send()
        for p in order:
            mlp_z(p).wait_send()
        for reduction in (out, qkv):
            reduction.core_done()
            reduction.outer_done()
        for item in (OUT, QKV):
            for s in range(1, planes):
                z_copy(item, s).wait_send()
        for j in range(per_half):

            @pl.when(gain_plane(j) != z)
            def _(j=j):
                gain_copy(j).wait_send()

        @pl.when(takes_part)
        def _():
            gain_x.wait_send()

        @pl.when(jnp.logical_not(takes_part))
        def _():
            gain_x.wait_recv()

    hbm = pl.BlockSpec(memory_space=pl.ANY)
    vmem = pl.BlockSpec(memory_space=pltpu.VMEM)
    dma = pltpu.SemaphoreType.DMA
    shape = jax.ShapeDtypeStruct
    return pl.pallas_call(
        kernel,
        name="grads",
        out_shape=(
            shape((depth, planes * units), BF),
            shape((query_cols, depth), BF),
            shape((depth, qkv_cols), BF),
            shape((8, depth), F32),
            shape((rows, half), BF),
        ),
        in_specs=[vmem] * 6 + [hbm] * 2,
        out_specs=(hbm, vmem, vmem, vmem, vmem),
        scratch_shapes=[
            pltpu.VMEM((1, contexts, out_strip, width), BF),
            pltpu.VMEM((planes, contexts, strip, qkv_cols), BF),
            pltpu.VMEM((outers, 1, out_strip, width), BF),
            pltpu.VMEM((outers, planes, strip, qkv_cols), BF),
            pltpu.VMEM((lots, 1, out_strip, width), BF),
            pltpu.VMEM((lots, planes, strip, qkv_cols), BF),
            pltpu.VMEM((lots, 1, out_strip, width), BF),
            pltpu.VMEM((lots, planes, strip, qkv_cols), BF),
            pltpu.VMEM((1, out_strip, width), BF),
            pltpu.VMEM((planes, strip, qkv_cols), BF),
            pltpu.VMEM((planes, out_strip, depth), BF),
            pltpu.VMEM((planes, strip, qkv_cols), BF),
            pltpu.VMEM((planes, 8, depth), F32),
            pltpu.VMEM((lots, 8, depth), F32),
            pltpu.VMEM((8, depth), F32),
            pltpu.VMEM((2, 8, depth), F32),
            pltpu.VMEM((planes, rows, half), BF),
            pltpu.VMEM((planes - 1, rows, half), BF),
            pltpu.VMEM((planes, rows, half), BF),
            dma((2, outers)),
            dma((2, outers)),
            dma((2, max(outers, 2))),
            dma((2, max(outers, 2))),
            dma((2, planes)),
            dma((2, planes)),
            dma((3, outers)),
            dma((3, outers)),
            dma((3, max(outers, 2))),
            dma((3, max(outers, 2))),
            dma((per_half + outers + 1,)),
            dma((planes + outers + 1,)),
            dma((planes,)),
            dma((planes,)),
            dma((planes,)),
            dma((planes,)),
            dma((2,)),
        ],
        compiler_params=pltpu.CompilerParams(
            collective_id=2, has_side_effects=True, vmem_limit_bytes=VMEM_LIMIT
        ),
        cost_estimate=pl.CostEstimate(flops=4 * 10**9, bytes_accessed=40 * 10**6, transcendentals=0),
    )


def shards(
    tokens,
    span_order,
    attn_gain,
    w_query,
    key_weight,
    value_weight,
    w_out,
    mlp_gain,
    w_gate,
    w_up,
    w_down,
    out_grad,
):
    planes = lax.axis_size("fsdp")
    contexts = lax.axis_size("context")
    tok_own, cot_own = tokens[0], out_grad[0]
    rows, own_cols = tok_own.shape
    width = own_cols * 2
    depth = width // planes
    units = w_gate.shape[1] // planes
    query_cols = w_query.shape[1]
    kv_cols = key_weight.shape[1]
    sizes = (planes, contexts, rows, width, query_cols, kv_cols, units)

    freqs = jnp.tile(rope_freqs(HEAD_WIDTH), LANES // (HEAD_WIDTH // 2))[None]
    (
        gate_w, up_w, down_w, cot_all, norm_all, qkv_w, out_w, gains, q_pad, kv_all, attn, log_sum, mid_own,
        normed_one, tok_all, scales, cosine_table, sine_table, pos_q, pos_k,
    ) = build_front(*sizes)(
        tok_own, cot_own, attn_gain[None], mlp_gain[None], w_query, key_weight, value_weight, w_out, w_gate, w_up,
        w_down, span_order, freqs,
    )
    input_grad, gate_out, up_strip, down_out, mid_full, qkv_grad, gain_rows, mlp_part = build_back(*sizes)(
        gate_w, up_w, down_w, norm_all, cot_all, qkv_w, out_w, q_pad, kv_all, mid_own, tok_all, gains,
        cosine_table, sine_table, pos_q, pos_k, log_sum, scales,
    )
    up_out, out_out, qkv_out, gain_out, result = build_grads(*sizes)(
        attn, mid_full, normed_one, qkv_grad, gain_rows, mid_own, up_strip, mlp_part
    )
    qkv_out = qkv_out.astype(F32)
    return (
        result[None],
        input_grad[None],
        gain_out[0],
        qkv_out[:, :query_cols],
        qkv_out[:, query_cols : query_cols + kv_cols],
        qkv_out[:, query_cols + kv_cols :],
        out_out.astype(F32),
        gain_out[1],
        gate_out.astype(F32),
        up_out.astype(F32),
        down_out.reshape(planes * units, depth).astype(F32),
    )


def solution(mesh):
    weight = P("fsdp", "tensor")
    turned = P("tensor", "fsdp")
    block = P("fsdp", "context", "tensor")
    gain = P("fsdp")
    return jax.shard_map(
        shards,
        mesh=mesh,
        in_specs=(
            block, P(), gain, weight, weight, weight, turned, gain, weight, weight, turned, block,
        ),
        out_specs=(
            block, block, gain, weight, weight, weight, turned, gain, weight, weight, turned,
        ),
        check_vma=False,
    )
```

```python
import math

import jax
import jax.numpy as jnp
from jax import lax
from jax.experimental import pallas as pl
from jax.experimental.pallas import tpu as pltpu
from jax.sharding import PartitionSpec as P

HEAD_WIDTH = 64
EPS = 1e-05
NEG = -1e30
BF = jnp.bfloat16
F32 = jnp.float32
LANES = 128
TILE = 256
WIDE = 512
FACTOR = 1.0 / math.sqrt(HEAD_WIDTH)
VMEM_LIMIT = 62 * 2**20
MESH = pl.DeviceIdType.MESH


def rope_freqs(head_size):
    half_size = head_size // 2
    index = jnp.arange(half_size, dtype=jnp.float32)
    base_freq = jnp.exp(-(2.0 * index / head_size) * math.log(500000.0))
    wavelen = 2.0 * math.pi / base_freq
    smooth = (8192.0 / wavelen - 1.0) / 3.0
    blended = (1.0 - smooth) * base_freq / 32.0 + smooth * base_freq
    return jnp.where(
        wavelen > 8192.0, base_freq / 32.0, jnp.where(wavelen < 2048.0, base_freq, blended)
    )


def dot_t(left, right):
    return lax.dot_general(left, right, (((1,), (1,)), ((), ())), preferred_element_type=F32)


def t_dot(left, right):
    return lax.dot_general(left, right, (((0,), (0,)), ((), ())), preferred_element_type=F32)


def build_front(planes, contexts, rows, width, query_cols, kv_cols, units):
    outers = contexts // 2
    half = width // 2
    depth = width // planes
    strip = depth // contexts
    out_strip = query_cols // contexts
    unit_strip = units // contexts
    seq_len = rows * contexts
    n_q, n_kv = query_cols // LANES, kv_cols // LANES
    heads = query_cols // HEAD_WIDTH
    group = query_cols // kv_cols
    qkv_cols = query_cols + 2 * kv_cols
    QKV, OUT, GATE, UP, DOWN, COT, NORM, GAIN = range(8)

    def kernel(
        tok, cot, gain_one_own, gain_two_own, query_own, key_own, value_own, out_own, gate_own, up_own, down_own,
        spans, freqs,
        gate_w, up_w, down_w, cot_all, norm_all, qkv_hbm, out_hbm, gains, q_pad, kv_all, attn, log_sum,
        mid_own, normed_one, tok_all, scales, cosine, sine, pos_q, pos_k,
        qkv_w, out_w, gains_own, lin, heads_out, send_half, recv_half, norm_own, sq_send, sq_recv,
        z_send, z_recv, y_send, y_recv, k_send, k_recv, x_send, x_recv, own_sem,
    ):
        z = lax.axis_index("fsdp")
        c = lax.axis_index("context")
        t = lax.axis_index("tensor")
        o, k = c // 2, c % 2

        def at_z(p):
            return (p, c, t)

        def at_o(other):
            return (z, other * 2 + k, t)

        at_k = (z, o * 2 + 1 - k, t)
        at_x = (z, c, 1 - t)

        def copy(src, dst, send_sem, recv_sem, device):
            return pltpu.make_async_remote_copy(
                src_ref=src, dst_ref=dst, send_sem=send_sem, recv_sem=recv_sem,
                device_id=device, device_id_type=MESH,
            )

        barrier = pltpu.get_barrier_semaphore()
        peers = [at_z(lax.rem(z + s, planes)) for s in range(1, planes)]
        peers += [at_o(lax.rem(o + s, outers)) for s in range(1, outers)] + [at_k, at_x]
        for peer in peers:
            pl.semaphore_signal(barrier, inc=1, device_id=peer, device_id_type=MESH)
        pl.semaphore_wait(barrier, len(peers))

        order = []
        for i in range(planes - 1):
            p = jnp.int32(0)
            for plane in range(planes):
                far = sorted((abs(q - plane), q) for q in range(planes) if q != plane)
                p = p + jnp.where(z == plane, far[i][1], 0)
            order.append(p)

        def slot(item, p, q):
            if item == QKV:
                return qkv_w.at[pl.ds(p * depth + q * strip, strip), :]
            if item == OUT:
                return out_w.at[pl.ds(q * out_strip, out_strip), pl.ds(p * depth, depth)]
            if item == GATE:
                return gate_w.at[pl.ds(p * depth + q * strip, strip), :]
            if item == UP:
                return up_w.at[pl.ds(p * depth + q * strip, strip), :]
            if item == DOWN:
                return down_w.at[pl.ds(q * unit_strip, unit_strip), pl.ds(p * depth, depth)]
            if item == COT:
                return cot_all.at[p, :, pl.ds(t * half, half)]
            return norm_all.at[p, :, pl.ds(t * half, half)]

        def z_copy(item, p, src, goal, way):
            return copy(src, slot(item, p, c), z_send.at[item, p, way], z_recv.at[item, p], at_z(goal))

        def z_wait(item, p):
            z_copy(item, p, slot(item, p, c), z, 0).wait_recv()

        def spread(item, src):
            @pl.when(z + 1 < planes)
            def _():
                z_copy(item, z, src, z + 1, 0).start()

            @pl.when(z > 0)
            def _():
                z_copy(item, z, src, z - 1, 1).start()

        def spread_done(item, src):
            @pl.when(z + 1 < planes)
            def _():
                z_copy(item, z, src, z + 1, 0).wait_send()

            @pl.when(z > 0)
            def _():
                z_copy(item, z, src, z - 1, 1).wait_send()

        def passes_on(p):
            return ((p < z) & (z + 1 < planes)) | ((p > z) & (z > 0))

        def onward(p):
            return jnp.where(p < z, z + 1, z - 1)

        def forward(item, p):
            @pl.when(passes_on(p))
            def _():
                z_copy(item, p, slot(item, p, c), onward(p), 0).start()

        def forward_done(item, p):
            @pl.when(passes_on(p))
            def _():
                z_copy(item, p, slot(item, p, c), onward(p), 0).wait_send()

        def y_copy(item, p, by):
            here = slot(item, p, c)
            return copy(here, here, y_send.at[item, p, by], y_recv.at[item, p, by], at_o(lax.rem(o + by, outers)))

        def y_wait(item, p, by):
            there = slot(item, p, lax.rem(o - by + outers, outers) * 2 + k)
            copy(there, there, y_send.at[item, p, by], y_recv.at[item, p, by], at_k).wait_recv()

        def k_copy(item, p, by):
            here = slot(item, p, lax.rem(o - by + outers, outers) * 2 + k)
            return copy(here, here, k_send.at[item, p, by], k_recv.at[item, p, by], at_k)

        def k_wait(item, p, by):
            there = slot(item, p, lax.rem(o - by + outers, outers) * 2 + 1 - k)
            copy(there, there, k_send.at[item, p, by], k_recv.at[item, p, by], at_k).wait_recv()

        def share(item, p):
            for by in range(1, outers):
                y_copy(item, p, by).start()
            k_copy(item, p, 0).start()

        def share_on(item, p):
            for by in range(1, outers):
                y_wait(item, p, by)
                k_copy(item, p, by).start()

        def shared(item, p):
            for by in range(outers):
                k_wait(item, p, by)

        def share_done(item, p):
            for by in range(1, outers):
                y_copy(item, p, by).wait_send()
            for by in range(outers):
                k_copy(item, p, by).wait_send()

        def x_copy(i, src, dst):
            return copy(src, dst, x_send.at[i], x_recv.at[i], at_x)

        gains_own[...] = jnp.zeros_like(gains_own)
        gains_own[0:1, :] = gain_one_own[...].astype(F32)
        gains_own[1:2, :] = gain_two_own[...].astype(F32)
        tok_cols = pl.ds(t * half, half)
        tok_copy = x_copy(0, tok, tok_all.at[:, tok_cols])
        tok_copy.start()
        gain_copies = [
            copy(
                gains_own, gains.at[:, pl.ds(z * depth, depth)], z_send.at[GAIN, lax.rem(z + s, planes), 0],
                z_recv.at[GAIN, z], at_z(lax.rem(z + s, planes)),
            )
            for s in range(1, planes)
        ]
        for one in gain_copies:
            one.start()
        home = pl.ds(z * depth, depth)
        own_qkv = [
            pltpu.make_async_copy(query_own, qkv_w.at[home, pl.ds(0, query_cols)], own_sem.at[0]),
            pltpu.make_async_copy(key_own, qkv_w.at[home, pl.ds(query_cols, kv_cols)], own_sem.at[7]),
            pltpu.make_async_copy(value_own, qkv_w.at[home, pl.ds(query_cols + kv_cols, kv_cols)], own_sem.at[8]),
        ]
        for one in own_qkv:
            one.start()
        for one in own_qkv:
            one.wait()
        qkv_src = slot(QKV, z, c)
        out_src = out_own.at[pl.ds(c * out_strip, out_strip), :]
        spread(QKV, qkv_src)
        own_copies = [
            pltpu.make_async_copy(out_own, out_w.at[:, pl.ds(z * depth, depth)], own_sem.at[1]),
            pltpu.make_async_copy(
                gate_own.at[:, pl.ds(z * units, units)], gate_w.at[pl.ds(z * depth, depth), :], own_sem.at[2]
            ),
            pltpu.make_async_copy(
                up_own.at[:, pl.ds(z * units, units)], up_w.at[pl.ds(z * depth, depth), :], own_sem.at[3]
            ),
            pltpu.make_async_copy(
                down_own.at[pl.ds(z * units, units), :], down_w.at[:, pl.ds(z * depth, depth)], own_sem.at[4]
            ),
            pltpu.make_async_copy(cot, slot(COT, z, c), own_sem.at[5]),
        ]
        for one in own_copies:
            one.start()
        gains[:, pl.ds(z * depth, depth)] = gains_own[...]
        tok_all[:, tok_cols] = tok[...]

        def positions(q, shape, axis):
            r = lax.broadcasted_iota(jnp.int32, shape, axis)
            return jnp.where(r < rows // 2, spans[q, 0], spans[q, 1]) * (rows // 2) + lax.rem(r, rows // 2)

        for q in range(contexts):
            pos_k[q * rows : (q + 1) * rows, :] = positions(q, (rows, 1), 0)
        pos_q[...] = positions(c, (8, rows), 1)
        angle = positions(c, (rows, LANES), 0).astype(F32) * freqs[...]
        cosine[...] = jnp.cos(angle)
        side_of = lax.rem(lax.broadcasted_iota(jnp.int32, (rows, LANES), 1), HEAD_WIDTH) < HEAD_WIDTH // 2
        sine[...] = jnp.where(side_of, -jnp.sin(angle), jnp.sin(angle))

        tok_copy.wait()
        for s in range(1, planes):
            p = lax.rem(z + s, planes)
            there = gains.at[:, pl.ds(p * depth, depth)]
            copy(there, there, z_send.at[GAIN, p, 0], z_recv.at[GAIN, p], at_k).wait_recv()
        x = tok_all[...].astype(F32)
        scale = lax.rsqrt(jnp.mean(x * x, -1, keepdims=True) + EPS)
        scales[0] = jnp.broadcast_to(scale, (rows, LANES))
        normed_one[...] = (x * scale * gains[0:1, :].astype(F32)).astype(BF)

        for p in order:
            z_wait(QKV, p)
            forward(QKV, p)
            share(QKV, p)

        spread(OUT, out_src)
        sends = []

        def send_units(item):
            for s in range(1, planes):
                goal = lax.rem(z + s, planes)
                if item == DOWN:
                    src = down_own.at[pl.ds(goal * units + c * unit_strip, unit_strip), :]
                else:
                    own = gate_own if item == GATE else up_own
                    src = own.at[pl.ds(c * strip, strip), pl.ds(goal * units, units)]
                one = z_copy(item, z, src, goal, s - 1)
                one.start()
                sends.append(one)

        def share_units(item):
            for s in range(1, planes):
                p = lax.rem(z + planes - s, planes)
                z_wait(item, p)
                share(item, p)

        def step(item, i):
            p = order[i]
            z_wait(item, p)
            forward(item, p)
            if item == OUT:
                share(OUT, p)
            else:
                base = 1 if item == COT else 3 + planes
                x_copy(base + p, slot(item, p, c), slot(item, p, c)).start()

        items = (GATE, UP, DOWN)
        last = planes - 1
        step(OUT, 0)
        spread(COT, cot)
        cot_copy = x_copy(1 + z, cot, slot(COT, z, c))
        cot_copy.start()
        for p in order:
            share_on(QKV, p)
        for p in order:
            shared(QKV, p)
        qkv_keep = pltpu.make_async_copy(qkv_w, qkv_hbm, own_sem.at[0])
        qkv_keep.start()

        n_tile = 2 * LANES

        @pl.loop(0, qkv_cols // n_tile)
        def _(i):
            cols = pl.ds(pl.multiple_of(i * n_tile, n_tile), n_tile)
            found = jnp.dot(normed_one[...], qkv_w[:, cols], preferred_element_type=F32)
            lin[2 * i] = found[:, :LANES]
            lin[2 * i + 1] = found[:, LANES:]

        lane = lax.broadcasted_iota(jnp.int32, (rows, LANES), 1)
        first = lax.rem(lane, HEAD_WIDTH) < HEAD_WIDTH // 2
        low = lane < HEAD_WIDTH

        def rotated(u):
            partner = jnp.where(
                first, pltpu.roll(u, LANES - HEAD_WIDTH // 2, 1), pltpu.roll(u, HEAD_WIDTH // 2, 1)
            )
            return u * cosine[...] + partner * sine[...]

        for i in range(n_kv):
            kv_all[c, i] = rotated(lin[n_q + i]).astype(BF)
            kv_all[c, n_kv + i] = lin[n_q + n_kv + i].astype(BF)

        def kv_slot(q):
            return kv_all.at[q]

        kv_sends = [
            copy(kv_slot(c), kv_slot(c), y_send.at[COT, 0, by], y_recv.at[COT, 0, by], at_o(lax.rem(o + by, outers)))
            for by in range(1, outers)
        ]
        kv_sends.append(copy(kv_slot(c), kv_slot(c), k_send.at[COT, 0, 0], k_recv.at[COT, 0, 0], at_k))
        for one in kv_sends:
            one.start()
        for i in range(1, last - 1):
            step(OUT, i)
        step(COT, 0)
        send_units(GATE)

        @pl.loop(0, n_q)
        def _(j):
            u = rotated(lin[j]).astype(BF).astype(F32) * FACTOR
            side = lax.rem((2 * j) // group, 2)
            lo = jnp.where(low, u, 0.0)
            hi = jnp.where(low, 0.0, u)
            q_pad[2 * j] = jnp.where(side == 0, lo, pltpu.roll(lo, HEAD_WIDTH, 1)).astype(BF)
            q_pad[2 * j + 1] = jnp.where(side == 1, hi, pltpu.roll(hi, HEAD_WIDTH, 1)).astype(BF)

        for by in range(1, outers):
            q = lax.rem(o - by + outers, outers) * 2 + k
            copy(kv_slot(q), kv_slot(q), y_send.at[COT, 0, by], y_recv.at[COT, 0, by], at_k).wait_recv()
            one = copy(kv_slot(q), kv_slot(q), k_send.at[COT, 0, by], k_recv.at[COT, 0, by], at_k)
            one.start()
            kv_sends.append(one)
        for by in range(outers):
            q = lax.rem(o - by + outers, outers) * 2 + 1 - k
            copy(kv_slot(q), kv_slot(q), k_send.at[COT, 0, by], k_recv.at[COT, 0, by], at_k).wait_recv()

        def attend(first_head, last_head):
            @pl.loop(first_head, last_head)
            def _(h):
                pair = h // (2 * group)
                keys = kv_all[:, pair].reshape(seq_len, LANES)
                values = kv_all[:, n_kv + pair].reshape(seq_len, LANES)
                scores = dot_t(keys, q_pad[h])
                scores = jnp.where(pos_q[0:1, :] >= pos_k[...], scores, NEG)
                top = jnp.max(scores, 0, keepdims=True)
                expo = jnp.exp(scores - top)
                total = jnp.sum(expo, 0, keepdims=True)
                weights = (expo * (1.0 / total)).astype(BF)
                heads_out[h] = t_dot(values, weights).T
                log_sum[pl.ds(h, 1), :] = top + jnp.log(total)

        attend(0, heads // 2)
        step(OUT, last - 1)
        for i in range(1, last - 1):
            step(COT, i)
        send_units(UP)
        for p in order:
            share_on(OUT, p)
        attend(heads // 2, heads)

        for j in range(n_q):
            side = (2 * j) // group % 2
            lo, hi = heads_out[2 * j], heads_out[2 * j + 1]
            if side == 0:
                hi = pltpu.roll(hi, HEAD_WIDTH, 1)
            else:
                lo = pltpu.roll(lo, HEAD_WIDTH, 1)
            attn[:, j * LANES : (j + 1) * LANES] = jnp.where(low, lo, hi).astype(BF)

        for p in order:
            shared(OUT, p)
        own_copies[0].wait()
        out_keep = pltpu.make_async_copy(out_w, out_hbm, own_sem.at[7])
        out_keep.start()

        n_out = half // n_tile

        @pl.loop(0, n_out)
        def _(i):
            cols = pl.ds(pl.multiple_of((1 - t) * half + i * n_tile, n_tile), n_tile)
            here = pl.ds(pl.multiple_of(i * n_tile, n_tile), n_tile)
            send_half[:, here] = jnp.dot(attn[...], out_w[:, cols], preferred_element_type=F32).astype(BF)

        half_copy = x_copy(1 + planes, send_half, recv_half)
        half_copy.start()

        @pl.loop(0, n_out)
        def _(i):
            cols = pl.ds(pl.multiple_of(t * half + i * n_tile, n_tile), n_tile)
            here = pl.ds(pl.multiple_of(i * n_tile, n_tile), n_tile)
            part = jnp.dot(attn[...], out_w[:, cols], preferred_element_type=F32)
            mid_own[:, here] = tok[:, here].astype(F32) + part

        half_copy.wait_recv()
        mid = mid_own[...] + recv_half[...].astype(F32)
        mid_own[...] = mid
        squares = jnp.sum(mid * mid, -1, keepdims=True)
        sq_send[...] = jnp.broadcast_to(squares, (rows, LANES))
        sq_copy = x_copy(2 + planes, sq_send, sq_recv)
        sq_copy.start()
        sq_copy.wait_recv()
        scale_two = lax.rsqrt((squares + sq_recv[:, 0:1]) * (1.0 / width) + EPS)
        scales[1] = jnp.broadcast_to(scale_two, (rows, LANES))
        gain_two = gains[1:2, pl.ds(pl.multiple_of(t * half, half), half)].astype(F32)
        norm_own[...] = (mid_own[...] * scale_two * gain_two).astype(BF)

        spread(NORM, norm_own)
        norm_copy = x_copy(3 + planes + z, norm_own, slot(NORM, z, c))
        norm_copy.start()
        norm_keep = pltpu.make_async_copy(norm_own, slot(NORM, z, c), own_sem.at[6])
        norm_keep.start()
        step(COT, last - 1)
        step(NORM, 0)
        send_units(DOWN)
        share_units(GATE)
        step(NORM, 1)
        share_units(UP)
        for i in range(2, last):
            step(NORM, i)
        for s in range(1, planes):
            share_on(GATE, lax.rem(z + planes - s, planes))
        share_units(DOWN)
        for s in range(1, planes):
            share_on(UP, lax.rem(z + planes - s, planes))
        for s in range(1, planes):
            share_on(DOWN, lax.rem(z + planes - s, planes))

        for s in range(1, planes):
            p = lax.rem(z + s, planes)
            for item in items:
                shared(item, p)
        for p in [z] + order:
            for base, item in ((1, COT), (3 + planes, NORM)):
                there = (cot_all if item == COT else norm_all).at[p, :, pl.ds((1 - t) * half, half)]
                copy(there, there, x_send.at[base + p], x_recv.at[base + p], at_x).wait_recv()
        for one in own_copies[1:] + [qkv_keep, out_keep]:
            one.wait()
        norm_keep.wait()
        tok_copy_out = [half_copy, sq_copy, cot_copy, norm_copy]
        for one in gain_copies + sends + kv_sends + tok_copy_out:
            one.wait_send()
        spread_done(QKV, qkv_src)
        spread_done(OUT, out_src)
        spread_done(COT, cot)
        spread_done(NORM, norm_own)
        for p in order:
            for item in (QKV, OUT, COT, NORM):
                forward_done(item, p)
            for item in (QKV, OUT, GATE, UP, DOWN):
                share_done(item, p)
            x_copy(1 + p, slot(COT, p, c), slot(COT, p, c)).wait_send()
            x_copy(3 + planes + p, slot(NORM, p, c), slot(NORM, p, c)).wait_send()

    hbm = pl.BlockSpec(memory_space=pl.ANY)
    vmem = pl.BlockSpec(memory_space=pltpu.VMEM)
    dma = pltpu.SemaphoreType.DMA
    shape = jax.ShapeDtypeStruct
    return pl.pallas_call(
        kernel,
        name="front",
        out_shape=(
            shape((width, units), BF),
            shape((width, units), BF),
            shape((units, width), BF),
            shape((planes, rows, width), BF),
            shape((planes, rows, width), BF),
            shape((width, qkv_cols), BF),
            shape((query_cols, width), BF),
            shape((8, width), F32),
            shape((heads, rows, LANES), BF),
            shape((contexts, 2 * n_kv, rows, LANES), BF),
            shape((rows, query_cols), BF),
            shape((heads, rows), F32),
            shape((rows, half), F32),
            shape((rows, width), BF),
            shape((rows, width), BF),
            shape((2, rows, LANES), F32),
            shape((rows, LANES), F32),
            shape((rows, LANES), F32),
            shape((8, rows), jnp.int32),
            shape((seq_len, 1), jnp.int32),
        ),
        in_specs=[vmem, hbm, vmem, vmem] + [hbm] * 7 + [pl.BlockSpec(memory_space=pltpu.SMEM), vmem],
        out_specs=(hbm,) * 7 + (vmem,) * 13,
        scratch_shapes=[
            pltpu.VMEM((width, qkv_cols), BF),
            pltpu.VMEM((query_cols, width), BF),
            pltpu.VMEM((8, depth), F32),
            pltpu.VMEM((qkv_cols // LANES, rows, LANES), F32),
            pltpu.VMEM((heads, rows, LANES), F32),
            pltpu.VMEM((rows, half), BF),
            pltpu.VMEM((rows, half), BF),
            pltpu.VMEM((rows, half), BF),
            pltpu.VMEM((rows, LANES), F32),
            pltpu.VMEM((rows, LANES), F32),
            dma((8, planes, planes)),
            dma((8, planes)),
            dma((6, planes, max(outers, 2))),
            dma((6, planes, max(outers, 2))),
            dma((6, planes, max(outers, 2))),
            dma((6, planes, max(outers, 2))),
            dma((3 + 2 * planes,)),
            dma((3 + 2 * planes,)),
            dma((9,)),
        ],
        compiler_params=pltpu.CompilerParams(
            collective_id=0, has_side_effects=True, vmem_limit_bytes=VMEM_LIMIT
        ),
        cost_estimate=pl.CostEstimate(flops=8 * 10**9, bytes_accessed=80 * 10**6, transcendentals=4 * 10**6),
    )


def add_strips(total, terms, chunk):
    lead, size, _ = total.shape
    steps = size // chunk

    @pl.loop(0, lead * steps)
    def _(i):
        a, r = i // steps, pl.ds(pl.multiple_of(lax.rem(i, steps) * chunk, chunk), chunk)
        found = terms[0][a, r, :].astype(F32)
        for term in terms[1:]:
            found = found + term[a, r, :].astype(F32)
        total[a, r, :] = found.astype(BF)


class Ring:
    def __init__(self, planes, contexts):
        self.planes, self.outers = planes, contexts // 2
        self.z = z = lax.axis_index("fsdp")
        self.c = c = lax.axis_index("context")
        self.t = t = lax.axis_index("tensor")
        self.o, self.k = c // 2, c % 2
        self.at_k = (z, self.o * 2 + 1 - self.k, t)
        self.at_x = (z, c, 1 - t)

    def at_z(self, p):
        return (p, self.c, self.t)

    def at_o(self, other):
        return (self.z, other * 2 + self.k, self.t)

    def after(self, by):
        return lax.rem(self.o + by, self.outers)

    def before(self, by):
        return lax.rem(self.o - by + self.outers, self.outers)

    def plane(self, by):
        return lax.rem(self.z + by, self.planes)

    def greet(self):
        barrier = pltpu.get_barrier_semaphore()
        peers = [self.at_z(self.plane(s)) for s in range(1, self.planes)]
        peers += [self.at_o(self.after(s)) for s in range(1, self.outers)] + [self.at_k, self.at_x]
        for peer in peers:
            pl.semaphore_signal(barrier, inc=1, device_id=peer, device_id_type=MESH)
        pl.semaphore_wait(barrier, len(peers))

    def by_distance(self):
        order = []
        for i in range(self.planes - 1):
            p = jnp.int32(0)
            for plane in range(self.planes):
                far = sorted((abs(q - plane), q) for q in range(self.planes) if q != plane)
                p = p + jnp.where(self.z == plane, far[i][1], 0)
            order.append(p)
        return order


def copy_to(src, dst, send_sem, recv_sem, device):
    return pltpu.make_async_remote_copy(
        src_ref=src, dst_ref=dst, send_sem=send_sem, recv_sem=recv_sem, device_id=device, device_id_type=MESH
    )


class Reduction:
    def __init__(self, ring, item, part, core_in, outer_out, outer_in, strip_sum, sems):
        self.ring, self.item, self.part = ring, item, part
        self.core_in, self.outer_out, self.outer_in, self.strip_sum = core_in, outer_out, outer_in, strip_sum
        self.k_send, self.k_recv, self.y_send, self.y_recv = sems
        self.chunk = 32 if strip_sum.shape[2] > 1024 else 64
        self.chunk = min(self.chunk, strip_sum.shape[1])

    def core_copy(self, other):
        g = self.ring
        return copy_to(
            self.part.at[:, other * 2 + 1 - g.k], self.core_in.at[other],
            self.k_send.at[self.item, other], self.k_recv.at[self.item, other], g.at_k,
        )

    def to_core(self):
        for other in range(self.ring.outers):
            self.core_copy(other).start()

    def outer_copy(self, by):
        g = self.ring
        return copy_to(
            self.outer_out.at[by - 1], self.outer_in.at[by - 1],
            self.y_send.at[self.item, by], self.y_recv.at[self.item, by], g.at_o(g.after(by)),
        )

    def from_core(self):
        g = self.ring
        for other in range(g.outers):
            self.core_copy(other).wait_recv()
        for by in range(1, g.outers):
            goal = g.after(by)
            add_strips(
                self.outer_out.at[by - 1], [self.part.at[:, goal * 2 + g.k], self.core_in.at[goal]], self.chunk
            )
            self.outer_copy(by).start()
        add_strips(self.strip_sum, [self.part.at[:, g.c], self.core_in.at[g.o]], self.chunk)

    def core_done(self):
        for other in range(self.ring.outers):
            self.core_copy(other).wait_send()

    def from_outer(self):
        for by in range(1, self.ring.outers):
            self.outer_copy(by).wait_recv()
        terms = [self.strip_sum] + [self.outer_in.at[by - 1] for by in range(1, self.ring.outers)]
        if len(terms) > 1:
            add_strips(self.strip_sum, terms, self.chunk)

    def outer_done(self):
        for by in range(1, self.ring.outers):
            self.outer_copy(by).wait_send()


class Share:
    def __init__(self, ring, item, slot, sems, source=None):
        self.ring, self.item, self.slot = ring, item, slot
        self.source = slot(ring.c) if source is None else source
        self.y_send, self.y_recv, self.k_send, self.k_recv = sems

    def outer_copy(self, by):
        g = self.ring
        return copy_to(
            self.source, self.slot(g.c), self.y_send.at[self.item, by], self.y_recv.at[self.item, by],
            g.at_o(g.after(by)),
        )

    def core_copy(self, by):
        g = self.ring
        there = self.slot(g.before(by) * 2 + g.k)
        return copy_to(
            self.source if by == 0 else there, there, self.k_send.at[self.item, by], self.k_recv.at[self.item, by],
            g.at_k,
        )

    def start(self):
        for by in range(1, self.ring.outers):
            self.outer_copy(by).start()
        self.core_copy(0).start()

    def pass_on(self):
        g = self.ring
        for by in range(1, g.outers):
            there = self.slot(g.before(by) * 2 + g.k)
            copy_to(there, there, self.y_send.at[self.item, by], self.y_recv.at[self.item, by], g.at_k).wait_recv()
            self.core_copy(by).start()

    def finish(self):
        g = self.ring
        for by in range(g.outers):
            there = self.slot(g.before(by) * 2 + 1 - g.k)
            copy_to(there, there, self.k_send.at[self.item, by], self.k_recv.at[self.item, by], g.at_k).wait_recv()
        for by in range(1, g.outers):
            self.outer_copy(by).wait_send()
        for by in range(g.outers):
            self.core_copy(by).wait_send()


def rotate_tile(u, cosine, sine, first):
    partner = jnp.where(
        first, pltpu.roll(u, LANES - HEAD_WIDTH // 2, 1), pltpu.roll(u, HEAD_WIDTH // 2, 1)
    )
    return u * cosine + partner * sine


def store_part(part, i, tile):
    size, taken = part.shape[2], tile.shape[0]
    per = part.shape[1] * size // taken
    for r in range(taken // size):
        part[i // per, lax.rem(i, per) * (taken // size) + r] = tile[r * size : (r + 1) * size].astype(BF)


def build_back(planes, contexts, rows, width, query_cols, kv_cols, units):
    outers = contexts // 2
    half = width // 2
    depth = width // planes
    strip = depth // contexts
    unit_strip = units // contexts
    seq_len = rows * contexts
    n_q, n_kv = query_cols // LANES, kv_cols // LANES
    heads = query_cols // HEAD_WIDTH
    group = query_cols // kv_cols
    qkv_cols = query_cols + 2 * kv_cols
    DOWN, GATE, UP, KV = range(4)
    lots = max(outers - 1, 1)

    def kernel(
        gate_hbm, up_hbm, down_hbm, norm_hbm, cot_hbm, qkv_hbm, out_hbm, q_hbm, kv_hbm, mid_hbm, tok_hbm,
        gains, cosine, sine, pos_q, pos_k, log_sum, scales,
        input_grad, gate_strip, up_strip, down_out, mid_full, qkv_grad, gain_rows, mlp_part,
        norm_x_in, norm_z_in, norm_x_out, norm_sum, mlp_stage,
        row_core_in, col_core_in, row_outer_in, col_outer_in, row_outer_out, col_outer_out, row_sum, col_sum,
        kv_core_in, kv_outer_in, sq_out, sq_in, first_x_out, first_x_in,
        x_send, x_recv, z_send, z_recv, k_send, k_recv, y_send, y_recv, grad_send, grad_recv, sy_send, sy_recv, sk_send,
        sk_recv, load_sem, stage_sem, credit,
    ):
        ring = Ring(planes, contexts)
        z, c, t, k, o = ring.z, ring.c, ring.t, ring.k, ring.o
        order = ring.by_distance()
        blocks = order[::-1] + [z]
        ring.greet()
        own_cols = pl.multiple_of(t * half, half)
        other_cols = pl.multiple_of((1 - t) * half, half)
        n_half = half // WIDE

        def x_copy(i, src, dst):
            return copy_to(src, dst, x_send.at[i], x_recv.at[i], ring.at_x)

        NORM, MID, SQ_TWO, FIRST, SQ_ONE = 0, planes, planes + 1, planes + 2, planes + 3

        def norm_x(i):
            return x_copy(NORM + i, norm_x_out.at[i % 2], norm_x_in.at[blocks[i]])

        def back_from(p, here):
            return lax.rem(p - here + planes, planes) - 1

        def norm_z(p):
            return copy_to(
                norm_sum.at[p], norm_z_in.at[back_from(z, p)], z_send.at[0, p], z_recv.at[0, z], ring.at_z(p)
            )

        def norm_z_wait(p):
            there = norm_z_in.at[back_from(p, z)]
            copy_to(there, there, z_send.at[0, p], z_recv.at[0, p], ring.at_k).wait_recv()

        def add_block(total, other, p):
            n = rows // 64

            @pl.loop(0, n)
            def _(i):
                r = pl.ds(pl.multiple_of(i * 64, 64), 64)
                total[p, r, :] = (total[p, r, :].astype(F32) + other[p, r, :].astype(F32)).astype(BF)

        def norm_on(i):
            norm_x(i).wait_recv()
            add_block(norm_sum, norm_x_in, blocks[i])

        sems = (k_send, k_recv, y_send, y_recv)

        def feed_forward(norm, cot, hid, gate_grad, up_grad):
            def load(i, src, dst):
                one = pltpu.make_async_copy(src, dst, load_sem.at[i])
                one.start()
                return one

            loads = [
                (load(2 * i, norm_hbm.at[p], norm.at[p]), load(2 * i + 1, cot_hbm.at[p], cot.at[p]))
                for i, p in enumerate(blocks)
            ]

            def product(part, left, right, size):
                total = planes * rows

                @pl.loop(0, left.shape[2] // size)
                def _(i):
                    cols = pl.ds(pl.multiple_of(i * size, size), size)
                    tile = t_dot(left[:, :, cols].reshape(total, size), right[...].reshape(total, right.shape[2]))
                    store_part(part, i, tile)

            def with_weights(gate_w, up_w, down_w, col_part):
                weights = [
                    load(2 * planes, gate_hbm, gate_w),
                    load(2 * planes + 1, up_hbm, up_w),
                    load(2 * planes + 2, down_hbm, down_w),
                ]
                for one in weights:
                    one.wait()
                def forward_block(i):
                    p = blocks[i]
                    loads[i][0].wait()
                    loads[i][1].wait()

                    @pl.loop(0, units // TILE)
                    def _(j):
                        cols = pl.ds(pl.multiple_of(j * TILE, TILE), TILE)
                        gate = jnp.dot(norm[p], gate_w[:, cols], preferred_element_type=F32)
                        up = jnp.dot(norm[p], up_w[:, cols], preferred_element_type=F32)
                        grad = dot_t(cot[p], down_w[cols, :])
                        sig = jax.nn.sigmoid(gate)
                        act = gate * sig
                        hid[p, :, cols] = (act * up).astype(BF)
                        gate_grad[p, :, cols] = (grad * up * sig * (1.0 + gate * (1.0 - sig))).astype(BF)
                        up_grad[p, :, cols] = (grad * act).astype(BF)

                def norm_block(i):
                    p = blocks[i]

                    def tile_of(at):
                        r = pl.ds(pl.multiple_of(at, WIDE), WIDE)
                        return dot_t(gate_grad[p], gate_w[r, :]) + dot_t(up_grad[p], up_w[r, :])

                    if i > 1:
                        norm_x(i - 2).wait_send()

                    @pl.loop(0, n_half)
                    def _(j):
                        here = pl.ds(pl.multiple_of(j * WIDE, WIDE), WIDE)
                        norm_x_out[i % 2, :, here] = tile_of(other_cols + j * WIDE).astype(BF)

                    norm_x(i).start()

                    @pl.loop(0, n_half)
                    def _(j):
                        here = pl.ds(pl.multiple_of(j * WIDE, WIDE), WIDE)
                        norm_sum[p, :, here] = tile_of(own_cols + j * WIDE).astype(BF)

                    if i > 1:
                        norm_on(i - 2)
                        norm_z(blocks[i - 2]).start()

                down = Reduction(
                    ring, DOWN, col_part, col_core_in, col_outer_out, col_outer_in, col_sum, sems
                )
                for i in range(planes):
                    forward_block(i)
                    norm_block(i)
                product(col_part, hid, cot, TILE)
                down.to_core()
                norm_on(planes - 2)
                norm_z(blocks[planes - 2]).start()

                def stage_copy(i):
                    return pltpu.make_async_copy(mlp_stage.at[i % 2], mlp_part.at[blocks[i]], stage_sem.at[i % 2])

                for i, p in enumerate(blocks):
                    if i > 1:
                        stage_copy(i - 2).wait()

                    @pl.loop(0, width // WIDE)
                    def _(j):
                        r = pl.ds(pl.multiple_of(j * WIDE, WIDE), WIDE)
                        mlp_stage[i % 2, :, r] = jnp.dot(hid[p], down_w[:, r], preferred_element_type=F32).astype(BF)

                    stage_copy(i).start()
                    if i == 0:
                        down.from_core()
                for i in range(max(planes - 2, 0), planes):
                    stage_copy(i).wait()
                down.core_done()

            pl.run_scoped(
                with_weights,
                pltpu.VMEM((width, units), BF), pltpu.VMEM((width, units), BF), pltpu.VMEM((units, width), BF),
                pltpu.VMEM((1, contexts, unit_strip, width), BF),
            )

            def with_parts(row_part):
                gate = Reduction(
                    ring, GATE, row_part, row_core_in, row_outer_out.at[0], row_outer_in.at[0], row_sum.at[0], sems
                )
                up = Reduction(
                    ring, UP, row_part, row_core_in, row_outer_out.at[1], row_outer_in.at[1], row_sum.at[1], sems
                )
                product(row_part, norm, gate_grad, WIDE)
                gate.to_core()
                norm_on(planes - 1)
                gate.from_core()
                gate.core_done()
                pl.semaphore_signal(credit, inc=1, device_id=ring.at_k, device_id_type=MESH)
                product(row_part, norm, up_grad, WIDE)
                pl.semaphore_wait(credit, 1)
                up.to_core()
                up.from_core()
                up.core_done()

            pl.run_scoped(with_parts, pltpu.VMEM((planes, contexts, strip, units), BF))

        block_bf = pltpu.VMEM((planes, rows, width), BF)
        unit_bf = pltpu.VMEM((planes, rows, units), BF)
        pl.run_scoped(feed_forward, block_bf, block_bf, unit_bf, unit_bf, unit_bf)

        down = Reduction(ring, DOWN, None, None, col_outer_out, col_outer_in, col_sum, sems)
        gate = Reduction(ring, GATE, None, None, row_outer_out.at[0], row_outer_in.at[0], row_sum.at[0], sems)
        up = Reduction(ring, UP, None, None, row_outer_out.at[1], row_outer_in.at[1], row_sum.at[1], sems)

        def strip_src(item, goal):
            if item == DOWN:
                return col_sum.at[0, :, pl.ds(pl.multiple_of(goal * depth, depth), depth)]
            return row_sum.at[0 if item == GATE else 1, goal]

        def strip_dst(item, home):
            if item == DOWN:
                return down_out.at[home, c]
            cols = pl.ds(pl.multiple_of(home * units, units), units)
            return (gate_strip if item == GATE else up_strip).at[:, cols]

        def strip_copy(item, s):
            goal = ring.plane(s)
            return copy_to(
                strip_src(item, goal), strip_dst(item, z), grad_send.at[item, s], grad_recv.at[item, z], ring.at_z(goal)
            )

        def strip_keep(item):
            return pltpu.make_async_copy(strip_src(item, z), strip_dst(item, z), grad_send.at[item, 0])

        def to_planes(item, reduction):
            reduction.from_outer()
            for s in range(1, planes):
                strip_copy(item, s).start()
            strip_keep(item).start()

        def from_planes(item):
            for s in range(1, planes):
                p = ring.plane(s)
                there = strip_dst(item, p)
                copy_to(there, there, grad_send.at[item, s], grad_recv.at[item, p], ring.at_k).wait_recv()
            strip_keep(item).wait()

        share_sems = (sy_send, sy_recv, sk_send, sk_recv)
        down_share = Share(ring, 0, lambda q: down_out.at[:, q], share_sems)

        def attention(mid_grad, q_pad, kv_all, tok, grad_pad, query_out, key_sum, value_sum, kv_grad, kv_out):
            loads = [
                pltpu.make_async_copy(mid_hbm, mid_grad, load_sem.at[0]),
                pltpu.make_async_copy(tok_hbm.at[:, pl.ds(own_cols, half)], tok, load_sem.at[1]),
                pltpu.make_async_copy(q_hbm, q_pad, load_sem.at[2]),
                pltpu.make_async_copy(kv_hbm, kv_all, load_sem.at[3]),
                pltpu.make_async_copy(cot_hbm.at[z, :, pl.ds(own_cols, half)], first_x_out, load_sem.at[4]),
            ]
            for one in loads:
                one.start()
            for one in loads:
                one.wait()
            key_sum[...] = jnp.zeros_like(key_sum)
            value_sum[...] = jnp.zeros_like(value_sum)
            gain_rows[...] = jnp.zeros_like(gain_rows)

            def norm_back(grad, normal, scale, gain, gain_row, i):
                scaled = grad * gain
                gain_rows[gain_row : gain_row + 1, :] = jnp.sum(grad * normal, 0, keepdims=True)
                mine = jnp.sum(scaled * normal, -1, keepdims=True)
                sq_out[i] = jnp.broadcast_to(mine, (rows, LANES))
                swap = x_copy(SQ_TWO if i == 0 else SQ_ONE, sq_out.at[i], sq_in.at[i])
                swap.start()
                swap.wait()
                inner = (mine + sq_in[i][:, 0:1]) * (1.0 / width)
                return scale * (scaled - normal * inner)

            for p in order:
                norm_z_wait(p)
            grad = norm_sum[z].astype(F32)
            for p in order:
                grad = grad + norm_z_in[back_from(p, z)].astype(F32)
            scale_two = scales[1][:, 0:1]
            gain_two = gains[1:2, pl.ds(own_cols, half)].astype(F32)
            back = norm_back(grad, mid_grad[...] * scale_two, scale_two, gain_two, 1, 0)
            mid_grad[...] = first_x_out[...].astype(F32) + back
            mine = mid_full.at[:, pl.ds(own_cols, half)]
            mid_full[:, pl.ds(own_cols, half)] = mid_grad[...].astype(BF)
            mid_swap = x_copy(MID, mine, mine)
            mid_swap.start()
            to_planes(DOWN, down)
            mid_swap.wait_recv()

            lane = lax.broadcasted_iota(jnp.int32, (rows, LANES), 1)
            first = lax.rem(lane, HEAD_WIDTH) < HEAD_WIDTH // 2
            low = lane < HEAD_WIDTH

            def with_out(out_w):
                one = pltpu.make_async_copy(out_hbm, out_w, load_sem.at[0])
                one.start()
                one.wait()

                @pl.loop(0, query_cols // TILE)
                def _(i):
                    r = pl.ds(pl.multiple_of(i * TILE, TILE), TILE)
                    found = dot_t(mid_full[...], out_w[r, :])
                    for half_tile in range(TILE // LANES):
                        j = i * (TILE // LANES) + half_tile
                        u = found[:, half_tile * LANES : (half_tile + 1) * LANES]
                        u = u.astype(BF).astype(F32)
                        side = lax.rem((2 * j) // group, 2)
                        lo = jnp.where(low, u, 0.0)
                        hi = jnp.where(low, 0.0, u)
                        grad_pad[2 * j] = jnp.where(side == 0, lo, pltpu.roll(lo, HEAD_WIDTH, 1)).astype(BF)
                        grad_pad[2 * j + 1] = jnp.where(side == 1, hi, pltpu.roll(hi, HEAD_WIDTH, 1)).astype(BF)

            pl.run_scoped(with_out, pltpu.VMEM((query_cols, width), BF))

            def attend_back(first_head, last_head):
                @pl.loop(first_head, last_head)
                def _(h):
                    pair = h // (2 * group)
                    keys = kv_all[:, pair].reshape(seq_len, LANES)
                    values = kv_all[:, n_kv + pair].reshape(seq_len, LANES)
                    scores = dot_t(keys, q_pad[h])
                    scores = jnp.where(pos_q[0:1, :] >= pos_k[...], scores, NEG)
                    weights = jnp.exp(scores - log_sum[pl.ds(h, 1), :])
                    weight_grad = dot_t(values, grad_pad[h])
                    inner = jnp.sum(weights * weight_grad, 0, keepdims=True)
                    score_grad = (weights * (weight_grad - inner)).astype(BF)
                    value_sum[pair] += jnp.dot(weights.astype(BF), grad_pad[h], preferred_element_type=F32)
                    key_sum[pair] += jnp.dot(score_grad, q_pad[h], preferred_element_type=F32)
                    query_out[h] = t_dot(keys, score_grad).T

            attend_back(0, heads // 2)
            to_planes(GATE, gate)
            attend_back(heads // 2, heads)
            for i in range(n_kv):
                kv_grad[:, i] = key_sum[i].astype(BF).reshape(contexts, rows, LANES)
                kv_grad[:, n_kv + i] = value_sum[i].astype(BF).reshape(contexts, rows, LANES)

            def kv_core(other):
                return copy_to(
                    kv_grad.at[other * 2 + 1 - k], kv_core_in.at[other], k_send.at[KV, other], k_recv.at[KV, other],
                    ring.at_k,
                )

            def kv_outer(by):
                return copy_to(
                    kv_out.at[by - 1], kv_outer_in.at[by - 1], y_send.at[KV, by], y_recv.at[KV, by],
                    ring.at_o(ring.after(by)),
                )

            for other in range(outers):
                kv_core(other).start()
            for j in range(n_q):
                side = (2 * j) // group % 2
                lo, hi = query_out[2 * j], query_out[2 * j + 1]
                if side == 0:
                    hi = pltpu.roll(hi, HEAD_WIDTH, 1)
                else:
                    lo = pltpu.roll(lo, HEAD_WIDTH, 1)
                u = jnp.where(low, lo, hi) * FACTOR
                qkv_grad[:, j * LANES : (j + 1) * LANES] = rotate_tile(u, cosine[...], -sine[...], first).astype(BF)
            for other in range(outers):
                kv_core(other).wait_recv()
            for by in range(1, outers):
                goal = ring.after(by)
                kv_out[by - 1] = (
                    kv_grad[goal * 2 + k].astype(F32) + kv_core_in[goal].astype(F32)
                ).astype(BF)
                kv_outer(by).start()
            to_planes(UP, up)
            from_planes(DOWN)
            down_share.start()
            kv_sum = kv_grad[c].astype(F32) + kv_core_in[o].astype(F32)
            for by in range(1, outers):
                kv_outer(by).wait_recv()
                kv_sum = kv_sum + kv_outer_in[by - 1].astype(F32)
            for i in range(n_kv):
                at = query_cols + i * LANES
                qkv_grad[:, at : at + LANES] = rotate_tile(kv_sum[i], cosine[...], -sine[...], first).astype(BF)
                qkv_grad[:, at + kv_cols : at + kv_cols + LANES] = kv_sum[n_kv + i].astype(BF)
            for other in range(outers):
                kv_core(other).wait_send()
            for by in range(1, outers):
                kv_outer(by).wait_send()

            first_swap = x_copy(FIRST, first_x_out, first_x_in)

            def with_qkv(qkv_w, own):
                one = pltpu.make_async_copy(qkv_hbm, qkv_w, load_sem.at[0])
                one.start()
                one.wait()

                def tile_of(at):
                    return dot_t(qkv_grad[...], qkv_w[pl.ds(pl.multiple_of(at, WIDE), WIDE), :])

                @pl.loop(0, n_half)
                def _(j):
                    here = pl.ds(pl.multiple_of(j * WIDE, WIDE), WIDE)
                    first_x_out[:, here] = tile_of(other_cols + j * WIDE).astype(BF)

                first_swap.start()

                @pl.loop(0, n_half)
                def _(j):
                    here = pl.ds(pl.multiple_of(j * WIDE, WIDE), WIDE)
                    own[:, here] = tile_of(own_cols + j * WIDE)

                first_swap.wait()
                scale_one = scales[0][:, 0:1]
                gain_one = gains[0:1, pl.ds(own_cols, half)].astype(F32)
                back = norm_back(
                    own[...] + first_x_in[...].astype(F32), tok[...].astype(F32) * scale_one, scale_one, gain_one, 0, 1
                )
                input_grad[...] = (mid_grad[...] + back).astype(BF)

            pl.run_scoped(with_qkv, pltpu.VMEM((width, qkv_cols), BF), pltpu.VMEM((rows, half), F32))
            mid_swap.wait_send()

        tile_f32 = pltpu.VMEM((rows, half), F32)
        pl.run_scoped(
            attention,
            tile_f32,
            pltpu.VMEM((heads, rows, LANES), BF),
            pltpu.VMEM((contexts, 2 * n_kv, rows, LANES), BF),
            pltpu.VMEM((rows, half), BF),
            pltpu.VMEM((heads, rows, LANES), BF),
            pltpu.VMEM((heads, rows, LANES), F32),
            pltpu.VMEM((n_kv, seq_len, LANES), F32),
            pltpu.VMEM((n_kv, seq_len, LANES), F32),
            pltpu.VMEM((contexts, 2 * n_kv, rows, LANES), BF),
            pltpu.VMEM((lots, 2 * n_kv, rows, LANES), BF),
        )

        down_share.pass_on()
        from_planes(GATE)
        from_planes(UP)
        down_share.finish()
        for item in (DOWN, GATE, UP):
            for s in range(1, planes):
                strip_copy(item, s).wait_send()
        for reduction in (down, gate, up):
            reduction.outer_done()
        for i in range(max(planes - 2, 0), planes):
            norm_x(i).wait_send()
        for p in order:
            norm_z(p).wait_send()

    hbm = pl.BlockSpec(memory_space=pl.ANY)
    vmem = pl.BlockSpec(memory_space=pltpu.VMEM)
    dma = pltpu.SemaphoreType.DMA
    shape = jax.ShapeDtypeStruct
    acts = pltpu.VMEM((planes, rows, half), BF)
    arrivals = pltpu.VMEM((planes - 1, rows, half), BF)
    return pl.pallas_call(
        kernel,
        name="back",
        out_shape=(
            shape((rows, half), BF),
            shape((strip, planes * units), BF),
            shape((strip, planes * units), BF),
            shape((planes, contexts, unit_strip, depth), BF),
            shape((rows, width), BF),
            shape((rows, qkv_cols), BF),
            shape((8, half), F32),
            shape((planes, rows, width), BF),
        ),
        in_specs=[hbm] * 11 + [vmem] * 7,
        out_specs=(vmem, hbm, hbm, hbm, vmem, vmem, vmem, hbm),
        scratch_shapes=[acts, arrivals, pltpu.VMEM((2, rows, half), BF), acts, pltpu.VMEM((2, rows, width), BF)]
        + [
            pltpu.VMEM((outers, planes, strip, units), BF),
            pltpu.VMEM((outers, 1, unit_strip, width), BF),
            pltpu.VMEM((2, lots, planes, strip, units), BF),
            pltpu.VMEM((lots, 1, unit_strip, width), BF),
            pltpu.VMEM((2, lots, planes, strip, units), BF),
            pltpu.VMEM((lots, 1, unit_strip, width), BF),
            pltpu.VMEM((2, planes, strip, units), BF),
            pltpu.VMEM((1, unit_strip, width), BF),
            pltpu.VMEM((outers, 2 * n_kv, rows, LANES), BF),
            pltpu.VMEM((lots, 2 * n_kv, rows, LANES), BF),
            pltpu.VMEM((2, rows, LANES), F32),
            pltpu.VMEM((2, rows, LANES), F32),
            pltpu.VMEM((rows, half), BF),
            pltpu.VMEM((rows, half), BF),
            dma((planes + 4,)),
            dma((planes + 4,)),
            dma((1, planes)),
            dma((1, planes)),
            dma((4, outers)),
            dma((4, outers)),
            dma((4, max(outers, 2))),
            dma((4, max(outers, 2))),
            dma((3, planes)),
            dma((3, planes)),
            dma((2, max(outers, 2))),
            dma((2, max(outers, 2))),
            dma((2, outers)),
            dma((2, outers)),
            dma((2 * planes + 3,)),
            dma((2,)),
            pltpu.SemaphoreType.REGULAR,
        ],
        compiler_params=pltpu.CompilerParams(
            collective_id=1, has_side_effects=True, vmem_limit_bytes=VMEM_LIMIT
        ),
        cost_estimate=pl.CostEstimate(flops=50 * 10**9, bytes_accessed=80 * 10**6, transcendentals=8 * 10**6),
    )


def build_grads(planes, contexts, rows, width, query_cols, kv_cols, units):
    outers = contexts // 2
    half = width // 2
    depth = width // planes
    strip = depth // contexts
    out_strip = query_cols // contexts
    unit_strip = units // contexts
    qkv_cols = query_cols + 2 * kv_cols
    lots = max(outers - 1, 1)
    per_half = planes // 2
    OUT, QKV, UP, GATE = range(4)

    def kernel(
        attn, mid_full, normed_one, qkv_grad, gain_rows, mid_own, gate_strip, up_strip, mlp_part,
        gate_out, up_out, out_out, qkv_out, gain_out, result,
        out_part, qkv_part, out_core, qkv_core, out_outer_out, qkv_outer_out, out_outer_in, qkv_outer_in,
        out_sum, qkv_sum, out_z, qkv_z, gain_z, gain_y, gain_k, gain_now, mlp_x_in, mlp_z_in, mlp_sum,
        k_send, k_recv, y_send, y_recv, z_send, z_recv, sk_send, sk_recv, sy_send, sy_recv, gain_send, gain_recv,
        mx_send, mx_recv, mz_send, mz_recv, own_sem,
    ):
        ring = Ring(planes, contexts)
        z, c, t, k, o = ring.z, ring.c, ring.t, ring.k, ring.o
        order = ring.by_distance()
        ring.greet()

        def rows_of(whole, size):
            return lambda q: whole.at[pl.ds(pl.multiple_of(q * size, size), size), :]

        share_sems = (sy_send, sy_recv, sk_send, sk_recv)
        up_share = Share(ring, UP, rows_of(up_out, strip), share_sems, up_strip)
        out_share = Share(ring, OUT, rows_of(out_out, out_strip), share_sems)
        qkv_share = Share(ring, QKV, rows_of(qkv_out, strip), share_sems)
        gate_share = Share(ring, GATE, rows_of(gate_out, strip), share_sems, gate_strip)
        gate_share.start()
        keeps = [
            pltpu.make_async_copy(gate_strip, rows_of(gate_out, strip)(c), own_sem.at[0]),
            pltpu.make_async_copy(up_strip, rows_of(up_out, strip)(c), own_sem.at[2]),
        ]
        for one in keeps:
            one.start()

        own_cols = pl.multiple_of(t * half, half)
        other_cols = pl.multiple_of((1 - t) * half, half)
        blocks = order[::-1] + [z]

        def mlp_x(p):
            return copy_to(
                mlp_part.at[p, :, pl.ds(other_cols, half)], mlp_x_in.at[p], mx_send.at[p], mx_recv.at[p], ring.at_x
            )

        def mlp_z(p):
            return copy_to(
                mlp_sum.at[p], mlp_z_in.at[lax.rem(z - p + planes, planes) - 1], mz_send.at[p], mz_recv.at[z],
                ring.at_z(p),
            )

        mlp_load = pltpu.make_async_copy(mlp_part.at[:, :, pl.ds(own_cols, half)], mlp_sum, own_sem.at[1])
        for p in blocks:
            mlp_x(p).start()
        mlp_load.start()

        def mlp_on(p):
            mlp_x(p).wait_recv()

            @pl.loop(0, rows // 64)
            def _(i):
                r = pl.ds(pl.multiple_of(i * 64, 64), 64)
                mlp_sum[p, r, :] = (mlp_sum[p, r, :].astype(F32) + mlp_x_in[p, r, :].astype(F32)).astype(BF)

        takes_part = z // per_half == t

        def gain_plane(j):
            return t * per_half + j

        def gain_copy(j):
            return copy_to(
                gain_rows.at[:, pl.ds(j * depth, depth)], gain_z.at[z], gain_send.at[j], gain_recv.at[z],
                ring.at_z(gain_plane(j)),
            )

        for j in range(per_half):

            @pl.when(gain_plane(j) != z)
            def _(j=j):
                gain_copy(j).start()

        gain_x = copy_to(
            gain_out, gain_out, gain_send.at[per_half], gain_recv.at[planes], ring.at_x
        )

        def gain_outer(by):
            return copy_to(
                gain_now.at[0], gain_y.at[by - 1], gain_send.at[per_half + by], gain_recv.at[planes + by],
                ring.at_o(ring.after(by)),
            )

        gain_core = copy_to(
            gain_now.at[1], gain_k, gain_send.at[per_half + outers], gain_recv.at[planes + outers], ring.at_k
        )

        def product(part, left, right):
            @pl.loop(0, left.shape[1] // TILE)
            def _(i):
                cols = pl.ds(pl.multiple_of(i * TILE, TILE), TILE)
                store_part(part, i, t_dot(left[:, cols], right[...]))

        sems = (k_send, k_recv, y_send, y_recv)
        out = Reduction(ring, 0, out_part, out_core, out_outer_out, out_outer_in, out_sum, sems)
        qkv = Reduction(ring, 1, qkv_part, qkv_core, qkv_outer_out, qkv_outer_in, qkv_sum, sems)
        product(qkv_part, normed_one, qkv_grad)
        qkv.to_core()
        product(out_part, attn, mid_full)
        qkv.from_core()
        out.to_core()

        @pl.when(takes_part)
        def _():
            mine = lax.rem(z, per_half) * depth
            total = gain_rows[:, pl.ds(pl.multiple_of(mine, depth), depth)]
            for s in range(1, planes):
                p = ring.plane(s)
                copy_to(gain_z.at[p], gain_z.at[p], gain_send.at[0], gain_recv.at[p], ring.at_k).wait_recv()
                total = total + gain_z[p]
            gain_now[0] = total
            for by in range(1, outers):
                gain_outer(by).start()

        out.from_core()
        mlp_load.wait()
        for p in blocks[:-1]:
            mlp_on(p)
            mlp_z(p).start()

        @pl.when(takes_part)
        def _():
            total = gain_now[0]
            for by in range(1, outers):
                gain_outer(by).wait()
                total = total + gain_y[by - 1]
            gain_now[1] = total
            gain_core.start()

        def piece(item, p):
            if item == OUT:
                return out_sum.at[0, :, pl.ds(pl.multiple_of(p * depth, depth), depth)]
            return qkv_sum.at[p]

        def landing(item, p):
            return (out_z if item == OUT else qkv_z).at[p]

        def z_copy(item, s):
            p = ring.plane(s)
            return copy_to(
                piece(item, p), landing(item, z), z_send.at[item, s], z_recv.at[item, z], ring.at_z(p)
            )

        def to_planes(item, reduction):
            reduction.from_outer()
            for s in range(1, planes):
                z_copy(item, s).start()

        def from_planes(item):
            for p in order:
                there = landing(item, p)
                copy_to(there, there, z_send.at[item, 0], z_recv.at[item, p], ring.at_k).wait_recv()
            size = out_strip if item == OUT else strip
            whole = out_out if item == OUT else qkv_out
            total = piece(item, z)[...].astype(F32)
            for p in order:
                total = total + landing(item, p)[...].astype(F32)
            whole[pl.ds(pl.multiple_of(c * size, size), size), :] = total.astype(BF)
            (out_share if item == OUT else qkv_share).start()

        to_planes(QKV, qkv)

        @pl.when(takes_part)
        def _():
            gain_core.wait()
            gain_out[...] = gain_now[1] + gain_k[...]
            gain_x.start()

        to_planes(OUT, out)
        up_share.start()
        from_planes(QKV)
        mlp_on(z)
        from_planes(OUT)
        total = mid_own[...] + mlp_sum[z].astype(F32)
        for p in order:
            there = mlp_z_in.at[lax.rem(p - z + planes, planes) - 1]
            copy_to(there, there, mz_send.at[p], mz_recv.at[p], ring.at_k).wait_recv()
            total = total + there[...].astype(F32)
        result[...] = total.astype(BF)
        for one in (gate_share, up_share, qkv_share, out_share):
            one.pass_on()
        for one in keeps:
            one.wait()
        for one in (gate_share, up_share, qkv_share, out_share):
            one.finish()
        for p in blocks:
            mlp_x(p).wait_send()
        for p in order:
            mlp_z(p).wait_send()
        for reduction in (out, qkv):
            reduction.core_done()
            reduction.outer_done()
        for item in (OUT, QKV):
            for s in range(1, planes):
                z_copy(item, s).wait_send()
        for j in range(per_half):

            @pl.when(gain_plane(j) != z)
            def _(j=j):
                gain_copy(j).wait_send()

        @pl.when(takes_part)
        def _():
            gain_x.wait_send()

        @pl.when(jnp.logical_not(takes_part))
        def _():
            gain_x.wait_recv()

    hbm = pl.BlockSpec(memory_space=pl.ANY)
    vmem = pl.BlockSpec(memory_space=pltpu.VMEM)
    dma = pltpu.SemaphoreType.DMA
    shape = jax.ShapeDtypeStruct
    return pl.pallas_call(
        kernel,
        name="grads",
        out_shape=(
            shape((depth, planes * units), BF),
            shape((depth, planes * units), BF),
            shape((query_cols, depth), BF),
            shape((depth, qkv_cols), BF),
            shape((8, depth), F32),
            shape((rows, half), BF),
        ),
        in_specs=[vmem] * 6 + [hbm] * 3,
        out_specs=(hbm, hbm, vmem, vmem, vmem, vmem),
        scratch_shapes=[
            pltpu.VMEM((1, contexts, out_strip, width), BF),
            pltpu.VMEM((planes, contexts, strip, qkv_cols), BF),
            pltpu.VMEM((outers, 1, out_strip, width), BF),
            pltpu.VMEM((outers, planes, strip, qkv_cols), BF),
            pltpu.VMEM((lots, 1, out_strip, width), BF),
            pltpu.VMEM((lots, planes, strip, qkv_cols), BF),
            pltpu.VMEM((lots, 1, out_strip, width), BF),
            pltpu.VMEM((lots, planes, strip, qkv_cols), BF),
            pltpu.VMEM((1, out_strip, width), BF),
            pltpu.VMEM((planes, strip, qkv_cols), BF),
            pltpu.VMEM((planes, out_strip, depth), BF),
            pltpu.VMEM((planes, strip, qkv_cols), BF),
            pltpu.VMEM((planes, 8, depth), F32),
            pltpu.VMEM((lots, 8, depth), F32),
            pltpu.VMEM((8, depth), F32),
            pltpu.VMEM((2, 8, depth), F32),
            pltpu.VMEM((planes, rows, half), BF),
            pltpu.VMEM((planes - 1, rows, half), BF),
            pltpu.VMEM((planes, rows, half), BF),
            dma((2, outers)),
            dma((2, outers)),
            dma((2, max(outers, 2))),
            dma((2, max(outers, 2))),
            dma((2, planes)),
            dma((2, planes)),
            dma((4, outers)),
            dma((4, outers)),
            dma((4, max(outers, 2))),
            dma((4, max(outers, 2))),
            dma((per_half + outers + 1,)),
            dma((planes + outers + 1,)),
            dma((planes,)),
            dma((planes,)),
            dma((planes,)),
            dma((planes,)),
            dma((3,)),
        ],
        compiler_params=pltpu.CompilerParams(
            collective_id=2, has_side_effects=True, vmem_limit_bytes=VMEM_LIMIT
        ),
        cost_estimate=pl.CostEstimate(flops=4 * 10**9, bytes_accessed=40 * 10**6, transcendentals=0),
    )


def shards(
    tokens,
    span_order,
    attn_gain,
    w_query,
    key_weight,
    value_weight,
    w_out,
    mlp_gain,
    w_gate,
    w_up,
    w_down,
    out_grad,
):
    planes = lax.axis_size("fsdp")
    contexts = lax.axis_size("context")
    tok_own, cot_own = tokens[0], out_grad[0]
    rows, own_cols = tok_own.shape
    width = own_cols * 2
    depth = width // planes
    units = w_gate.shape[1] // planes
    query_cols = w_query.shape[1]
    kv_cols = key_weight.shape[1]
    sizes = (planes, contexts, rows, width, query_cols, kv_cols, units)

    freqs = jnp.tile(rope_freqs(HEAD_WIDTH), LANES // (HEAD_WIDTH // 2))[None]
    (
        gate_w, up_w, down_w, cot_all, norm_all, qkv_w, out_w, gains, q_pad, kv_all, attn, log_sum, mid_own,
        normed_one, tok_all, scales, cosine_table, sine_table, pos_q, pos_k,
    ) = build_front(*sizes)(
        tok_own, cot_own, attn_gain[None], mlp_gain[None], w_query, key_weight, value_weight, w_out, w_gate, w_up,
        w_down, span_order, freqs,
    )
    input_grad, gate_strip, up_strip, down_out, mid_full, qkv_grad, gain_rows, mlp_part = build_back(*sizes)(
        gate_w, up_w, down_w, norm_all, cot_all, qkv_w, out_w, q_pad, kv_all, mid_own, tok_all, gains,
        cosine_table, sine_table, pos_q, pos_k, log_sum, scales,
    )
    gate_out, up_out, out_out, qkv_out, gain_out, result = build_grads(*sizes)(
        attn, mid_full, normed_one, qkv_grad, gain_rows, mid_own, gate_strip, up_strip, mlp_part
    )
    qkv_out = qkv_out.astype(F32)
    return (
        result[None],
        input_grad[None],
        gain_out[0],
        qkv_out[:, :query_cols],
        qkv_out[:, query_cols : query_cols + kv_cols],
        qkv_out[:, query_cols + kv_cols :],
        out_out.astype(F32),
        gain_out[1],
        gate_out.astype(F32),
        up_out.astype(F32),
        down_out.reshape(planes * units, depth).astype(F32),
    )


def solution(mesh):
    weight = P("fsdp", "tensor")
    turned = P("tensor", "fsdp")
    block = P("fsdp", "context", "tensor")
    gain = P("fsdp")
    return jax.shard_map(
        shards,
        mesh=mesh,
        in_specs=(
            block, P(), gain, weight, weight, weight, turned, gain, weight, weight, turned, block,
        ),
        out_specs=(
            block, block, gain, weight, weight, weight, turned, gain, weight, weight, turned,
        ),
        check_vma=False,
    )
```

```python
import math

import jax
import jax.numpy as jnp
from jax import lax
from jax.experimental import pallas as pl
from jax.experimental.pallas import tpu as pltpu
from jax.sharding import PartitionSpec as P

HEAD_WIDTH = 64
EPS = 1e-05
NEG = -1e30
BF = jnp.bfloat16
F32 = jnp.float32
LANES = 128
TILE = 256
WIDE = 512
STEP = 32
FACTOR = 1.0 / math.sqrt(HEAD_WIDTH)
VMEM_LIMIT = 62 * 2**20
MESH = pl.DeviceIdType.MESH


def rope_freqs(head_size):
    half_size = head_size // 2
    index = jnp.arange(half_size, dtype=jnp.float32)
    base_freq = jnp.exp(-(2.0 * index / head_size) * math.log(500000.0))
    wavelen = 2.0 * math.pi / base_freq
    smooth = (8192.0 / wavelen - 1.0) / 3.0
    blended = (1.0 - smooth) * base_freq / 32.0 + smooth * base_freq
    return jnp.where(
        wavelen > 8192.0, base_freq / 32.0, jnp.where(wavelen < 2048.0, base_freq, blended)
    )


def dot_t(left, right):
    return lax.dot_general(left, right, (((1,), (1,)), ((), ())), preferred_element_type=F32)


def t_dot(left, right):
    return lax.dot_general(left, right, (((0,), (0,)), ((), ())), preferred_element_type=F32)


def build_front(planes, contexts, rows, width, query_cols, kv_cols, units):
    outers = contexts // 2
    half = width // 2
    depth = width // planes
    strip = depth // contexts
    out_strip = query_cols // contexts
    unit_strip = units // contexts
    seq_len = rows * contexts
    n_q, n_kv = query_cols // LANES, kv_cols // LANES
    heads = query_cols // HEAD_WIDTH
    group = query_cols // kv_cols
    qkv_cols = query_cols + 2 * kv_cols
    QKV, OUT, GATE, UP, DOWN, COT, NORM, GAIN, LATE = range(9)
    half_rows = rows // 2
    base_of = {COT: 1, NORM: 3 + planes, LATE: 3 + 2 * planes}

    def kernel(
        tok, cot, gain_one_own, gain_two_own, query_own, key_own, value_own, out_own, gate_own, up_own, down_own,
        spans, freqs,
        gate_hbm, up_hbm, down_hbm, cot_hbm, norm_hbm, qkv_hbm, out_hbm, hid_hbm, gate_grad_hbm, up_grad_hbm, gains, q_hbm, kv_hbm, attn_hbm,
        log_sum, mid_hbm, normed_hbm, tok_hbm, scales, cosine, sine, pos_q, pos_k,
        q_pad, kv_all, attn, mid_own, normed_one, tok_all,
        gate_w, up_w, down_w, cot_all, norm_all, acts, qkv_w, out_w, gains_own, lin, heads_out, send_half, recv_half, norm_own, sq_send, sq_recv,
        z_send, z_recv, y_send, y_recv, k_send, k_recv, x_send, x_recv, own_sem, act_sem,
    ):
        z = lax.axis_index("fsdp")
        c = lax.axis_index("context")
        t = lax.axis_index("tensor")
        o, k = c // 2, c % 2

        def at_z(p):
            return (p, c, t)

        def at_o(other):
            return (z, other * 2 + k, t)

        at_k = (z, o * 2 + 1 - k, t)
        at_x = (z, c, 1 - t)

        def copy(src, dst, send_sem, recv_sem, device):
            return pltpu.make_async_remote_copy(
                src_ref=src, dst_ref=dst, send_sem=send_sem, recv_sem=recv_sem,
                device_id=device, device_id_type=MESH,
            )

        barrier = pltpu.get_barrier_semaphore()
        peers = [at_z(lax.rem(z + s, planes)) for s in range(1, planes)]
        peers += [at_o(lax.rem(o + s, outers)) for s in range(1, outers)] + [at_k, at_x]
        for peer in peers:
            pl.semaphore_signal(barrier, inc=1, device_id=peer, device_id_type=MESH)
        pl.semaphore_wait(barrier, len(peers))

        order = []
        for i in range(planes - 1):
            p = jnp.int32(0)
            for plane in range(planes):
                far = sorted((abs(q - plane), q) for q in range(planes) if q != plane)
                p = p + jnp.where(z == plane, far[i][1], 0)
            order.append(p)

        def slot(item, p, q):
            if item == QKV:
                return qkv_w.at[pl.ds(p * depth + q * strip, strip), :]
            if item == OUT:
                return out_w.at[pl.ds(q * out_strip, out_strip), pl.ds(p * depth, depth)]
            if item == GATE:
                return gate_w.at[pl.ds(p * depth + q * strip, strip), :]
            if item == UP:
                return up_w.at[pl.ds(p * depth + q * strip, strip), :]
            if item == DOWN:
                return down_w.at[pl.ds(q * unit_strip, unit_strip), pl.ds(p * depth, depth)]
            if item == COT:
                return cot_all.at[p, :, pl.ds(t * half, half)]
            return norm_all.at[p, pl.ds(0 if item == NORM else half_rows, half_rows), pl.ds(t * half, half)]

        def z_copy(item, p, src, goal, way):
            return copy(src, slot(item, p, c), z_send.at[item, p, way], z_recv.at[item, p], at_z(goal))

        def z_wait(item, p):
            z_copy(item, p, slot(item, p, c), z, 0).wait_recv()

        def spread(item, src):
            @pl.when(z + 1 < planes)
            def _():
                z_copy(item, z, src, z + 1, 0).start()

            @pl.when(z > 0)
            def _():
                z_copy(item, z, src, z - 1, 1).start()

        def spread_done(item, src):
            @pl.when(z + 1 < planes)
            def _():
                z_copy(item, z, src, z + 1, 0).wait_send()

            @pl.when(z > 0)
            def _():
                z_copy(item, z, src, z - 1, 1).wait_send()

        def passes_on(p):
            return ((p < z) & (z + 1 < planes)) | ((p > z) & (z > 0))

        def onward(p):
            return jnp.where(p < z, z + 1, z - 1)

        def forward(item, p):
            @pl.when(passes_on(p))
            def _():
                z_copy(item, p, slot(item, p, c), onward(p), 0).start()

        def forward_done(item, p):
            @pl.when(passes_on(p))
            def _():
                z_copy(item, p, slot(item, p, c), onward(p), 0).wait_send()

        def y_copy(item, p, by):
            here = slot(item, p, c)
            return copy(here, here, y_send.at[item, p, by], y_recv.at[item, p, by], at_o(lax.rem(o + by, outers)))

        def y_wait(item, p, by):
            there = slot(item, p, lax.rem(o - by + outers, outers) * 2 + k)
            copy(there, there, y_send.at[item, p, by], y_recv.at[item, p, by], at_k).wait_recv()

        def k_copy(item, p, by):
            here = slot(item, p, lax.rem(o - by + outers, outers) * 2 + k)
            return copy(here, here, k_send.at[item, p, by], k_recv.at[item, p, by], at_k)

        def k_wait(item, p, by):
            there = slot(item, p, lax.rem(o - by + outers, outers) * 2 + 1 - k)
            copy(there, there, k_send.at[item, p, by], k_recv.at[item, p, by], at_k).wait_recv()

        def share(item, p):
            for by in range(1, outers):
                y_copy(item, p, by).start()
            k_copy(item, p, 0).start()

        def share_on(item, p):
            for by in range(1, outers):
                y_wait(item, p, by)
                k_copy(item, p, by).start()

        def shared(item, p):
            for by in range(outers):
                k_wait(item, p, by)

        def share_done(item, p):
            for by in range(1, outers):
                y_copy(item, p, by).wait_send()
            for by in range(outers):
                k_copy(item, p, by).wait_send()

        def x_copy(i, src, dst):
            return copy(src, dst, x_send.at[i], x_recv.at[i], at_x)

        gains_own[...] = jnp.zeros_like(gains_own)
        gains_own[0:1, :] = gain_one_own[...].astype(F32)
        gains_own[1:2, :] = gain_two_own[...].astype(F32)
        tok_cols = pl.ds(t * half, half)
        tok_copy = x_copy(0, tok, tok_all.at[:, tok_cols])
        tok_copy.start()
        gain_copies = [
            copy(
                gains_own, gains.at[:, pl.ds(z * depth, depth)], z_send.at[GAIN, lax.rem(z + s, planes), 0],
                z_recv.at[GAIN, z], at_z(lax.rem(z + s, planes)),
            )
            for s in range(1, planes)
        ]
        for one in gain_copies:
            one.start()
        home = pl.ds(z * depth, depth)
        own_qkv = [
            pltpu.make_async_copy(query_own, qkv_w.at[home, pl.ds(0, query_cols)], own_sem.at[0]),
            pltpu.make_async_copy(key_own, qkv_w.at[home, pl.ds(query_cols, kv_cols)], own_sem.at[7]),
            pltpu.make_async_copy(value_own, qkv_w.at[home, pl.ds(query_cols + kv_cols, kv_cols)], own_sem.at[8]),
        ]
        for one in own_qkv:
            one.start()
        for one in own_qkv:
            one.wait()
        qkv_src = slot(QKV, z, c)
        out_src = out_own.at[pl.ds(c * out_strip, out_strip), :]
        spread(QKV, qkv_src)
        own_copies = [
            pltpu.make_async_copy(out_own, out_w.at[:, pl.ds(z * depth, depth)], own_sem.at[1]),
            pltpu.make_async_copy(
                gate_own.at[:, pl.ds(z * units, units)], gate_w.at[pl.ds(z * depth, depth), :], own_sem.at[2]
            ),
            pltpu.make_async_copy(
                up_own.at[:, pl.ds(z * units, units)], up_w.at[pl.ds(z * depth, depth), :], own_sem.at[3]
            ),
            pltpu.make_async_copy(
                down_own.at[pl.ds(z * units, units), :], down_w.at[:, pl.ds(z * depth, depth)], own_sem.at[4]
            ),
            pltpu.make_async_copy(cot, slot(COT, z, c), own_sem.at[5]),
        ]
        for one in own_copies:
            one.start()
        gains[:, pl.ds(z * depth, depth)] = gains_own[...]
        tok_all[:, tok_cols] = tok[...]

        def at_distance(i, act):
            for p in (z - (i + 1), z + (i + 1)):

                @pl.when((p >= 0) & (p < planes))
                def _(p=p):
                    act(p)

        def qkv_step(i):
            def act(p):
                z_wait(QKV, p)
                forward(QKV, p)
                share(QKV, p)

            at_distance(i, act)

        qkv_step(0)

        def positions(q, shape, axis):
            r = lax.broadcasted_iota(jnp.int32, shape, axis)
            return jnp.where(r < rows // 2, spans[q, 0], spans[q, 1]) * (rows // 2) + lax.rem(r, rows // 2)

        for q in range(contexts):
            pos_k[q * rows : (q + 1) * rows, :] = positions(q, (rows, 1), 0)
        pos_q[...] = positions(c, (8, rows), 1)
        side_of = lax.rem(lax.broadcasted_iota(jnp.int32, (rows, LANES), 1), HEAD_WIDTH) < HEAD_WIDTH // 2
        angle = positions(c, (rows, LANES), 0).astype(F32) * freqs[...]
        cosine[...] = jnp.cos(angle)
        turned = jnp.sin(angle)
        sine[...] = jnp.where(side_of, -turned, turned)
        qkv_step(1)

        tok_copy.wait()
        for s in range(1, planes):
            p = lax.rem(z + s, planes)
            there = gains.at[:, pl.ds(p * depth, depth)]
            copy(there, there, z_send.at[GAIN, p, 0], z_recv.at[GAIN, p], at_k).wait_recv()

        @pl.loop(0, rows // STEP)
        def _(i):
            r = pl.ds(pl.multiple_of(i * STEP, STEP), STEP)
            x = tok_all[r, :].astype(F32)
            scale = lax.rsqrt(jnp.mean(x * x, -1, keepdims=True) + EPS)
            scales[0, r, :] = jnp.broadcast_to(scale, (STEP, LANES))
            normed_one[r, :] = (x * scale * gains[0:1, :]).astype(BF)

        for i in range(2, planes - 1):
            qkv_step(i)

        spread(OUT, out_src)
        sends = []

        def send_units(item):
            for i, goal in enumerate(order):
                if item == DOWN:
                    src = down_own.at[pl.ds(goal * units + c * unit_strip, unit_strip), :]
                else:
                    own = gate_own if item == GATE else up_own
                    src = own.at[pl.ds(c * strip, strip), pl.ds(goal * units, units)]
                one = z_copy(item, z, src, goal, i)
                one.start()
                sends.append(one)

        def share_units(item):
            for p in order:
                z_wait(item, p)
                share(item, p)

        def cross(item, i):
            base = base_of[item]
            at_distance(i, lambda p: x_copy(base + p, slot(item, p, c), slot(item, p, c)).start())

        def step(item, i, crosses=True):
            def act(p):
                z_wait(item, p)
                forward(item, p)
                if item == OUT:
                    share(OUT, p)

            at_distance(i, act)
            if item != OUT and crosses:
                cross(item, i)

        items = (GATE, UP, DOWN)
        last = planes - 1
        step(OUT, 0)
        spread(COT, cot)
        cot_copy = x_copy(1 + z, cot, slot(COT, z, c))
        cot_copy.start()
        for p in order:
            share_on(QKV, p)
        for p in order:
            shared(QKV, p)
        qkv_keep = pltpu.make_async_copy(qkv_w, qkv_hbm, own_sem.at[0])
        qkv_keep.start()

        n_tile = 2 * LANES

        @pl.loop(0, qkv_cols // n_tile)
        def _(i):
            cols = pl.ds(pl.multiple_of(i * n_tile, n_tile), n_tile)
            found = jnp.dot(normed_one[...], qkv_w[:, cols], preferred_element_type=F32)
            lin[2 * i] = found[:, :LANES]
            lin[2 * i + 1] = found[:, LANES:]

        lane = lax.broadcasted_iota(jnp.int32, (rows, LANES), 1)
        first = lax.rem(lane, HEAD_WIDTH) < HEAD_WIDTH // 2
        low = lane < HEAD_WIDTH

        def rotated(u):
            partner = jnp.where(
                first, pltpu.roll(u, LANES - HEAD_WIDTH // 2, 1), pltpu.roll(u, HEAD_WIDTH // 2, 1)
            )
            return u * cosine[...] + partner * sine[...]

        for i in range(n_kv):
            kv_all[c, i] = rotated(lin[n_q + i]).astype(BF)
            kv_all[c, n_kv + i] = lin[n_q + n_kv + i].astype(BF)

        def kv_slot(q):
            return kv_all.at[q]

        kv_sends = [
            copy(kv_slot(c), kv_slot(c), y_send.at[COT, 0, by], y_recv.at[COT, 0, by], at_o(lax.rem(o + by, outers)))
            for by in range(1, outers)
        ]
        kv_sends.append(copy(kv_slot(c), kv_slot(c), k_send.at[COT, 0, 0], k_recv.at[COT, 0, 0], at_k))
        for one in kv_sends:
            one.start()
        for i in range(1, last - 1):
            step(OUT, i)
        step(COT, 0)
        send_units(GATE)

        @pl.loop(0, n_q)
        def _(j):
            u = rotated(lin[j]).astype(BF).astype(F32) * FACTOR
            side = lax.rem((2 * j) // group, 2)
            lo = jnp.where(low, u, 0.0)
            hi = jnp.where(low, 0.0, u)
            q_pad[2 * j] = jnp.where(side == 0, lo, pltpu.roll(lo, HEAD_WIDTH, 1)).astype(BF)
            q_pad[2 * j + 1] = jnp.where(side == 1, hi, pltpu.roll(hi, HEAD_WIDTH, 1)).astype(BF)

        for by in range(1, outers):
            q = lax.rem(o - by + outers, outers) * 2 + k
            copy(kv_slot(q), kv_slot(q), y_send.at[COT, 0, by], y_recv.at[COT, 0, by], at_k).wait_recv()
            one = copy(kv_slot(q), kv_slot(q), k_send.at[COT, 0, by], k_recv.at[COT, 0, by], at_k)
            one.start()
            kv_sends.append(one)
        for by in range(outers):
            q = lax.rem(o - by + outers, outers) * 2 + 1 - k
            copy(kv_slot(q), kv_slot(q), k_send.at[COT, 0, by], k_recv.at[COT, 0, by], at_k).wait_recv()

        def attend(first_head, last_head):
            @pl.loop(first_head, last_head)
            def _(h):
                pair = h // (2 * group)
                keys = kv_all[:, pair].reshape(seq_len, LANES)
                values = kv_all[:, n_kv + pair].reshape(seq_len, LANES)
                scores = dot_t(keys, q_pad[h])
                scores = jnp.where(pos_q[0:1, :] >= pos_k[...], scores, NEG)
                top = jnp.max(scores, 0, keepdims=True)
                expo = jnp.exp(scores - top)
                total = jnp.sum(expo, 0, keepdims=True)
                weights = (expo * (1.0 / total)).astype(BF)
                heads_out[h] = t_dot(values, weights).T
                log_sum[pl.ds(h, 1), :] = top + jnp.log(total)

        attend(0, heads // 2)
        step(OUT, last - 1)
        for i in range(1, last - 1):
            step(COT, i, False)
        send_units(UP)
        send_units(DOWN)
        for p in order:
            share_on(OUT, p)
        attend(heads // 2, heads)

        for j in range(n_q):
            side = (2 * j) // group % 2
            lo, hi = heads_out[2 * j], heads_out[2 * j + 1]
            if side == 0:
                hi = pltpu.roll(hi, HEAD_WIDTH, 1)
            else:
                lo = pltpu.roll(lo, HEAD_WIDTH, 1)
            attn[:, j * LANES : (j + 1) * LANES] = jnp.where(low, lo, hi).astype(BF)

        for p in order:
            shared(OUT, p)
        own_copies[0].wait()
        out_keep = pltpu.make_async_copy(out_w, out_hbm, own_sem.at[7])
        out_keep.start()

        n_out = half // n_tile

        @pl.loop(0, n_out)
        def _(i):
            cols = pl.ds(pl.multiple_of((1 - t) * half + i * n_tile, n_tile), n_tile)
            here = pl.ds(pl.multiple_of(i * n_tile, n_tile), n_tile)
            send_half[:, here] = jnp.dot(attn[...], out_w[:, cols], preferred_element_type=F32).astype(BF)

        half_copy = x_copy(1 + planes, send_half, recv_half)
        half_copy.start()
        for i in range(1, last - 1):
            cross(COT, i)

        @pl.loop(0, n_out)
        def _(i):
            cols = pl.ds(pl.multiple_of(t * half + i * n_tile, n_tile), n_tile)
            here = pl.ds(pl.multiple_of(i * n_tile, n_tile), n_tile)
            part = jnp.dot(attn[...], out_w[:, cols], preferred_element_type=F32)
            mid_own[:, here] = tok[:, here].astype(F32) + part

        half_copy.wait_recv()

        @pl.loop(0, rows // STEP)
        def _(i):
            r = pl.ds(pl.multiple_of(i * STEP, STEP), STEP)
            mid = mid_own[r, :] + recv_half[r, :].astype(F32)
            mid_own[r, :] = mid
            sq_send[r, :] = jnp.broadcast_to(jnp.sum(mid * mid, -1, keepdims=True), (STEP, LANES))

        sq_copy = x_copy(2 + planes, sq_send, sq_recv)
        sq_copy.start()
        sq_copy.wait_recv()
        gain_two = gains[1:2, pl.ds(pl.multiple_of(t * half, half), half)]

        @pl.loop(0, rows // STEP)
        def _(i):
            r = pl.ds(pl.multiple_of(i * STEP, STEP), STEP)
            squares = sq_send[r, 0:1] + sq_recv[r, 0:1]
            scale = lax.rsqrt(squares * (1.0 / width) + EPS)
            scales[1, r, :] = jnp.broadcast_to(scale, (STEP, LANES))
            norm_own[r, :] = (mid_own[r, :] * scale * gain_two).astype(BF)

        norm_src = {
            NORM: norm_own.at[pl.ds(0, half_rows), :], LATE: norm_own.at[pl.ds(half_rows, half_rows), :]
        }
        norm_copies = []
        for item, src in norm_src.items():
            spread(item, src)
            one = x_copy(base_of[item] + z, src, slot(item, z, c))
            one.start()
            norm_copies.append(one)
        norm_keep = pltpu.make_async_copy(norm_own, norm_all.at[z, :, pl.ds(t * half, half)], own_sem.at[6])
        norm_keep.start()
        moved = (
            (q_pad, q_hbm), (kv_all, kv_hbm), (attn, attn_hbm), (mid_own, mid_hbm), (normed_one, normed_hbm),
            (tok_all, tok_hbm),
        )
        moves = [
            pltpu.make_async_copy(src, dst, act_sem.at[3 + 5 * planes + i]) for i, (src, dst) in enumerate(moved)
        ]
        for one in moves:
            one.start()
        share_units(GATE)
        share_units(UP)
        step(COT, last - 1)
        for item in (GATE, UP):
            for p in order:
                share_on(item, p)
        share_units(DOWN)
        for i in range(last - 1):
            step(NORM, i)
            step(LATE, i)
        for p in order:
            share_on(DOWN, p)
        for item in items:
            for s in range(1, planes):
                shared(item, lax.rem(z + s, planes))
        for one in own_copies[1:]:
            one.wait()
        norm_keep.wait()
        unit_keeps = [
            pltpu.make_async_copy(src, dst, act_sem.at[i])
            for i, (src, dst) in enumerate(((gate_w, gate_hbm), (up_w, up_hbm), (down_w, down_hbm)))
        ]
        for one in unit_keeps:
            one.start()

        def forward_block(p):
            other = pl.ds((1 - t) * half, half)
            for item, there in (
                (COT, cot_all.at[p, :, other]),
                (NORM, norm_all.at[p, pl.ds(0, half_rows), other]),
                (LATE, norm_all.at[p, pl.ds(half_rows, half_rows), other]),
            ):
                base = base_of[item]
                copy(there, there, x_send.at[base + p], x_recv.at[base + p], at_x).wait_recv()

            @pl.loop(0, units // TILE)
            def _(j):
                cols = pl.ds(pl.multiple_of(j * TILE, TILE), TILE)
                gate = jnp.dot(norm_all[p], gate_w[:, cols], preferred_element_type=F32)
                up = jnp.dot(norm_all[p], up_w[:, cols], preferred_element_type=F32)
                grad = dot_t(cot_all[p], down_w[cols, :])
                sig = jax.nn.sigmoid(gate)
                act = gate * sig
                acts[0, p, :, cols] = (act * up).astype(BF)
                acts[1, p, :, cols] = (grad * up * sig * (1.0 + gate * (1.0 - sig))).astype(BF)
                acts[2, p, :, cols] = (grad * act).astype(BF)

            kinds = (
                (acts.at[0, p], hid_hbm), (acts.at[1, p], gate_grad_hbm), (acts.at[2, p], up_grad_hbm),
                (norm_all.at[p], norm_hbm), (cot_all.at[p], cot_hbm),
            )
            found = [
                pltpu.make_async_copy(src, whole.at[p], act_sem.at[3 + i + 5 * len(kept)])
                for i, (src, whole) in enumerate(kinds)
            ]
            for one in found:
                one.start()
            kept.append(found)

        kept = []
        forward_block(z)
        forward_block(order[0])
        step(NORM, last - 1)
        step(LATE, last - 1)
        for p in order[1:]:
            forward_block(p)

        for found in kept:
            for one in found:
                one.wait()
        for one in unit_keeps + moves:
            one.wait()
        for one in [qkv_keep, out_keep]:
            one.wait()
        tok_copy_out = [half_copy, sq_copy, cot_copy] + norm_copies
        for one in gain_copies + sends + kv_sends + tok_copy_out:
            one.wait_send()
        spread_done(QKV, qkv_src)
        spread_done(OUT, out_src)
        spread_done(COT, cot)
        for item, src in norm_src.items():
            spread_done(item, src)
        for p in order:
            for item in (QKV, OUT, COT, NORM, LATE):
                forward_done(item, p)
            for item in (QKV, OUT, GATE, UP, DOWN):
                share_done(item, p)
            for item, base in base_of.items():
                x_copy(base + p, slot(item, p, c), slot(item, p, c)).wait_send()

    hbm = pl.BlockSpec(memory_space=pl.ANY)
    vmem = pl.BlockSpec(memory_space=pltpu.VMEM)
    dma = pltpu.SemaphoreType.DMA
    shape = jax.ShapeDtypeStruct
    return pl.pallas_call(
        kernel,
        name="front",
        out_shape=(
            shape((width, units), BF),
            shape((width, units), BF),
            shape((units, width), BF),
            shape((planes, rows, width), BF),
            shape((planes, rows, width), BF),
            shape((width, qkv_cols), BF),
            shape((query_cols, width), BF),
            shape((planes, rows, units), BF),
            shape((planes, rows, units), BF),
            shape((planes, rows, units), BF),
            shape((8, width), F32),
            shape((heads, rows, LANES), BF),
            shape((contexts, 2 * n_kv, rows, LANES), BF),
            shape((rows, query_cols), BF),
            shape((heads, rows), F32),
            shape((rows, half), F32),
            shape((rows, width), BF),
            shape((rows, width), BF),
            shape((2, rows, LANES), F32),
            shape((rows, LANES), F32),
            shape((rows, LANES), F32),
            shape((8, rows), jnp.int32),
            shape((seq_len, 1), jnp.int32),
        ),
        in_specs=[vmem, hbm, vmem, vmem] + [hbm] * 7 + [pl.BlockSpec(memory_space=pltpu.SMEM), vmem],
        out_specs=(hbm,) * 10 + (vmem, hbm, hbm, hbm, vmem, hbm, hbm, hbm) + (vmem,) * 5,
        scratch_shapes=[
            pltpu.VMEM((heads, rows, LANES), BF),
            pltpu.VMEM((contexts, 2 * n_kv, rows, LANES), BF),
            pltpu.VMEM((rows, query_cols), BF),
            pltpu.VMEM((rows, half), F32),
            pltpu.VMEM((rows, width), BF),
            pltpu.VMEM((rows, width), BF),
            pltpu.VMEM((width, units), BF),
            pltpu.VMEM((width, units), BF),
            pltpu.VMEM((units, width), BF),
            pltpu.VMEM((planes, rows, width), BF),
            pltpu.VMEM((planes, rows, width), BF),
            pltpu.VMEM((3, planes, rows, units), BF),
            pltpu.VMEM((width, qkv_cols), BF),
            pltpu.VMEM((query_cols, width), BF),
            pltpu.VMEM((8, depth), F32),
            pltpu.VMEM((qkv_cols // LANES, rows, LANES), F32),
            pltpu.VMEM((heads, rows, LANES), F32),
            pltpu.VMEM((rows, half), BF),
            pltpu.VMEM((rows, half), BF),
            pltpu.VMEM((rows, half), BF),
            pltpu.VMEM((rows, LANES), F32),
            pltpu.VMEM((rows, LANES), F32),
            dma((9, planes, planes)),
            dma((9, planes)),
            dma((6, planes, max(outers, 2))),
            dma((6, planes, max(outers, 2))),
            dma((6, planes, max(outers, 2))),
            dma((6, planes, max(outers, 2))),
            dma((3 + 3 * planes,)),
            dma((3 + 3 * planes,)),
            dma((9,)),
            dma((9 + 5 * planes,)),
        ],
        compiler_params=pltpu.CompilerParams(
            collective_id=0, has_side_effects=True, vmem_limit_bytes=VMEM_LIMIT
        ),
        cost_estimate=pl.CostEstimate(flops=8 * 10**9, bytes_accessed=80 * 10**6, transcendentals=4 * 10**6),
    )


def add_strips(total, terms, chunk):
    lead, size, _ = total.shape
    steps = size // chunk

    @pl.loop(0, lead * steps)
    def _(i):
        a, r = i // steps, pl.ds(pl.multiple_of(lax.rem(i, steps) * chunk, chunk), chunk)
        found = terms[0][a, r, :].astype(F32)
        for term in terms[1:]:
            found = found + term[a, r, :].astype(F32)
        total[a, r, :] = found.astype(BF)


class Ring:
    def __init__(self, planes, contexts):
        self.planes, self.outers = planes, contexts // 2
        self.z = z = lax.axis_index("fsdp")
        self.c = c = lax.axis_index("context")
        self.t = t = lax.axis_index("tensor")
        self.o, self.k = c // 2, c % 2
        self.at_k = (z, self.o * 2 + 1 - self.k, t)
        self.at_x = (z, c, 1 - t)

    def at_z(self, p):
        return (p, self.c, self.t)

    def at_o(self, other):
        return (self.z, other * 2 + self.k, self.t)

    def after(self, by):
        return lax.rem(self.o + by, self.outers)

    def before(self, by):
        return lax.rem(self.o - by + self.outers, self.outers)

    def plane(self, by):
        return lax.rem(self.z + by, self.planes)

    def greet(self):
        barrier = pltpu.get_barrier_semaphore()
        peers = [self.at_z(self.plane(s)) for s in range(1, self.planes)]
        peers += [self.at_o(self.after(s)) for s in range(1, self.outers)] + [self.at_k, self.at_x]
        for peer in peers:
            pl.semaphore_signal(barrier, inc=1, device_id=peer, device_id_type=MESH)
        pl.semaphore_wait(barrier, len(peers))

    def by_distance(self):
        order = []
        for i in range(self.planes - 1):
            p = jnp.int32(0)
            for plane in range(self.planes):
                far = sorted((abs(q - plane), q) for q in range(self.planes) if q != plane)
                p = p + jnp.where(self.z == plane, far[i][1], 0)
            order.append(p)
        return order


def copy_to(src, dst, send_sem, recv_sem, device):
    return pltpu.make_async_remote_copy(
        src_ref=src, dst_ref=dst, send_sem=send_sem, recv_sem=recv_sem, device_id=device, device_id_type=MESH
    )


class Reduction:
    def __init__(self, ring, item, part, core_in, outer_out, outer_in, strip_sum, sems):
        self.ring, self.item, self.part = ring, item, part
        self.core_in, self.outer_out, self.outer_in, self.strip_sum = core_in, outer_out, outer_in, strip_sum
        self.k_send, self.k_recv, self.y_send, self.y_recv = sems
        self.chunk = 32 if strip_sum.shape[2] > 1024 else 64
        self.chunk = min(self.chunk, strip_sum.shape[1])

    def core_copy(self, other):
        g = self.ring
        return copy_to(
            self.part.at[:, other * 2 + 1 - g.k], self.core_in.at[other],
            self.k_send.at[self.item, other], self.k_recv.at[self.item, other], g.at_k,
        )

    def to_core(self):
        for other in range(self.ring.outers):
            self.core_copy(other).start()

    def outer_copy(self, by):
        g = self.ring
        return copy_to(
            self.outer_out.at[by - 1], self.outer_in.at[by - 1],
            self.y_send.at[self.item, by], self.y_recv.at[self.item, by], g.at_o(g.after(by)),
        )

    def from_core(self):
        g = self.ring
        for other in range(g.outers):
            self.core_copy(other).wait_recv()
        for by in range(1, g.outers):
            goal = g.after(by)
            add_strips(
                self.outer_out.at[by - 1], [self.part.at[:, goal * 2 + g.k], self.core_in.at[goal]], self.chunk
            )
            self.outer_copy(by).start()
        add_strips(self.strip_sum, [self.part.at[:, g.c], self.core_in.at[g.o]], self.chunk)

    def core_done(self):
        for other in range(self.ring.outers):
            self.core_copy(other).wait_send()

    def from_outer(self):
        for by in range(1, self.ring.outers):
            self.outer_copy(by).wait_recv()
        terms = [self.strip_sum] + [self.outer_in.at[by - 1] for by in range(1, self.ring.outers)]
        if len(terms) > 1:
            add_strips(self.strip_sum, terms, self.chunk)

    def outer_done(self):
        for by in range(1, self.ring.outers):
            self.outer_copy(by).wait_send()


class Share:
    def __init__(self, ring, item, slot, sems, source=None):
        self.ring, self.item, self.slot = ring, item, slot
        self.source = slot(ring.c) if source is None else source
        self.y_send, self.y_recv, self.k_send, self.k_recv = sems

    def outer_copy(self, by):
        g = self.ring
        return copy_to(
            self.source, self.slot(g.c), self.y_send.at[self.item, by], self.y_recv.at[self.item, by],
            g.at_o(g.after(by)),
        )

    def core_copy(self, by):
        g = self.ring
        there = self.slot(g.before(by) * 2 + g.k)
        return copy_to(
            self.source if by == 0 else there, there, self.k_send.at[self.item, by], self.k_recv.at[self.item, by],
            g.at_k,
        )

    def start(self):
        for by in range(1, self.ring.outers):
            self.outer_copy(by).start()
        self.core_copy(0).start()

    def pass_on(self):
        g = self.ring
        for by in range(1, g.outers):
            there = self.slot(g.before(by) * 2 + g.k)
            copy_to(there, there, self.y_send.at[self.item, by], self.y_recv.at[self.item, by], g.at_k).wait_recv()
            self.core_copy(by).start()

    def finish(self):
        g = self.ring
        for by in range(g.outers):
            there = self.slot(g.before(by) * 2 + 1 - g.k)
            copy_to(there, there, self.k_send.at[self.item, by], self.k_recv.at[self.item, by], g.at_k).wait_recv()
        for by in range(1, g.outers):
            self.outer_copy(by).wait_send()
        for by in range(g.outers):
            self.core_copy(by).wait_send()


def rotate_tile(u, cosine, sine, first):
    partner = jnp.where(
        first, pltpu.roll(u, LANES - HEAD_WIDTH // 2, 1), pltpu.roll(u, HEAD_WIDTH // 2, 1)
    )
    return u * cosine + partner * sine


def store_part(part, i, tile):
    size, taken = part.shape[2], tile.shape[0]
    per = part.shape[1] * size // taken
    for r in range(taken // size):
        part[i // per, lax.rem(i, per) * (taken // size) + r] = tile[r * size : (r + 1) * size].astype(BF)


def build_back(planes, contexts, rows, width, query_cols, kv_cols, units):
    outers = contexts // 2
    half = width // 2
    depth = width // planes
    strip = depth // contexts
    unit_strip = units // contexts
    seq_len = rows * contexts
    n_q, n_kv = query_cols // LANES, kv_cols // LANES
    heads = query_cols // HEAD_WIDTH
    group = query_cols // kv_cols
    qkv_cols = query_cols + 2 * kv_cols
    DOWN, GATE, UP, KV = range(4)
    lots = max(outers - 1, 1)

    def kernel(
        gate_hbm, up_hbm, down_hbm, norm_hbm, cot_hbm, hid_hbm, gate_grad_hbm, up_grad_hbm, qkv_hbm, out_hbm, q_hbm, kv_hbm, mid_hbm, tok_hbm,
        gains, cosine, sine, pos_q, pos_k, log_sum, scales,
        input_grad, gate_strip, up_strip, down_out, mid_full, qkv_grad, gain_rows, mlp_part,
        norm_x_in, norm_z_in, norm_x_out, norm_sum, mlp_stage, hid, down_w,
        row_core_in, col_core_in, row_outer_in, col_outer_in, row_outer_out, col_outer_out, row_sum, col_sum,
        kv_core_in, kv_outer_in, sq_out, sq_in, first_x_out, first_x_in,
        x_send, x_recv, z_send, z_recv, k_send, k_recv, y_send, y_recv, grad_send, grad_recv, sy_send, sy_recv, sk_send,
        sk_recv, load_sem, stage_sem, credit,
    ):
        ring = Ring(planes, contexts)
        z, c, t, k, o = ring.z, ring.c, ring.t, ring.k, ring.o
        order = ring.by_distance()
        blocks = order[::-1] + [z]
        ring.greet()
        own_cols = pl.multiple_of(t * half, half)
        other_cols = pl.multiple_of((1 - t) * half, half)
        n_half = half // WIDE

        def x_copy(i, src, dst):
            return copy_to(src, dst, x_send.at[i], x_recv.at[i], ring.at_x)

        NORM, MID, SQ_TWO, FIRST, SQ_ONE = 0, planes, planes + 1, planes + 2, planes + 3

        def norm_x(i):
            return x_copy(NORM + i, norm_x_out.at[i % 2], norm_x_in.at[blocks[i]])

        def back_from(p, here):
            return lax.rem(p - here + planes, planes) - 1

        def norm_z(p):
            return copy_to(
                norm_sum.at[p], norm_z_in.at[back_from(z, p)], z_send.at[0, p], z_recv.at[0, z], ring.at_z(p)
            )

        def norm_z_wait(p):
            there = norm_z_in.at[back_from(p, z)]
            copy_to(there, there, z_send.at[0, p], z_recv.at[0, p], ring.at_k).wait_recv()

        def add_block(total, other, p):
            n = rows // 64

            @pl.loop(0, n)
            def _(i):
                r = pl.ds(pl.multiple_of(i * 64, 64), 64)
                total[p, r, :] = (total[p, r, :].astype(F32) + other[p, r, :].astype(F32)).astype(BF)

        def norm_on(i):
            norm_x(i).wait_recv()
            add_block(norm_sum, norm_x_in, blocks[i])

        sems = (k_send, k_recv, y_send, y_recv)

        def feed_forward(norm, cot, gate_grad, up_grad):
            def load(i, src, dst):
                one = pltpu.make_async_copy(src, dst, load_sem.at[i])
                one.start()
                return one

            def product(part, left, right, size):
                total = planes * rows

                @pl.loop(0, left.shape[2] // size)
                def _(i):
                    cols = pl.ds(pl.multiple_of(i * size, size), size)
                    tile = t_dot(left[:, :, cols].reshape(total, size), right[...].reshape(total, right.shape[2]))
                    store_part(part, i, tile)

            def with_weights(gate_w, up_w, col_part):
                weights = [load(0, gate_hbm, gate_w), load(1, up_hbm, up_w)]
                loads = [
                    (load(2 + 2 * i, gate_grad_hbm.at[p], gate_grad.at[p]), load(3 + 2 * i, up_grad_hbm.at[p], up_grad.at[p]))
                    for i, p in enumerate(blocks)
                ]
                later = [
                    load(2 + 2 * planes, hid_hbm, hid), load(3 + 2 * planes, cot_hbm, cot),
                    load(4 + 2 * planes, norm_hbm, norm), load(5 + 2 * planes, down_hbm, down_w),
                ]
                for one in weights:
                    one.wait()

                def norm_block(i):
                    p = blocks[i]
                    for one in loads[i]:
                        one.wait()

                    def tile_of(at):
                        r = pl.ds(pl.multiple_of(at, WIDE), WIDE)
                        return dot_t(gate_grad[p], gate_w[r, :]) + dot_t(up_grad[p], up_w[r, :])

                    if i > 1:
                        norm_x(i - 2).wait_send()

                    @pl.loop(0, n_half)
                    def _(j):
                        here = pl.ds(pl.multiple_of(j * WIDE, WIDE), WIDE)
                        norm_x_out[i % 2, :, here] = tile_of(other_cols + j * WIDE).astype(BF)

                    norm_x(i).start()

                    @pl.loop(0, n_half)
                    def _(j):
                        here = pl.ds(pl.multiple_of(j * WIDE, WIDE), WIDE)
                        norm_sum[p, :, here] = tile_of(own_cols + j * WIDE).astype(BF)

                    if i > 1:
                        norm_on(i - 2)
                        norm_z(blocks[i - 2]).start()

                down = Reduction(
                    ring, DOWN, col_part, col_core_in, col_outer_out, col_outer_in, col_sum, sems
                )
                for i in range(planes - 2):
                    norm_block(i)
                later[0].wait()
                later[1].wait()
                product(col_part, hid, cot, TILE)
                down.to_core()
                norm_block(planes - 2)
                down.from_core()
                norm_block(planes - 1)
                later[2].wait()
                later[3].wait()
                down.core_done()

            pl.run_scoped(
                with_weights,
                pltpu.VMEM((width, units), BF), pltpu.VMEM((width, units), BF), pltpu.VMEM((1, contexts, unit_strip, width), BF),
            )

            def with_parts(row_part):
                gate = Reduction(
                    ring, GATE, row_part, row_core_in, row_outer_out.at[0], row_outer_in.at[0], row_sum.at[0], sems
                )
                up = Reduction(
                    ring, UP, row_part, row_core_in, row_outer_out.at[1], row_outer_in.at[1], row_sum.at[1], sems
                )
                product(row_part, norm, gate_grad, WIDE)
                gate.to_core()
                norm_on(planes - 2)
                norm_z(blocks[planes - 2]).start()
                gate.from_core()
                gate.core_done()
                pl.semaphore_signal(credit, inc=1, device_id=ring.at_k, device_id_type=MESH)
                product(row_part, norm, up_grad, WIDE)
                pl.semaphore_wait(credit, 1)
                up.to_core()
                norm_on(planes - 1)
                up.from_core()
                up.core_done()

            pl.run_scoped(with_parts, pltpu.VMEM((planes, contexts, strip, units), BF))

        block_bf = pltpu.VMEM((planes, rows, width), BF)
        unit_bf = pltpu.VMEM((planes, rows, units), BF)
        pl.run_scoped(feed_forward, block_bf, block_bf, unit_bf, unit_bf)

        down = Reduction(ring, DOWN, None, None, col_outer_out, col_outer_in, col_sum, sems)
        gate = Reduction(ring, GATE, None, None, row_outer_out.at[0], row_outer_in.at[0], row_sum.at[0], sems)
        up = Reduction(ring, UP, None, None, row_outer_out.at[1], row_outer_in.at[1], row_sum.at[1], sems)

        def strip_src(item, goal):
            if item == DOWN:
                return col_sum.at[0, :, pl.ds(pl.multiple_of(goal * depth, depth), depth)]
            return row_sum.at[0 if item == GATE else 1, goal]

        def strip_dst(item, home):
            if item == DOWN:
                return down_out.at[home, c]
            cols = pl.ds(pl.multiple_of(home * units, units), units)
            return (gate_strip if item == GATE else up_strip).at[:, cols]

        def strip_copy(item, s):
            goal = ring.plane(s)
            return copy_to(
                strip_src(item, goal), strip_dst(item, z), grad_send.at[item, s], grad_recv.at[item, z], ring.at_z(goal)
            )

        def strip_keep(item):
            return pltpu.make_async_copy(strip_src(item, z), strip_dst(item, z), grad_send.at[item, 0])

        def to_planes(item, reduction):
            reduction.from_outer()
            for s in range(1, planes):
                strip_copy(item, s).start()
            strip_keep(item).start()

        def from_planes(item):
            for s in range(1, planes):
                p = ring.plane(s)
                there = strip_dst(item, p)
                copy_to(there, there, grad_send.at[item, s], grad_recv.at[item, p], ring.at_k).wait_recv()
            strip_keep(item).wait()

        share_sems = (sy_send, sy_recv, sk_send, sk_recv)
        down_share = Share(ring, 0, lambda q: down_out.at[:, q], share_sems)

        def stage_copy(i):
            return pltpu.make_async_copy(mlp_stage.at[i % 2], mlp_part.at[blocks[i]], stage_sem.at[i % 2])

        def attention(out_w, mid_keep, mid_grad, q_pad, kv_all, tok, grad_pad, query_out, key_sum, value_sum, kv_grad, kv_out):
            loads = [
                pltpu.make_async_copy(mid_hbm, mid_grad, load_sem.at[0]),
                pltpu.make_async_copy(tok_hbm.at[:, pl.ds(own_cols, half)], tok, load_sem.at[1]),
                pltpu.make_async_copy(q_hbm, q_pad, load_sem.at[2]),
                pltpu.make_async_copy(kv_hbm, kv_all, load_sem.at[3]),
                pltpu.make_async_copy(cot_hbm.at[z, :, pl.ds(own_cols, half)], first_x_out, load_sem.at[4]),
            ]
            for one in loads:
                one.start()
            out_load = pltpu.make_async_copy(out_hbm, out_w, load_sem.at[5])
            out_load.start()
            for one in loads:
                one.wait()
            key_sum[...] = jnp.zeros_like(key_sum)
            value_sum[...] = jnp.zeros_like(value_sum)
            gain_rows[...] = jnp.zeros_like(gain_rows)

            def norm_back(grad_of, normal_of, finish, row, i):
                gain = gains[row : row + 1, pl.ds(own_cols, half)]

                def chunk(j):
                    return pl.ds(pl.multiple_of(j * STEP, STEP), STEP)

                @pl.loop(0, rows // STEP)
                def _(j):
                    r = chunk(j)
                    grad, normal = grad_of(r), normal_of(r)
                    both = grad * normal
                    gain_rows[row : row + 1, :] += jnp.sum(both, 0, keepdims=True)
                    sq_out[i, r, :] = jnp.broadcast_to(jnp.sum(both * gain, -1, keepdims=True), (STEP, LANES))

                swap = x_copy(SQ_TWO if i == 0 else SQ_ONE, sq_out.at[i], sq_in.at[i])
                swap.start()
                swap.wait()

                @pl.loop(0, rows // STEP)
                def _(j):
                    r = chunk(j)
                    inner = (sq_out[i, r, 0:1] + sq_in[i, r, 0:1]) * (1.0 / width)
                    finish(r, scales[row, r, 0:1] * (grad_of(r) * gain - normal_of(r) * inner))

            for p in order:
                norm_z_wait(p)

            def norm_grad_of(r):
                grad = norm_sum[z, r, :].astype(F32)
                for i in range(planes - 1):
                    grad = grad + norm_z_in[i, r, :].astype(F32)
                return grad

            def mid_finish(r, back):
                found = first_x_out[r, :].astype(F32) + back
                mid_keep[r, :] = found
                mid_full[r, pl.ds(own_cols, half)] = found.astype(BF)

            norm_back(norm_grad_of, lambda r: mid_grad[r, :] * scales[1, r, 0:1], mid_finish, 1, 0)
            mine = mid_full.at[:, pl.ds(own_cols, half)]
            mid_swap = x_copy(MID, mine, mine)
            mid_swap.start()
            for i, p in enumerate(blocks):
                if i > 1:
                    stage_copy(i - 2).wait()

                @pl.loop(0, width // WIDE)
                def _(j):
                    r = pl.ds(pl.multiple_of(j * WIDE, WIDE), WIDE)
                    mlp_stage[i % 2, :, r] = jnp.dot(hid[p], down_w[:, r], preferred_element_type=F32).astype(BF)

                stage_copy(i).start()
            to_planes(DOWN, down)
            mid_swap.wait_recv()
            out_load.wait()

            lane = lax.broadcasted_iota(jnp.int32, (rows, LANES), 1)
            first = lax.rem(lane, HEAD_WIDTH) < HEAD_WIDTH // 2
            low = lane < HEAD_WIDTH

            @pl.loop(0, query_cols // TILE)
            def _(i):
                r = pl.ds(pl.multiple_of(i * TILE, TILE), TILE)
                found = dot_t(mid_full[...], out_w[r, :])
                for half_tile in range(TILE // LANES):
                    j = i * (TILE // LANES) + half_tile
                    u = found[:, half_tile * LANES : (half_tile + 1) * LANES]
                    u = u.astype(BF).astype(F32)
                    side = lax.rem((2 * j) // group, 2)
                    lo = jnp.where(low, u, 0.0)
                    hi = jnp.where(low, 0.0, u)
                    grad_pad[2 * j] = jnp.where(side == 0, lo, pltpu.roll(lo, HEAD_WIDTH, 1)).astype(BF)
                    grad_pad[2 * j + 1] = jnp.where(side == 1, hi, pltpu.roll(hi, HEAD_WIDTH, 1)).astype(BF)

            for i in range(max(planes - 2, 0), planes):
                stage_copy(i).wait()

            def attend_back(first_head, last_head):
                @pl.loop(first_head, last_head)
                def _(h):
                    pair = h // (2 * group)
                    keys = kv_all[:, pair].reshape(seq_len, LANES)
                    values = kv_all[:, n_kv + pair].reshape(seq_len, LANES)
                    scores = dot_t(keys, q_pad[h])
                    scores = jnp.where(pos_q[0:1, :] >= pos_k[...], scores, NEG)
                    weights = jnp.exp(scores - log_sum[pl.ds(h, 1), :])
                    weight_grad = dot_t(values, grad_pad[h])
                    inner = jnp.sum(weights * weight_grad, 0, keepdims=True)
                    score_grad = (weights * (weight_grad - inner)).astype(BF)
                    value_sum[pair] += jnp.dot(weights.astype(BF), grad_pad[h], preferred_element_type=F32)
                    key_sum[pair] += jnp.dot(score_grad, q_pad[h], preferred_element_type=F32)
                    query_out[h] = t_dot(keys, score_grad).T

            attend_back(0, heads // 2)
            to_planes(GATE, gate)
            attend_back(heads // 2, heads)
            for i in range(n_kv):
                kv_grad[:, i] = key_sum[i].astype(BF).reshape(contexts, rows, LANES)
                kv_grad[:, n_kv + i] = value_sum[i].astype(BF).reshape(contexts, rows, LANES)

            first_swap = x_copy(FIRST, first_x_out, first_x_in)

            def with_qkv(qkv_w, own):
                qkv_load = pltpu.make_async_copy(qkv_hbm, qkv_w, load_sem.at[0])
                qkv_load.start()

                def kv_core(other):
                    return copy_to(
                        kv_grad.at[other * 2 + 1 - k], kv_core_in.at[other], k_send.at[KV, other], k_recv.at[KV, other],
                        ring.at_k,
                    )

                def kv_outer(by):
                    return copy_to(
                        kv_out.at[by - 1], kv_outer_in.at[by - 1], y_send.at[KV, by], y_recv.at[KV, by],
                        ring.at_o(ring.after(by)),
                    )

                for other in range(outers):
                    kv_core(other).start()
                for j in range(n_q):
                    side = (2 * j) // group % 2
                    lo, hi = query_out[2 * j], query_out[2 * j + 1]
                    if side == 0:
                        hi = pltpu.roll(hi, HEAD_WIDTH, 1)
                    else:
                        lo = pltpu.roll(lo, HEAD_WIDTH, 1)
                    u = jnp.where(low, lo, hi) * FACTOR
                    qkv_grad[:, j * LANES : (j + 1) * LANES] = rotate_tile(u, cosine[...], -sine[...], first).astype(BF)
                for other in range(outers):
                    kv_core(other).wait_recv()
                for by in range(1, outers):
                    goal = ring.after(by)
                    kv_out[by - 1] = (
                        kv_grad[goal * 2 + k].astype(F32) + kv_core_in[goal].astype(F32)
                    ).astype(BF)
                    kv_outer(by).start()
                to_planes(UP, up)
                from_planes(DOWN)
                down_share.start()
                kv_sum = kv_grad[c].astype(F32) + kv_core_in[o].astype(F32)
                for by in range(1, outers):
                    kv_outer(by).wait_recv()
                    kv_sum = kv_sum + kv_outer_in[by - 1].astype(F32)
                for i in range(n_kv):
                    at = query_cols + i * LANES
                    qkv_grad[:, at : at + LANES] = rotate_tile(kv_sum[i], cosine[...], -sine[...], first).astype(BF)
                    qkv_grad[:, at + kv_cols : at + kv_cols + LANES] = kv_sum[n_kv + i].astype(BF)
                for other in range(outers):
                    kv_core(other).wait_send()
                for by in range(1, outers):
                    kv_outer(by).wait_send()

                qkv_load.wait()

                def tile_of(at):
                    return dot_t(qkv_grad[...], qkv_w[pl.ds(pl.multiple_of(at, WIDE), WIDE), :])

                @pl.loop(0, n_half)
                def _(j):
                    here = pl.ds(pl.multiple_of(j * WIDE, WIDE), WIDE)
                    first_x_out[:, here] = tile_of(other_cols + j * WIDE).astype(BF)

                first_swap.start()

                @pl.loop(0, n_half)
                def _(j):
                    here = pl.ds(pl.multiple_of(j * WIDE, WIDE), WIDE)
                    own[:, here] = tile_of(own_cols + j * WIDE)

                first_swap.wait()

                def input_finish(r, back):
                    input_grad[r, :] = (mid_keep[r, :] + back).astype(BF)

                norm_back(
                    lambda r: own[r, :] + first_x_in[r, :].astype(F32),
                    lambda r: tok[r, :].astype(F32) * scales[0, r, 0:1],
                    input_finish, 0, 1,
                )

            pl.run_scoped(with_qkv, pltpu.VMEM((width, qkv_cols), BF), pltpu.VMEM((rows, half), F32))
            mid_swap.wait_send()

        tile_f32 = pltpu.VMEM((rows, half), F32)
        pl.run_scoped(
            attention,
            pltpu.VMEM((query_cols, width), BF),
            tile_f32,
            tile_f32,
            pltpu.VMEM((heads, rows, LANES), BF),
            pltpu.VMEM((contexts, 2 * n_kv, rows, LANES), BF),
            pltpu.VMEM((rows, half), BF),
            pltpu.VMEM((heads, rows, LANES), BF),
            pltpu.VMEM((heads, rows, LANES), F32),
            pltpu.VMEM((n_kv, seq_len, LANES), F32),
            pltpu.VMEM((n_kv, seq_len, LANES), F32),
            pltpu.VMEM((contexts, 2 * n_kv, rows, LANES), BF),
            pltpu.VMEM((lots, 2 * n_kv, rows, LANES), BF),
        )

        down_share.pass_on()
        from_planes(GATE)
        from_planes(UP)
        down_share.finish()
        for item in (DOWN, GATE, UP):
            for s in range(1, planes):
                strip_copy(item, s).wait_send()
        for reduction in (down, gate, up):
            reduction.outer_done()
        for i in range(max(planes - 2, 0), planes):
            norm_x(i).wait_send()
        for p in order:
            norm_z(p).wait_send()

    hbm = pl.BlockSpec(memory_space=pl.ANY)
    vmem = pl.BlockSpec(memory_space=pltpu.VMEM)
    dma = pltpu.SemaphoreType.DMA
    shape = jax.ShapeDtypeStruct
    acts = pltpu.VMEM((planes, rows, half), BF)
    arrivals = pltpu.VMEM((planes - 1, rows, half), BF)
    unit_acts = pltpu.VMEM((planes, rows, units), BF)
    return pl.pallas_call(
        kernel,
        name="back",
        out_shape=(
            shape((rows, half), BF),
            shape((strip, planes * units), BF),
            shape((strip, planes * units), BF),
            shape((planes, contexts, unit_strip, depth), BF),
            shape((rows, width), BF),
            shape((rows, qkv_cols), BF),
            shape((8, half), F32),
            shape((planes, rows, width), BF),
        ),
        in_specs=[hbm] * 14 + [vmem] * 7,
        out_specs=(vmem, hbm, hbm, hbm, vmem, vmem, vmem, hbm),
        scratch_shapes=[acts, arrivals, pltpu.VMEM((2, rows, half), BF), acts, pltpu.VMEM((2, rows, width), BF), unit_acts, pltpu.VMEM((units, width), BF)]
        + [
            pltpu.VMEM((outers, planes, strip, units), BF),
            pltpu.VMEM((outers, 1, unit_strip, width), BF),
            pltpu.VMEM((2, lots, planes, strip, units), BF),
            pltpu.VMEM((lots, 1, unit_strip, width), BF),
            pltpu.VMEM((2, lots, planes, strip, units), BF),
            pltpu.VMEM((lots, 1, unit_strip, width), BF),
            pltpu.VMEM((2, planes, strip, units), BF),
            pltpu.VMEM((1, unit_strip, width), BF),
            pltpu.VMEM((outers, 2 * n_kv, rows, LANES), BF),
            pltpu.VMEM((lots, 2 * n_kv, rows, LANES), BF),
            pltpu.VMEM((2, rows, LANES), F32),
            pltpu.VMEM((2, rows, LANES), F32),
            pltpu.VMEM((rows, half), BF),
            pltpu.VMEM((rows, half), BF),
            dma((planes + 4,)),
            dma((planes + 4,)),
            dma((1, planes)),
            dma((1, planes)),
            dma((4, outers)),
            dma((4, outers)),
            dma((4, max(outers, 2))),
            dma((4, max(outers, 2))),
            dma((3, planes)),
            dma((3, planes)),
            dma((2, max(outers, 2))),
            dma((2, max(outers, 2))),
            dma((2, outers)),
            dma((2, outers)),
            dma((2 * planes + 6,)),
            dma((2,)),
            pltpu.SemaphoreType.REGULAR,
        ],
        compiler_params=pltpu.CompilerParams(
            collective_id=1, has_side_effects=True, vmem_limit_bytes=VMEM_LIMIT
        ),
        cost_estimate=pl.CostEstimate(flops=50 * 10**9, bytes_accessed=80 * 10**6, transcendentals=8 * 10**6),
    )


def build_grads(planes, contexts, rows, width, query_cols, kv_cols, units):
    outers = contexts // 2
    half = width // 2
    depth = width // planes
    strip = depth // contexts
    out_strip = query_cols // contexts
    unit_strip = units // contexts
    qkv_cols = query_cols + 2 * kv_cols
    lots = max(outers - 1, 1)
    per_half = planes // 2
    OUT, QKV, UP, GATE = range(4)

    def kernel(
        attn, mid_full, normed_one, qkv_grad, gain_rows, mid_own, gate_strip, up_strip, mlp_part,
        gate_out, up_out, out_out, qkv_out, gain_out, result,
        out_part, qkv_part, out_core, qkv_core, out_outer_out, qkv_outer_out, out_outer_in, qkv_outer_in,
        out_sum, qkv_sum, out_z, qkv_z, gain_z, gain_y, gain_k, gain_now, mlp_x_in, mlp_z_in, mlp_sum,
        k_send, k_recv, y_send, y_recv, z_send, z_recv, sk_send, sk_recv, sy_send, sy_recv, gain_send, gain_recv,
        mx_send, mx_recv, mz_send, mz_recv, own_sem,
    ):
        ring = Ring(planes, contexts)
        z, c, t, k, o = ring.z, ring.c, ring.t, ring.k, ring.o
        order = ring.by_distance()
        ring.greet()

        def rows_of(whole, size):
            return lambda q: whole.at[pl.ds(pl.multiple_of(q * size, size), size), :]

        share_sems = (sy_send, sy_recv, sk_send, sk_recv)
        up_share = Share(ring, UP, rows_of(up_out, strip), share_sems, up_strip)
        out_share = Share(ring, OUT, rows_of(out_out, out_strip), share_sems)
        qkv_share = Share(ring, QKV, rows_of(qkv_out, strip), share_sems)
        gate_share = Share(ring, GATE, rows_of(gate_out, strip), share_sems, gate_strip)
        gate_share.start()
        keeps = [
            pltpu.make_async_copy(gate_strip, rows_of(gate_out, strip)(c), own_sem.at[0]),
            pltpu.make_async_copy(up_strip, rows_of(up_out, strip)(c), own_sem.at[2]),
        ]
        for one in keeps:
            one.start()

        own_cols = pl.multiple_of(t * half, half)
        other_cols = pl.multiple_of((1 - t) * half, half)
        blocks = order[::-1] + [z]

        def mlp_x(p):
            return copy_to(
                mlp_part.at[p, :, pl.ds(other_cols, half)], mlp_x_in.at[p], mx_send.at[p], mx_recv.at[p], ring.at_x
            )

        def mlp_z(p):
            return copy_to(
                mlp_sum.at[p], mlp_z_in.at[lax.rem(z - p + planes, planes) - 1], mz_send.at[p], mz_recv.at[z],
                ring.at_z(p),
            )

        mlp_load = pltpu.make_async_copy(mlp_part.at[:, :, pl.ds(own_cols, half)], mlp_sum, own_sem.at[1])
        for p in blocks:
            mlp_x(p).start()
        mlp_load.start()

        def mlp_on(p):
            mlp_x(p).wait_recv()

            @pl.loop(0, rows // 64)
            def _(i):
                r = pl.ds(pl.multiple_of(i * 64, 64), 64)
                mlp_sum[p, r, :] = (mlp_sum[p, r, :].astype(F32) + mlp_x_in[p, r, :].astype(F32)).astype(BF)

        takes_part = z // per_half == t

        def gain_plane(j):
            return t * per_half + j

        def gain_copy(j):
            return copy_to(
                gain_rows.at[:, pl.ds(j * depth, depth)], gain_z.at[z], gain_send.at[j], gain_recv.at[z],
                ring.at_z(gain_plane(j)),
            )

        for j in range(per_half):

            @pl.when(gain_plane(j) != z)
            def _(j=j):
                gain_copy(j).start()

        gain_x = copy_to(
            gain_out, gain_out, gain_send.at[per_half], gain_recv.at[planes], ring.at_x
        )

        def gain_outer(by):
            return copy_to(
                gain_now.at[0], gain_y.at[by - 1], gain_send.at[per_half + by], gain_recv.at[planes + by],
                ring.at_o(ring.after(by)),
            )

        gain_core = copy_to(
            gain_now.at[1], gain_k, gain_send.at[per_half + outers], gain_recv.at[planes + outers], ring.at_k
        )

        def product(part, left, right):
            @pl.loop(0, left.shape[1] // TILE)
            def _(i):
                cols = pl.ds(pl.multiple_of(i * TILE, TILE), TILE)
                store_part(part, i, t_dot(left[:, cols], right[...]))

        sems = (k_send, k_recv, y_send, y_recv)
        out = Reduction(ring, 0, out_part, out_core, out_outer_out, out_outer_in, out_sum, sems)
        qkv = Reduction(ring, 1, qkv_part, qkv_core, qkv_outer_out, qkv_outer_in, qkv_sum, sems)
        product(qkv_part, normed_one, qkv_grad)
        qkv.to_core()
        product(out_part, attn, mid_full)
        qkv.from_core()
        out.to_core()

        @pl.when(takes_part)
        def _():
            mine = lax.rem(z, per_half) * depth
            total = gain_rows[:, pl.ds(pl.multiple_of(mine, depth), depth)]
            for s in range(1, planes):
                p = ring.plane(s)
                copy_to(gain_z.at[p], gain_z.at[p], gain_send.at[0], gain_recv.at[p], ring.at_k).wait_recv()
                total = total + gain_z[p]
            gain_now[0] = total
            for by in range(1, outers):
                gain_outer(by).start()

        out.from_core()
        mlp_load.wait()
        for p in blocks[:-1]:
            mlp_on(p)
            mlp_z(p).start()

        @pl.when(takes_part)
        def _():
            total = gain_now[0]
            for by in range(1, outers):
                gain_outer(by).wait()
                total = total + gain_y[by - 1]
            gain_now[1] = total
            gain_core.start()

        def piece(item, p):
            if item == OUT:
                return out_sum.at[0, :, pl.ds(pl.multiple_of(p * depth, depth), depth)]
            return qkv_sum.at[p]

        def landing(item, p):
            return (out_z if item == OUT else qkv_z).at[p]

        def z_copy(item, s):
            p = ring.plane(s)
            return copy_to(
                piece(item, p), landing(item, z), z_send.at[item, s], z_recv.at[item, z], ring.at_z(p)
            )

        def to_planes(item, reduction):
            reduction.from_outer()
            for s in range(1, planes):
                z_copy(item, s).start()

        def from_planes(item):
            for p in order:
                there = landing(item, p)
                copy_to(there, there, z_send.at[item, 0], z_recv.at[item, p], ring.at_k).wait_recv()
            size = out_strip if item == OUT else strip
            whole = out_out if item == OUT else qkv_out
            total = piece(item, z)[...].astype(F32)
            for p in order:
                total = total + landing(item, p)[...].astype(F32)
            whole[pl.ds(pl.multiple_of(c * size, size), size), :] = total.astype(BF)
            (out_share if item == OUT else qkv_share).start()

        to_planes(QKV, qkv)

        @pl.when(takes_part)
        def _():
            gain_core.wait()
            gain_out[...] = gain_now[1] + gain_k[...]
            gain_x.start()

        to_planes(OUT, out)
        up_share.start()
        from_planes(QKV)
        mlp_on(z)
        from_planes(OUT)
        total = mid_own[...] + mlp_sum[z].astype(F32)
        for p in order:
            there = mlp_z_in.at[lax.rem(p - z + planes, planes) - 1]
            copy_to(there, there, mz_send.at[p], mz_recv.at[p], ring.at_k).wait_recv()
            total = total + there[...].astype(F32)
        result[...] = total.astype(BF)
        for one in (gate_share, up_share, qkv_share, out_share):
            one.pass_on()
        for one in keeps:
            one.wait()
        for one in (gate_share, up_share, qkv_share, out_share):
            one.finish()
        for p in blocks:
            mlp_x(p).wait_send()
        for p in order:
            mlp_z(p).wait_send()
        for reduction in (out, qkv):
            reduction.core_done()
            reduction.outer_done()
        for item in (OUT, QKV):
            for s in range(1, planes):
                z_copy(item, s).wait_send()
        for j in range(per_half):

            @pl.when(gain_plane(j) != z)
            def _(j=j):
                gain_copy(j).wait_send()

        @pl.when(takes_part)
        def _():
            gain_x.wait_send()

        @pl.when(jnp.logical_not(takes_part))
        def _():
            gain_x.wait_recv()

    hbm = pl.BlockSpec(memory_space=pl.ANY)
    vmem = pl.BlockSpec(memory_space=pltpu.VMEM)
    dma = pltpu.SemaphoreType.DMA
    shape = jax.ShapeDtypeStruct
    return pl.pallas_call(
        kernel,
        name="grads",
        out_shape=(
            shape((depth, planes * units), BF),
            shape((depth, planes * units), BF),
            shape((query_cols, depth), BF),
            shape((depth, qkv_cols), BF),
            shape((8, depth), F32),
            shape((rows, half), BF),
        ),
        in_specs=[vmem] * 6 + [hbm] * 3,
        out_specs=(hbm, hbm, vmem, vmem, vmem, vmem),
        scratch_shapes=[
            pltpu.VMEM((1, contexts, out_strip, width), BF),
            pltpu.VMEM((planes, contexts, strip, qkv_cols), BF),
            pltpu.VMEM((outers, 1, out_strip, width), BF),
            pltpu.VMEM((outers, planes, strip, qkv_cols), BF),
            pltpu.VMEM((lots, 1, out_strip, width), BF),
            pltpu.VMEM((lots, planes, strip, qkv_cols), BF),
            pltpu.VMEM((lots, 1, out_strip, width), BF),
            pltpu.VMEM((lots, planes, strip, qkv_cols), BF),
            pltpu.VMEM((1, out_strip, width), BF),
            pltpu.VMEM((planes, strip, qkv_cols), BF),
            pltpu.VMEM((planes, out_strip, depth), BF),
            pltpu.VMEM((planes, strip, qkv_cols), BF),
            pltpu.VMEM((planes, 8, depth), F32),
            pltpu.VMEM((lots, 8, depth), F32),
            pltpu.VMEM((8, depth), F32),
            pltpu.VMEM((2, 8, depth), F32),
            pltpu.VMEM((planes, rows, half), BF),
            pltpu.VMEM((planes - 1, rows, half), BF),
            pltpu.VMEM((planes, rows, half), BF),
            dma((2, outers)),
            dma((2, outers)),
            dma((2, max(outers, 2))),
            dma((2, max(outers, 2))),
            dma((2, planes)),
            dma((2, planes)),
            dma((4, outers)),
            dma((4, outers)),
            dma((4, max(outers, 2))),
            dma((4, max(outers, 2))),
            dma((per_half + outers + 1,)),
            dma((planes + outers + 1,)),
            dma((planes,)),
            dma((planes,)),
            dma((planes,)),
            dma((planes,)),
            dma((3,)),
        ],
        compiler_params=pltpu.CompilerParams(
            collective_id=2, has_side_effects=True, vmem_limit_bytes=VMEM_LIMIT
        ),
        cost_estimate=pl.CostEstimate(flops=4 * 10**9, bytes_accessed=40 * 10**6, transcendentals=0),
    )


def shards(
    tokens,
    span_order,
    attn_gain,
    w_query,
    key_weight,
    value_weight,
    w_out,
    mlp_gain,
    w_gate,
    w_up,
    w_down,
    out_grad,
):
    planes = lax.axis_size("fsdp")
    contexts = lax.axis_size("context")
    tok_own, cot_own = tokens[0], out_grad[0]
    rows, own_cols = tok_own.shape
    width = own_cols * 2
    depth = width // planes
    units = w_gate.shape[1] // planes
    query_cols = w_query.shape[1]
    kv_cols = key_weight.shape[1]
    sizes = (planes, contexts, rows, width, query_cols, kv_cols, units)

    freqs = jnp.tile(rope_freqs(HEAD_WIDTH), LANES // (HEAD_WIDTH // 2))[None]
    (
        gate_w, up_w, down_w, cot_all, norm_all, qkv_w, out_w, hid, gate_grad, up_grad, gains, q_pad, kv_all, attn, log_sum, mid_own,
        normed_one, tok_all, scales, cosine_table, sine_table, pos_q, pos_k,
    ) = build_front(*sizes)(
        tok_own, cot_own, attn_gain[None], mlp_gain[None], w_query, key_weight, value_weight, w_out, w_gate, w_up,
        w_down, span_order, freqs,
    )
    input_grad, gate_strip, up_strip, down_out, mid_full, qkv_grad, gain_rows, mlp_part = build_back(*sizes)(
        gate_w, up_w, down_w, norm_all, cot_all, hid, gate_grad, up_grad, qkv_w, out_w, q_pad, kv_all, mid_own, tok_all, gains,
        cosine_table, sine_table, pos_q, pos_k, log_sum, scales,
    )
    gate_out, up_out, out_out, qkv_out, gain_out, result = build_grads(*sizes)(
        attn, mid_full, normed_one, qkv_grad, gain_rows, mid_own, gate_strip, up_strip, mlp_part
    )
    qkv_out = qkv_out.astype(F32)
    return (
        result[None],
        input_grad[None],
        gain_out[0],
        qkv_out[:, :query_cols],
        qkv_out[:, query_cols : query_cols + kv_cols],
        qkv_out[:, query_cols + kv_cols :],
        out_out.astype(F32),
        gain_out[1],
        gate_out.astype(F32),
        up_out.astype(F32),
        down_out.reshape(planes * units, depth).astype(F32),
    )


def solution(mesh):
    weight = P("fsdp", "tensor")
    turned = P("tensor", "fsdp")
    block = P("fsdp", "context", "tensor")
    gain = P("fsdp")
    return jax.shard_map(
        shards,
        mesh=mesh,
        in_specs=(
            block, P(), gain, weight, weight, weight, turned, gain, weight, weight, turned, block,
        ),
        out_specs=(
            block, block, gain, weight, weight, weight, turned, gain, weight, weight, turned,
        ),
        check_vma=False,
    )
```

```python
import math

import jax
import jax.numpy as jnp
from jax import lax
from jax.experimental import pallas as pl
from jax.experimental.pallas import tpu as pltpu
from jax.sharding import PartitionSpec as P

HEAD_WIDTH = 64
EPS = 1e-05
NEG = -1e30
BF = jnp.bfloat16
F32 = jnp.float32
LANES = 128
TILE = 256
WIDE = 512
STEP = 32
FACTOR = 1.0 / math.sqrt(HEAD_WIDTH)
VMEM_LIMIT = 62 * 2**20
MESH = pl.DeviceIdType.MESH


def rope_freqs(head_size):
    half_size = head_size // 2
    index = jnp.arange(half_size, dtype=jnp.float32)
    base_freq = jnp.exp(-(2.0 * index / head_size) * math.log(500000.0))
    wavelen = 2.0 * math.pi / base_freq
    smooth = (8192.0 / wavelen - 1.0) / 3.0
    blended = (1.0 - smooth) * base_freq / 32.0 + smooth * base_freq
    return jnp.where(
        wavelen > 8192.0, base_freq / 32.0, jnp.where(wavelen < 2048.0, base_freq, blended)
    )


def dot_t(left, right):
    return lax.dot_general(left, right, (((1,), (1,)), ((), ())), preferred_element_type=F32)


def t_dot(left, right):
    return lax.dot_general(left, right, (((0,), (0,)), ((), ())), preferred_element_type=F32)


def build_front(planes, contexts, rows, width, query_cols, kv_cols, units):
    outers = contexts // 2
    half = width // 2
    depth = width // planes
    strip = depth // contexts
    out_strip = query_cols // contexts
    unit_strip = units // contexts
    seq_len = rows * contexts
    n_q, n_kv = query_cols // LANES, kv_cols // LANES
    heads = query_cols // HEAD_WIDTH
    group = query_cols // kv_cols
    qkv_cols = query_cols + 2 * kv_cols
    QKV, OUT, GATE, UP, DOWN, COT, NORM, GAIN, LATE, MORE = range(10)
    half_strip = strip // 2
    half_rows = rows // 2
    base_of = {COT: 1, NORM: 3 + planes, LATE: 3 + 2 * planes}

    def kernel(
        tok, cot, gain_one_own, gain_two_own, query_own, key_own, value_own, out_own, gate_own, up_own, down_own,
        spans, freqs,
        gate_hbm, up_hbm, down_hbm, cot_hbm, norm_hbm, qkv_hbm, out_hbm, hid_hbm, gate_grad_hbm, up_grad_hbm, gains, q_hbm, kv_hbm, attn_hbm,
        log_sum, mid_hbm, normed_hbm, tok_hbm, scales, cosine, sine, pos_q, pos_k,
        q_pad, kv_all, attn, mid_own, normed_one, tok_all,
        gate_w, up_w, down_w, cot_all, norm_all, acts, qkv_w, out_w, gains_own, lin, heads_out, send_half, recv_half, norm_own, sq_send, sq_recv,
        z_send, z_recv, y_send, y_recv, k_send, k_recv, x_send, x_recv, own_sem, act_sem,
    ):
        z = lax.axis_index("fsdp")
        c = lax.axis_index("context")
        t = lax.axis_index("tensor")
        o, k = c // 2, c % 2

        def at_z(p):
            return (p, c, t)

        def at_o(other):
            return (z, other * 2 + k, t)

        at_k = (z, o * 2 + 1 - k, t)
        at_x = (z, c, 1 - t)

        def copy(src, dst, send_sem, recv_sem, device):
            return pltpu.make_async_remote_copy(
                src_ref=src, dst_ref=dst, send_sem=send_sem, recv_sem=recv_sem,
                device_id=device, device_id_type=MESH,
            )

        barrier = pltpu.get_barrier_semaphore()
        peers = [at_z(lax.rem(z + s, planes)) for s in range(1, planes)]
        peers += [at_o(lax.rem(o + s, outers)) for s in range(1, outers)] + [at_k, at_x]
        for peer in peers:
            pl.semaphore_signal(barrier, inc=1, device_id=peer, device_id_type=MESH)
        pl.semaphore_wait(barrier, len(peers))

        order = []
        for i in range(planes - 1):
            p = jnp.int32(0)
            for plane in range(planes):
                far = sorted((abs(q - plane), q) for q in range(planes) if q != plane)
                p = p + jnp.where(z == plane, far[i][1], 0)
            order.append(p)

        def slot(item, p, q):
            if item in (QKV, MORE):
                skip = 0 if item == QKV else half_strip
                return qkv_w.at[pl.ds(p * depth + q * strip + skip, half_strip), :]
            if item == OUT:
                return out_w.at[pl.ds(q * out_strip, out_strip), pl.ds(p * depth, depth)]
            if item == GATE:
                return gate_w.at[pl.ds(p * depth + q * strip, strip), :]
            if item == UP:
                return up_w.at[pl.ds(p * depth + q * strip, strip), :]
            if item == DOWN:
                return down_w.at[pl.ds(q * unit_strip, unit_strip), pl.ds(p * depth, depth)]
            if item == COT:
                return cot_all.at[p, :, pl.ds(t * half, half)]
            return norm_all.at[p, pl.ds(0 if item == NORM else half_rows, half_rows), pl.ds(t * half, half)]

        def z_copy(item, p, src, goal, way):
            return copy(src, slot(item, p, c), z_send.at[item, p, way], z_recv.at[item, p], at_z(goal))

        def z_wait(item, p):
            z_copy(item, p, slot(item, p, c), z, 0).wait_recv()

        def spread(item, src):
            @pl.when(z + 1 < planes)
            def _():
                z_copy(item, z, src, z + 1, 0).start()

            @pl.when(z > 0)
            def _():
                z_copy(item, z, src, z - 1, 1).start()

        def spread_done(item, src):
            @pl.when(z + 1 < planes)
            def _():
                z_copy(item, z, src, z + 1, 0).wait_send()

            @pl.when(z > 0)
            def _():
                z_copy(item, z, src, z - 1, 1).wait_send()

        def passes_on(p):
            return ((p < z) & (z + 1 < planes)) | ((p > z) & (z > 0))

        def onward(p):
            return jnp.where(p < z, z + 1, z - 1)

        def forward(item, p):
            @pl.when(passes_on(p))
            def _():
                z_copy(item, p, slot(item, p, c), onward(p), 0).start()

        def forward_done(item, p):
            @pl.when(passes_on(p))
            def _():
                z_copy(item, p, slot(item, p, c), onward(p), 0).wait_send()

        def y_copy(item, p, by):
            here = slot(item, p, c)
            return copy(here, here, y_send.at[item, p, by], y_recv.at[item, p, by], at_o(lax.rem(o + by, outers)))

        def y_wait(item, p, by):
            there = slot(item, p, lax.rem(o - by + outers, outers) * 2 + k)
            copy(there, there, y_send.at[item, p, by], y_recv.at[item, p, by], at_k).wait_recv()

        def k_copy(item, p, by):
            here = slot(item, p, lax.rem(o - by + outers, outers) * 2 + k)
            return copy(here, here, k_send.at[item, p, by], k_recv.at[item, p, by], at_k)

        def k_wait(item, p, by):
            there = slot(item, p, lax.rem(o - by + outers, outers) * 2 + 1 - k)
            copy(there, there, k_send.at[item, p, by], k_recv.at[item, p, by], at_k).wait_recv()

        def share(item, p):
            for by in range(1, outers):
                y_copy(item, p, by).start()
            k_copy(item, p, 0).start()

        def share_on(item, p):
            for by in range(1, outers):
                y_wait(item, p, by)
                k_copy(item, p, by).start()

        def shared(item, p):
            for by in range(outers):
                k_wait(item, p, by)

        def share_done(item, p):
            for by in range(1, outers):
                y_copy(item, p, by).wait_send()
            for by in range(outers):
                k_copy(item, p, by).wait_send()

        def x_copy(i, src, dst):
            return copy(src, dst, x_send.at[i], x_recv.at[i], at_x)

        gains_own[...] = jnp.zeros_like(gains_own)
        gains_own[0:1, :] = gain_one_own[...].astype(F32)
        gains_own[1:2, :] = gain_two_own[...].astype(F32)
        tok_cols = pl.ds(t * half, half)
        tok_copy = x_copy(0, tok, tok_all.at[:, tok_cols])
        tok_copy.start()
        gain_copies = [
            copy(
                gains_own, gains.at[:, pl.ds(z * depth, depth)], z_send.at[GAIN, lax.rem(z + s, planes), 0],
                z_recv.at[GAIN, z], at_z(lax.rem(z + s, planes)),
            )
            for s in range(1, planes)
        ]
        for one in gain_copies:
            one.start()
        home = pl.ds(z * depth, depth)
        own_qkv = [
            pltpu.make_async_copy(query_own, qkv_w.at[home, pl.ds(0, query_cols)], own_sem.at[0]),
            pltpu.make_async_copy(key_own, qkv_w.at[home, pl.ds(query_cols, kv_cols)], own_sem.at[7]),
            pltpu.make_async_copy(value_own, qkv_w.at[home, pl.ds(query_cols + kv_cols, kv_cols)], own_sem.at[8]),
        ]
        for one in own_qkv:
            one.start()
        for one in own_qkv:
            one.wait()
        out_src = out_own.at[pl.ds(c * out_strip, out_strip), :]
        for item in (QKV, MORE):
            spread(item, slot(item, z, c))
        own_copies = [
            pltpu.make_async_copy(out_own, out_w.at[:, pl.ds(z * depth, depth)], own_sem.at[1]),
            pltpu.make_async_copy(
                gate_own.at[:, pl.ds(z * units, units)], gate_w.at[pl.ds(z * depth, depth), :], own_sem.at[2]
            ),
            pltpu.make_async_copy(
                up_own.at[:, pl.ds(z * units, units)], up_w.at[pl.ds(z * depth, depth), :], own_sem.at[3]
            ),
            pltpu.make_async_copy(
                down_own.at[pl.ds(z * units, units), :], down_w.at[:, pl.ds(z * depth, depth)], own_sem.at[4]
            ),
            pltpu.make_async_copy(cot, slot(COT, z, c), own_sem.at[5]),
        ]
        for one in own_copies:
            one.start()
        gains[:, pl.ds(z * depth, depth)] = gains_own[...]
        tok_all[:, tok_cols] = tok[...]

        def at_distance(i, act):
            lower, upper = z - (i + 1), z + (i + 1)
            inner = z < planes // 2
            for p in (jnp.where(inner, upper, lower), jnp.where(inner, lower, upper)):

                @pl.when((p >= 0) & (p < planes))
                def _(p=p):
                    act(p)

        def qkv_step(i):
            for item in (QKV, MORE):

                def act(p, item=item):
                    z_wait(item, p)
                    forward(item, p)
                    share(item, p)

                at_distance(i, act)

        qkv_step(0)

        def positions(q, shape, axis):
            r = lax.broadcasted_iota(jnp.int32, shape, axis)
            return jnp.where(r < rows // 2, spans[q, 0], spans[q, 1]) * (rows // 2) + lax.rem(r, rows // 2)

        for q in range(contexts):
            pos_k[q * rows : (q + 1) * rows, :] = positions(q, (rows, 1), 0)
        pos_q[...] = positions(c, (8, rows), 1)
        side_of = lax.rem(lax.broadcasted_iota(jnp.int32, (rows, LANES), 1), HEAD_WIDTH) < HEAD_WIDTH // 2
        angle = positions(c, (rows, LANES), 0).astype(F32) * freqs[...]
        cosine[...] = jnp.cos(angle)
        turned = jnp.sin(angle)
        sine[...] = jnp.where(side_of, -turned, turned)
        qkv_step(1)

        tok_copy.wait()
        for s in range(1, planes):
            p = lax.rem(z + s, planes)
            there = gains.at[:, pl.ds(p * depth, depth)]
            copy(there, there, z_send.at[GAIN, p, 0], z_recv.at[GAIN, p], at_k).wait_recv()

        @pl.loop(0, rows // STEP)
        def _(i):
            r = pl.ds(pl.multiple_of(i * STEP, STEP), STEP)
            x = tok_all[r, :].astype(F32)
            scale = lax.rsqrt(jnp.mean(x * x, -1, keepdims=True) + EPS)
            scales[0, r, :] = jnp.broadcast_to(scale, (STEP, LANES))
            normed_one[r, :] = (x * scale * gains[0:1, :]).astype(BF)

        for i in range(2, planes - 1):
            qkv_step(i)

        spread(OUT, out_src)
        sends = []

        def send_units(item):
            for i, goal in enumerate(order):
                if item == DOWN:
                    src = down_own.at[pl.ds(goal * units + c * unit_strip, unit_strip), :]
                else:
                    own = gate_own if item == GATE else up_own
                    src = own.at[pl.ds(c * strip, strip), pl.ds(goal * units, units)]
                one = z_copy(item, z, src, goal, i)
                one.start()
                sends.append(one)

        def share_units(item):
            for p in order:
                z_wait(item, p)
                share(item, p)

        def cross(item, i):
            base = base_of[item]
            at_distance(i, lambda p: x_copy(base + p, slot(item, p, c), slot(item, p, c)).start())

        def step(item, i, crosses=True):
            def act(p):
                z_wait(item, p)
                forward(item, p)
                if item == OUT:
                    share(OUT, p)

            at_distance(i, act)
            if item != OUT and crosses:
                cross(item, i)

        items = (GATE, UP, DOWN)
        last = planes - 1
        step(OUT, 0)
        spread(COT, cot)
        cot_copy = x_copy(1 + z, cot, slot(COT, z, c))
        cot_copy.start()
        for p in order:
            for item in (QKV, MORE):
                share_on(item, p)
        for p in order:
            for item in (QKV, MORE):
                shared(item, p)
        qkv_keep = pltpu.make_async_copy(qkv_w, qkv_hbm, own_sem.at[0])
        qkv_keep.start()

        n_tile = 2 * LANES

        @pl.loop(0, qkv_cols // n_tile)
        def _(i):
            cols = pl.ds(pl.multiple_of(i * n_tile, n_tile), n_tile)
            found = jnp.dot(normed_one[...], qkv_w[:, cols], preferred_element_type=F32)
            lin[2 * i] = found[:, :LANES]
            lin[2 * i + 1] = found[:, LANES:]

        lane = lax.broadcasted_iota(jnp.int32, (rows, LANES), 1)
        first = lax.rem(lane, HEAD_WIDTH) < HEAD_WIDTH // 2
        low = lane < HEAD_WIDTH

        def rotated(u):
            partner = jnp.where(
                first, pltpu.roll(u, LANES - HEAD_WIDTH // 2, 1), pltpu.roll(u, HEAD_WIDTH // 2, 1)
            )
            return u * cosine[...] + partner * sine[...]

        for i in range(n_kv):
            kv_all[c, i] = rotated(lin[n_q + i]).astype(BF)
            kv_all[c, n_kv + i] = lin[n_q + n_kv + i].astype(BF)

        def kv_slot(q):
            return kv_all.at[q]

        kv_sends = [
            copy(kv_slot(c), kv_slot(c), y_send.at[COT, 0, by], y_recv.at[COT, 0, by], at_o(lax.rem(o + by, outers)))
            for by in range(1, outers)
        ]
        kv_sends.append(copy(kv_slot(c), kv_slot(c), k_send.at[COT, 0, 0], k_recv.at[COT, 0, 0], at_k))
        for one in kv_sends:
            one.start()
        for i in range(1, last - 1):
            step(OUT, i)
        step(COT, 0)
        send_units(GATE)

        @pl.loop(0, n_q)
        def _(j):
            u = rotated(lin[j]).astype(BF).astype(F32) * FACTOR
            side = lax.rem((2 * j) // group, 2)
            lo = jnp.where(low, u, 0.0)
            hi = jnp.where(low, 0.0, u)
            q_pad[2 * j] = jnp.where(side == 0, lo, pltpu.roll(lo, HEAD_WIDTH, 1)).astype(BF)
            q_pad[2 * j + 1] = jnp.where(side == 1, hi, pltpu.roll(hi, HEAD_WIDTH, 1)).astype(BF)

        for by in range(1, outers):
            q = lax.rem(o - by + outers, outers) * 2 + k
            copy(kv_slot(q), kv_slot(q), y_send.at[COT, 0, by], y_recv.at[COT, 0, by], at_k).wait_recv()
            one = copy(kv_slot(q), kv_slot(q), k_send.at[COT, 0, by], k_recv.at[COT, 0, by], at_k)
            one.start()
            kv_sends.append(one)
        for by in range(outers):
            q = lax.rem(o - by + outers, outers) * 2 + 1 - k
            copy(kv_slot(q), kv_slot(q), k_send.at[COT, 0, by], k_recv.at[COT, 0, by], at_k).wait_recv()

        def attend(first_head, last_head):
            @pl.loop(first_head, last_head)
            def _(h):
                pair = h // (2 * group)
                keys = kv_all[:, pair].reshape(seq_len, LANES)
                values = kv_all[:, n_kv + pair].reshape(seq_len, LANES)
                scores = dot_t(keys, q_pad[h])
                scores = jnp.where(pos_q[0:1, :] >= pos_k[...], scores, NEG)
                top = jnp.max(scores, 0, keepdims=True)
                expo = jnp.exp(scores - top)
                total = jnp.sum(expo, 0, keepdims=True)
                weights = (expo * (1.0 / total)).astype(BF)
                heads_out[h] = t_dot(values, weights).T
                log_sum[pl.ds(h, 1), :] = top + jnp.log(total)

        attend(0, heads // 2)
        step(OUT, last - 1)
        for i in range(1, last - 1):
            step(COT, i, False)
        send_units(UP)
        send_units(DOWN)
        for p in order:
            share_on(OUT, p)
        attend(heads // 2, heads)

        for j in range(n_q):
            side = (2 * j) // group % 2
            lo, hi = heads_out[2 * j], heads_out[2 * j + 1]
            if side == 0:
                hi = pltpu.roll(hi, HEAD_WIDTH, 1)
            else:
                lo = pltpu.roll(lo, HEAD_WIDTH, 1)
            attn[:, j * LANES : (j + 1) * LANES] = jnp.where(low, lo, hi).astype(BF)

        for p in order:
            shared(OUT, p)
        own_copies[0].wait()
        out_keep = pltpu.make_async_copy(out_w, out_hbm, own_sem.at[7])
        out_keep.start()

        n_out = half // n_tile

        @pl.loop(0, n_out)
        def _(i):
            cols = pl.ds(pl.multiple_of((1 - t) * half + i * n_tile, n_tile), n_tile)
            here = pl.ds(pl.multiple_of(i * n_tile, n_tile), n_tile)
            send_half[:, here] = jnp.dot(attn[...], out_w[:, cols], preferred_element_type=F32).astype(BF)

        half_copy = x_copy(1 + planes, send_half, recv_half)
        half_copy.start()
        for i in range(1, last - 1):
            cross(COT, i)

        @pl.loop(0, n_out)
        def _(i):
            cols = pl.ds(pl.multiple_of(t * half + i * n_tile, n_tile), n_tile)
            here = pl.ds(pl.multiple_of(i * n_tile, n_tile), n_tile)
            part = jnp.dot(attn[...], out_w[:, cols], preferred_element_type=F32)
            mid_own[:, here] = tok[:, here].astype(F32) + part

        half_copy.wait_recv()

        @pl.loop(0, rows // STEP)
        def _(i):
            r = pl.ds(pl.multiple_of(i * STEP, STEP), STEP)
            mid = mid_own[r, :] + recv_half[r, :].astype(F32)
            mid_own[r, :] = mid
            sq_send[r, :] = jnp.broadcast_to(jnp.sum(mid * mid, -1, keepdims=True), (STEP, LANES))

        sq_copy = x_copy(2 + planes, sq_send, sq_recv)
        sq_copy.start()
        sq_copy.wait_recv()
        gain_two = gains[1:2, pl.ds(pl.multiple_of(t * half, half), half)]

        @pl.loop(0, rows // STEP)
        def _(i):
            r = pl.ds(pl.multiple_of(i * STEP, STEP), STEP)
            squares = sq_send[r, 0:1] + sq_recv[r, 0:1]
            scale = lax.rsqrt(squares * (1.0 / width) + EPS)
            scales[1, r, :] = jnp.broadcast_to(scale, (STEP, LANES))
            norm_own[r, :] = (mid_own[r, :] * scale * gain_two).astype(BF)

        norm_src = {
            NORM: norm_own.at[pl.ds(0, half_rows), :], LATE: norm_own.at[pl.ds(half_rows, half_rows), :]
        }
        norm_copies = []
        for item, src in norm_src.items():
            spread(item, src)
            one = x_copy(base_of[item] + z, src, slot(item, z, c))
            one.start()
            norm_copies.append(one)
        norm_keep = pltpu.make_async_copy(norm_own, norm_all.at[z, :, pl.ds(t * half, half)], own_sem.at[6])
        norm_keep.start()
        moved = (
            (q_pad, q_hbm), (kv_all, kv_hbm), (attn, attn_hbm), (mid_own, mid_hbm), (normed_one, normed_hbm),
            (tok_all, tok_hbm),
        )
        moves = [
            pltpu.make_async_copy(src, dst, act_sem.at[3 + 5 * planes + i]) for i, (src, dst) in enumerate(moved)
        ]
        for one in moves:
            one.start()
        share_units(GATE)
        share_units(UP)
        step(COT, last - 1)
        for item in (GATE, UP):
            for p in order:
                share_on(item, p)
        share_units(DOWN)
        for i in range(last - 1):
            step(NORM, i)
            step(LATE, i)
        for p in order:
            share_on(DOWN, p)
        for item in items:
            for s in range(1, planes):
                shared(item, lax.rem(z + s, planes))
        for one in own_copies[1:]:
            one.wait()
        norm_keep.wait()
        unit_keeps = [
            pltpu.make_async_copy(src, dst, act_sem.at[i])
            for i, (src, dst) in enumerate(((gate_w, gate_hbm), (up_w, up_hbm), (down_w, down_hbm)))
        ]
        for one in unit_keeps:
            one.start()

        def forward_block(p):
            other = pl.ds((1 - t) * half, half)
            for item, there in (
                (COT, cot_all.at[p, :, other]),
                (NORM, norm_all.at[p, pl.ds(0, half_rows), other]),
                (LATE, norm_all.at[p, pl.ds(half_rows, half_rows), other]),
            ):
                base = base_of[item]
                copy(there, there, x_send.at[base + p], x_recv.at[base + p], at_x).wait_recv()

            @pl.loop(0, units // TILE)
            def _(j):
                cols = pl.ds(pl.multiple_of(j * TILE, TILE), TILE)
                gate = jnp.dot(norm_all[p], gate_w[:, cols], preferred_element_type=F32)
                up = jnp.dot(norm_all[p], up_w[:, cols], preferred_element_type=F32)
                grad = dot_t(cot_all[p], down_w[cols, :])
                sig = jax.nn.sigmoid(gate)
                act = gate * sig
                acts[0, p, :, cols] = (act * up).astype(BF)
                acts[1, p, :, cols] = (grad * up * sig * (1.0 + gate * (1.0 - sig))).astype(BF)
                acts[2, p, :, cols] = (grad * act).astype(BF)

            kinds = (
                (acts.at[0, p], hid_hbm), (acts.at[1, p], gate_grad_hbm), (acts.at[2, p], up_grad_hbm),
                (norm_all.at[p], norm_hbm), (cot_all.at[p], cot_hbm),
            )
            found = [
                pltpu.make_async_copy(src, whole.at[p], act_sem.at[3 + i + 5 * len(kept)])
                for i, (src, whole) in enumerate(kinds)
            ]
            for one in found:
                one.start()
            kept.append(found)

        kept = []
        forward_block(z)
        forward_block(order[0])
        step(NORM, last - 1)
        step(LATE, last - 1)
        for p in order[1:]:
            forward_block(p)

        for found in kept:
            for one in found:
                one.wait()
        for one in unit_keeps + moves:
            one.wait()
        for one in [qkv_keep, out_keep]:
            one.wait()
        tok_copy_out = [half_copy, sq_copy, cot_copy] + norm_copies
        for one in gain_copies + sends + kv_sends + tok_copy_out:
            one.wait_send()
        for item in (QKV, MORE):
            spread_done(item, slot(item, z, c))
        spread_done(OUT, out_src)
        spread_done(COT, cot)
        for item, src in norm_src.items():
            spread_done(item, src)
        for p in order:
            for item in (QKV, MORE, OUT, COT, NORM, LATE):
                forward_done(item, p)
            for item in (QKV, MORE, OUT, GATE, UP, DOWN):
                share_done(item, p)
            for item, base in base_of.items():
                x_copy(base + p, slot(item, p, c), slot(item, p, c)).wait_send()

    hbm = pl.BlockSpec(memory_space=pl.ANY)
    vmem = pl.BlockSpec(memory_space=pltpu.VMEM)
    dma = pltpu.SemaphoreType.DMA
    shape = jax.ShapeDtypeStruct
    return pl.pallas_call(
        kernel,
        name="front",
        out_shape=(
            shape((width, units), BF),
            shape((width, units), BF),
            shape((units, width), BF),
            shape((planes, rows, width), BF),
            shape((planes, rows, width), BF),
            shape((width, qkv_cols), BF),
            shape((query_cols, width), BF),
            shape((planes, rows, units), BF),
            shape((planes, rows, units), BF),
            shape((planes, rows, units), BF),
            shape((8, width), F32),
            shape((heads, rows, LANES), BF),
            shape((contexts, 2 * n_kv, rows, LANES), BF),
            shape((rows, query_cols), BF),
            shape((heads, rows), F32),
            shape((rows, half), F32),
            shape((rows, width), BF),
            shape((rows, width), BF),
            shape((2, rows, LANES), F32),
            shape((rows, LANES), F32),
            shape((rows, LANES), F32),
            shape((8, rows), jnp.int32),
            shape((seq_len, 1), jnp.int32),
        ),
        in_specs=[vmem, hbm, vmem, vmem] + [hbm] * 7 + [pl.BlockSpec(memory_space=pltpu.SMEM), vmem],
        out_specs=(hbm,) * 10 + (vmem, hbm, hbm, hbm, vmem, hbm, hbm, hbm) + (vmem,) * 5,
        scratch_shapes=[
            pltpu.VMEM((heads, rows, LANES), BF),
            pltpu.VMEM((contexts, 2 * n_kv, rows, LANES), BF),
            pltpu.VMEM((rows, query_cols), BF),
            pltpu.VMEM((rows, half), F32),
            pltpu.VMEM((rows, width), BF),
            pltpu.VMEM((rows, width), BF),
            pltpu.VMEM((width, units), BF),
            pltpu.VMEM((width, units), BF),
            pltpu.VMEM((units, width), BF),
            pltpu.VMEM((planes, rows, width), BF),
            pltpu.VMEM((planes, rows, width), BF),
            pltpu.VMEM((3, planes, rows, units), BF),
            pltpu.VMEM((width, qkv_cols), BF),
            pltpu.VMEM((query_cols, width), BF),
            pltpu.VMEM((8, depth), F32),
            pltpu.VMEM((qkv_cols // LANES, rows, LANES), F32),
            pltpu.VMEM((heads, rows, LANES), F32),
            pltpu.VMEM((rows, half), BF),
            pltpu.VMEM((rows, half), BF),
            pltpu.VMEM((rows, half), BF),
            pltpu.VMEM((rows, LANES), F32),
            pltpu.VMEM((rows, LANES), F32),
            dma((10, planes, planes)),
            dma((10, planes)),
            dma((10, planes, max(outers, 2))),
            dma((10, planes, max(outers, 2))),
            dma((10, planes, max(outers, 2))),
            dma((10, planes, max(outers, 2))),
            dma((3 + 3 * planes,)),
            dma((3 + 3 * planes,)),
            dma((9,)),
            dma((9 + 5 * planes,)),
        ],
        compiler_params=pltpu.CompilerParams(
            collective_id=0, has_side_effects=True, vmem_limit_bytes=VMEM_LIMIT
        ),
        cost_estimate=pl.CostEstimate(flops=8 * 10**9, bytes_accessed=80 * 10**6, transcendentals=4 * 10**6),
    )


def add_strips(total, terms, chunk):
    lead, size, _ = total.shape
    steps = size // chunk

    @pl.loop(0, lead * steps)
    def _(i):
        a, r = i // steps, pl.ds(pl.multiple_of(lax.rem(i, steps) * chunk, chunk), chunk)
        found = terms[0][a, r, :].astype(F32)
        for term in terms[1:]:
            found = found + term[a, r, :].astype(F32)
        total[a, r, :] = found.astype(BF)


class Ring:
    def __init__(self, planes, contexts):
        self.planes, self.outers = planes, contexts // 2
        self.z = z = lax.axis_index("fsdp")
        self.c = c = lax.axis_index("context")
        self.t = t = lax.axis_index("tensor")
        self.o, self.k = c // 2, c % 2
        self.at_k = (z, self.o * 2 + 1 - self.k, t)
        self.at_x = (z, c, 1 - t)

    def at_z(self, p):
        return (p, self.c, self.t)

    def at_o(self, other):
        return (self.z, other * 2 + self.k, self.t)

    def after(self, by):
        return lax.rem(self.o + by, self.outers)

    def before(self, by):
        return lax.rem(self.o - by + self.outers, self.outers)

    def plane(self, by):
        return lax.rem(self.z + by, self.planes)

    def greet(self):
        barrier = pltpu.get_barrier_semaphore()
        peers = [self.at_z(self.plane(s)) for s in range(1, self.planes)]
        peers += [self.at_o(self.after(s)) for s in range(1, self.outers)] + [self.at_k, self.at_x]
        for peer in peers:
            pl.semaphore_signal(barrier, inc=1, device_id=peer, device_id_type=MESH)
        pl.semaphore_wait(barrier, len(peers))

    def by_distance(self):
        order = []
        for i in range(self.planes - 1):
            p = jnp.int32(0)
            for plane in range(self.planes):
                far = sorted((abs(q - plane), q) for q in range(self.planes) if q != plane)
                p = p + jnp.where(self.z == plane, far[i][1], 0)
            order.append(p)
        return order


def copy_to(src, dst, send_sem, recv_sem, device):
    return pltpu.make_async_remote_copy(
        src_ref=src, dst_ref=dst, send_sem=send_sem, recv_sem=recv_sem, device_id=device, device_id_type=MESH
    )


class Reduction:
    def __init__(self, ring, item, part, core_in, outer_out, outer_in, strip_sum, sems):
        self.ring, self.item, self.part = ring, item, part
        self.core_in, self.outer_out, self.outer_in, self.strip_sum = core_in, outer_out, outer_in, strip_sum
        self.k_send, self.k_recv, self.y_send, self.y_recv = sems
        self.chunk = 32 if strip_sum.shape[2] > 1024 else 64
        self.chunk = min(self.chunk, strip_sum.shape[1])

    def core_copy(self, other):
        g = self.ring
        return copy_to(
            self.part.at[:, other * 2 + 1 - g.k], self.core_in.at[other],
            self.k_send.at[self.item, other], self.k_recv.at[self.item, other], g.at_k,
        )

    def to_core(self):
        for other in range(self.ring.outers):
            self.core_copy(other).start()

    def outer_copy(self, by):
        g = self.ring
        return copy_to(
            self.outer_out.at[by - 1], self.outer_in.at[by - 1],
            self.y_send.at[self.item, by], self.y_recv.at[self.item, by], g.at_o(g.after(by)),
        )

    def from_core(self):
        g = self.ring
        for other in range(g.outers):
            self.core_copy(other).wait_recv()
        for by in range(1, g.outers):
            goal = g.after(by)
            add_strips(
                self.outer_out.at[by - 1], [self.part.at[:, goal * 2 + g.k], self.core_in.at[goal]], self.chunk
            )
            self.outer_copy(by).start()
        add_strips(self.strip_sum, [self.part.at[:, g.c], self.core_in.at[g.o]], self.chunk)

    def core_done(self):
        for other in range(self.ring.outers):
            self.core_copy(other).wait_send()

    def from_outer(self):
        for by in range(1, self.ring.outers):
            self.outer_copy(by).wait_recv()
        terms = [self.strip_sum] + [self.outer_in.at[by - 1] for by in range(1, self.ring.outers)]
        if len(terms) > 1:
            add_strips(self.strip_sum, terms, self.chunk)

    def outer_done(self):
        for by in range(1, self.ring.outers):
            self.outer_copy(by).wait_send()


class Share:
    def __init__(self, ring, item, slot, sems, source=None):
        self.ring, self.item, self.slot = ring, item, slot
        self.source = slot(ring.c) if source is None else source
        self.y_send, self.y_recv, self.k_send, self.k_recv = sems

    def outer_copy(self, by):
        g = self.ring
        return copy_to(
            self.source, self.slot(g.c), self.y_send.at[self.item, by], self.y_recv.at[self.item, by],
            g.at_o(g.after(by)),
        )

    def core_copy(self, by):
        g = self.ring
        there = self.slot(g.before(by) * 2 + g.k)
        return copy_to(
            self.source if by == 0 else there, there, self.k_send.at[self.item, by], self.k_recv.at[self.item, by],
            g.at_k,
        )

    def start(self):
        for by in range(1, self.ring.outers):
            self.outer_copy(by).start()
        self.core_copy(0).start()

    def pass_on(self):
        g = self.ring
        for by in range(1, g.outers):
            there = self.slot(g.before(by) * 2 + g.k)
            copy_to(there, there, self.y_send.at[self.item, by], self.y_recv.at[self.item, by], g.at_k).wait_recv()
            self.core_copy(by).start()

    def finish(self):
        g = self.ring
        for by in range(g.outers):
            there = self.slot(g.before(by) * 2 + 1 - g.k)
            copy_to(there, there, self.k_send.at[self.item, by], self.k_recv.at[self.item, by], g.at_k).wait_recv()
        for by in range(1, g.outers):
            self.outer_copy(by).wait_send()
        for by in range(g.outers):
            self.core_copy(by).wait_send()


def rotate_tile(u, cosine, sine, first):
    partner = jnp.where(
        first, pltpu.roll(u, LANES - HEAD_WIDTH // 2, 1), pltpu.roll(u, HEAD_WIDTH // 2, 1)
    )
    return u * cosine + partner * sine


def store_part(part, i, tile):
    size, taken = part.shape[2], tile.shape[0]
    per = part.shape[1] * size // taken
    for r in range(taken // size):
        part[i // per, lax.rem(i, per) * (taken // size) + r] = tile[r * size : (r + 1) * size].astype(BF)


def build_back(planes, contexts, rows, width, query_cols, kv_cols, units):
    outers = contexts // 2
    half = width // 2
    depth = width // planes
    strip = depth // contexts
    unit_strip = units // contexts
    seq_len = rows * contexts
    n_q, n_kv = query_cols // LANES, kv_cols // LANES
    heads = query_cols // HEAD_WIDTH
    group = query_cols // kv_cols
    qkv_cols = query_cols + 2 * kv_cols
    DOWN, GATE, UP, KV = range(4)
    lots = max(outers - 1, 1)

    def kernel(
        gate_hbm, up_hbm, down_hbm, norm_hbm, cot_hbm, hid_hbm, gate_grad_hbm, up_grad_hbm, qkv_hbm, out_hbm, q_hbm, kv_hbm, mid_hbm, tok_hbm,
        gains, cosine, sine, pos_q, pos_k, log_sum, scales,
        input_grad, gate_strip, up_strip, down_out, mid_full, qkv_grad, gain_rows, mlp_part,
        norm_x_in, norm_z_in, norm_x_out, norm_sum, mlp_stage, hid, down_w,
        row_core_in, col_core_in, row_outer_in, col_outer_in, row_outer_out, col_outer_out, row_sum, col_sum,
        kv_core_in, kv_outer_in, sq_out, sq_in, first_x_out, first_x_in,
        x_send, x_recv, z_send, z_recv, k_send, k_recv, y_send, y_recv, grad_send, grad_recv, sy_send, sy_recv, sk_send,
        sk_recv, load_sem, stage_sem, credit,
    ):
        ring = Ring(planes, contexts)
        z, c, t, k, o = ring.z, ring.c, ring.t, ring.k, ring.o
        order = ring.by_distance()
        blocks = order[::-1] + [z]
        ring.greet()
        own_cols = pl.multiple_of(t * half, half)
        other_cols = pl.multiple_of((1 - t) * half, half)
        n_half = half // WIDE

        def x_copy(i, src, dst):
            return copy_to(src, dst, x_send.at[i], x_recv.at[i], ring.at_x)

        NORM, MID, SQ_TWO, FIRST, SQ_ONE = 0, planes, planes + 1, planes + 2, planes + 3

        def norm_x(i):
            return x_copy(NORM + i, norm_x_out.at[i % 2], norm_x_in.at[blocks[i]])

        def back_from(p, here):
            return lax.rem(p - here + planes, planes) - 1

        def norm_z(p):
            return copy_to(
                norm_sum.at[p], norm_z_in.at[back_from(z, p)], z_send.at[0, p], z_recv.at[0, z], ring.at_z(p)
            )

        def norm_z_wait(p):
            there = norm_z_in.at[back_from(p, z)]
            copy_to(there, there, z_send.at[0, p], z_recv.at[0, p], ring.at_k).wait_recv()

        def add_block(total, other, p):
            n = rows // 64

            @pl.loop(0, n)
            def _(i):
                r = pl.ds(pl.multiple_of(i * 64, 64), 64)
                total[p, r, :] = (total[p, r, :].astype(F32) + other[p, r, :].astype(F32)).astype(BF)

        def norm_on(i):
            norm_x(i).wait_recv()
            add_block(norm_sum, norm_x_in, blocks[i])

        sems = (k_send, k_recv, y_send, y_recv)

        def feed_forward(norm, cot, gate_grad, up_grad):
            def load(i, src, dst):
                one = pltpu.make_async_copy(src, dst, load_sem.at[i])
                one.start()
                return one

            def product(part, left, right, size):
                total = planes * rows

                @pl.loop(0, left.shape[2] // size)
                def _(i):
                    cols = pl.ds(pl.multiple_of(i * size, size), size)
                    tile = t_dot(left[:, :, cols].reshape(total, size), right[...].reshape(total, right.shape[2]))
                    store_part(part, i, tile)

            def with_weights(gate_w, up_w, col_part):
                weights = [load(0, gate_hbm, gate_w), load(1, up_hbm, up_w)]
                loads = [
                    (load(2 + 2 * i, gate_grad_hbm.at[p], gate_grad.at[p]), load(3 + 2 * i, up_grad_hbm.at[p], up_grad.at[p]))
                    for i, p in enumerate(blocks)
                ]
                later = [
                    load(2 + 2 * planes, hid_hbm, hid), load(3 + 2 * planes, cot_hbm, cot),
                    load(4 + 2 * planes, norm_hbm, norm), load(5 + 2 * planes, down_hbm, down_w),
                ]
                for one in weights:
                    one.wait()

                def norm_block(i):
                    p = blocks[i]
                    for one in loads[i]:
                        one.wait()

                    def tile_of(at):
                        r = pl.ds(pl.multiple_of(at, WIDE), WIDE)
                        return dot_t(gate_grad[p], gate_w[r, :]) + dot_t(up_grad[p], up_w[r, :])

                    if i > 1:
                        norm_x(i - 2).wait_send()

                    @pl.loop(0, n_half)
                    def _(j):
                        here = pl.ds(pl.multiple_of(j * WIDE, WIDE), WIDE)
                        norm_x_out[i % 2, :, here] = tile_of(other_cols + j * WIDE).astype(BF)

                    norm_x(i).start()

                    @pl.loop(0, n_half)
                    def _(j):
                        here = pl.ds(pl.multiple_of(j * WIDE, WIDE), WIDE)
                        norm_sum[p, :, here] = tile_of(own_cols + j * WIDE).astype(BF)

                    if i > 1:
                        norm_on(i - 2)
                        norm_z(blocks[i - 2]).start()

                down = Reduction(
                    ring, DOWN, col_part, col_core_in, col_outer_out, col_outer_in, col_sum, sems
                )
                for i in range(planes - 2):
                    norm_block(i)
                later[0].wait()
                later[1].wait()
                product(col_part, hid, cot, TILE)
                down.to_core()
                norm_block(planes - 2)
                down.from_core()
                norm_block(planes - 1)
                later[2].wait()
                later[3].wait()
                down.core_done()

            pl.run_scoped(
                with_weights,
                pltpu.VMEM((width, units), BF), pltpu.VMEM((width, units), BF), pltpu.VMEM((1, contexts, unit_strip, width), BF),
            )

            def with_parts(row_part):
                gate = Reduction(
                    ring, GATE, row_part, row_core_in, row_outer_out.at[0], row_outer_in.at[0], row_sum.at[0], sems
                )
                up = Reduction(
                    ring, UP, row_part, row_core_in, row_outer_out.at[1], row_outer_in.at[1], row_sum.at[1], sems
                )
                product(row_part, norm, gate_grad, WIDE)
                gate.to_core()
                norm_on(planes - 2)
                norm_z(blocks[planes - 2]).start()
                gate.from_core()
                gate.core_done()
                pl.semaphore_signal(credit, inc=1, device_id=ring.at_k, device_id_type=MESH)
                product(row_part, norm, up_grad, WIDE)
                pl.semaphore_wait(credit, 1)
                up.to_core()
                norm_on(planes - 1)
                up.from_core()
                up.core_done()

            pl.run_scoped(with_parts, pltpu.VMEM((planes, contexts, strip, units), BF))

        block_bf = pltpu.VMEM((planes, rows, width), BF)
        unit_bf = pltpu.VMEM((planes, rows, units), BF)
        pl.run_scoped(feed_forward, block_bf, block_bf, unit_bf, unit_bf)

        down = Reduction(ring, DOWN, None, None, col_outer_out, col_outer_in, col_sum, sems)
        gate = Reduction(ring, GATE, None, None, row_outer_out.at[0], row_outer_in.at[0], row_sum.at[0], sems)
        up = Reduction(ring, UP, None, None, row_outer_out.at[1], row_outer_in.at[1], row_sum.at[1], sems)

        def strip_src(item, goal):
            if item == DOWN:
                return col_sum.at[0, :, pl.ds(pl.multiple_of(goal * depth, depth), depth)]
            return row_sum.at[0 if item == GATE else 1, goal]

        def strip_dst(item, home):
            if item == DOWN:
                return down_out.at[home, c]
            cols = pl.ds(pl.multiple_of(home * units, units), units)
            return (gate_strip if item == GATE else up_strip).at[:, cols]

        def strip_copy(item, s):
            goal = ring.plane(s)
            return copy_to(
                strip_src(item, goal), strip_dst(item, z), grad_send.at[item, s], grad_recv.at[item, z], ring.at_z(goal)
            )

        def strip_keep(item):
            return pltpu.make_async_copy(strip_src(item, z), strip_dst(item, z), grad_send.at[item, 0])

        def to_planes(item, reduction):
            reduction.from_outer()
            for s in range(1, planes):
                strip_copy(item, s).start()
            strip_keep(item).start()

        def from_planes(item):
            for s in range(1, planes):
                p = ring.plane(s)
                there = strip_dst(item, p)
                copy_to(there, there, grad_send.at[item, s], grad_recv.at[item, p], ring.at_k).wait_recv()
            strip_keep(item).wait()

        share_sems = (sy_send, sy_recv, sk_send, sk_recv)
        down_share = Share(ring, 0, lambda q: down_out.at[:, q], share_sems)

        def stage_copy(i):
            return pltpu.make_async_copy(mlp_stage.at[i % 2], mlp_part.at[blocks[i]], stage_sem.at[i % 2])

        def attention(out_w, mid_keep, mid_grad, q_pad, kv_all, tok, grad_pad, query_out, key_sum, value_sum, kv_grad, kv_out):
            loads = [
                pltpu.make_async_copy(mid_hbm, mid_grad, load_sem.at[0]),
                pltpu.make_async_copy(tok_hbm.at[:, pl.ds(own_cols, half)], tok, load_sem.at[1]),
                pltpu.make_async_copy(q_hbm, q_pad, load_sem.at[2]),
                pltpu.make_async_copy(kv_hbm, kv_all, load_sem.at[3]),
                pltpu.make_async_copy(cot_hbm.at[z, :, pl.ds(own_cols, half)], first_x_out, load_sem.at[4]),
            ]
            for one in loads:
                one.start()
            out_load = pltpu.make_async_copy(out_hbm, out_w, load_sem.at[5])
            out_load.start()
            for one in loads:
                one.wait()
            key_sum[...] = jnp.zeros_like(key_sum)
            value_sum[...] = jnp.zeros_like(value_sum)
            gain_rows[...] = jnp.zeros_like(gain_rows)

            def norm_back(grad_of, normal_of, finish, row, i):
                gain = gains[row : row + 1, pl.ds(own_cols, half)]

                def chunk(j):
                    return pl.ds(pl.multiple_of(j * STEP, STEP), STEP)

                @pl.loop(0, rows // STEP)
                def _(j):
                    r = chunk(j)
                    grad, normal = grad_of(r), normal_of(r)
                    both = grad * normal
                    gain_rows[row : row + 1, :] += jnp.sum(both, 0, keepdims=True)
                    sq_out[i, r, :] = jnp.broadcast_to(jnp.sum(both * gain, -1, keepdims=True), (STEP, LANES))

                swap = x_copy(SQ_TWO if i == 0 else SQ_ONE, sq_out.at[i], sq_in.at[i])
                swap.start()
                swap.wait()

                @pl.loop(0, rows // STEP)
                def _(j):
                    r = chunk(j)
                    inner = (sq_out[i, r, 0:1] + sq_in[i, r, 0:1]) * (1.0 / width)
                    finish(r, scales[row, r, 0:1] * (grad_of(r) * gain - normal_of(r) * inner))

            for p in order:
                norm_z_wait(p)

            def norm_grad_of(r):
                grad = norm_sum[z, r, :].astype(F32)
                for i in range(planes - 1):
                    grad = grad + norm_z_in[i, r, :].astype(F32)
                return grad

            def mid_finish(r, back):
                found = first_x_out[r, :].astype(F32) + back
                mid_keep[r, :] = found
                mid_full[r, pl.ds(own_cols, half)] = found.astype(BF)

            norm_back(norm_grad_of, lambda r: mid_grad[r, :] * scales[1, r, 0:1], mid_finish, 1, 0)
            mine = mid_full.at[:, pl.ds(own_cols, half)]
            mid_swap = x_copy(MID, mine, mine)
            mid_swap.start()
            for i, p in enumerate(blocks):
                if i > 1:
                    stage_copy(i - 2).wait()

                @pl.loop(0, width // WIDE)
                def _(j):
                    r = pl.ds(pl.multiple_of(j * WIDE, WIDE), WIDE)
                    mlp_stage[i % 2, :, r] = jnp.dot(hid[p], down_w[:, r], preferred_element_type=F32).astype(BF)

                stage_copy(i).start()
            to_planes(DOWN, down)
            mid_swap.wait_recv()
            out_load.wait()

            lane = lax.broadcasted_iota(jnp.int32, (rows, LANES), 1)
            first = lax.rem(lane, HEAD_WIDTH) < HEAD_WIDTH // 2
            low = lane < HEAD_WIDTH

            @pl.loop(0, query_cols // TILE)
            def _(i):
                r = pl.ds(pl.multiple_of(i * TILE, TILE), TILE)
                found = dot_t(mid_full[...], out_w[r, :])
                for half_tile in range(TILE // LANES):
                    j = i * (TILE // LANES) + half_tile
                    u = found[:, half_tile * LANES : (half_tile + 1) * LANES]
                    u = u.astype(BF).astype(F32)
                    side = lax.rem((2 * j) // group, 2)
                    lo = jnp.where(low, u, 0.0)
                    hi = jnp.where(low, 0.0, u)
                    grad_pad[2 * j] = jnp.where(side == 0, lo, pltpu.roll(lo, HEAD_WIDTH, 1)).astype(BF)
                    grad_pad[2 * j + 1] = jnp.where(side == 1, hi, pltpu.roll(hi, HEAD_WIDTH, 1)).astype(BF)

            for i in range(max(planes - 2, 0), planes):
                stage_copy(i).wait()

            def attend_back(first_head, last_head):
                @pl.loop(first_head, last_head)
                def _(h):
                    pair = h // (2 * group)
                    keys = kv_all[:, pair].reshape(seq_len, LANES)
                    values = kv_all[:, n_kv + pair].reshape(seq_len, LANES)
                    scores = dot_t(keys, q_pad[h])
                    scores = jnp.where(pos_q[0:1, :] >= pos_k[...], scores, NEG)
                    weights = jnp.exp(scores - log_sum[pl.ds(h, 1), :])
                    weight_grad = dot_t(values, grad_pad[h])
                    inner = jnp.sum(weights * weight_grad, 0, keepdims=True)
                    score_grad = (weights * (weight_grad - inner)).astype(BF)
                    value_sum[pair] += jnp.dot(weights.astype(BF), grad_pad[h], preferred_element_type=F32)
                    key_sum[pair] += jnp.dot(score_grad, q_pad[h], preferred_element_type=F32)
                    query_out[h] = t_dot(keys, score_grad).T

            attend_back(0, heads // 2)
            to_planes(GATE, gate)
            attend_back(heads // 2, heads)
            for i in range(n_kv):
                kv_grad[:, i] = key_sum[i].astype(BF).reshape(contexts, rows, LANES)
                kv_grad[:, n_kv + i] = value_sum[i].astype(BF).reshape(contexts, rows, LANES)

            first_swap = x_copy(FIRST, first_x_out, first_x_in)

            def with_qkv(qkv_w, own):
                qkv_load = pltpu.make_async_copy(qkv_hbm, qkv_w, load_sem.at[0])
                qkv_load.start()

                def kv_core(other):
                    return copy_to(
                        kv_grad.at[other * 2 + 1 - k], kv_core_in.at[other], k_send.at[KV, other], k_recv.at[KV, other],
                        ring.at_k,
                    )

                def kv_outer(by):
                    return copy_to(
                        kv_out.at[by - 1], kv_outer_in.at[by - 1], y_send.at[KV, by], y_recv.at[KV, by],
                        ring.at_o(ring.after(by)),
                    )

                for other in range(outers):
                    kv_core(other).start()
                for j in range(n_q):
                    side = (2 * j) // group % 2
                    lo, hi = query_out[2 * j], query_out[2 * j + 1]
                    if side == 0:
                        hi = pltpu.roll(hi, HEAD_WIDTH, 1)
                    else:
                        lo = pltpu.roll(lo, HEAD_WIDTH, 1)
                    u = jnp.where(low, lo, hi) * FACTOR
                    qkv_grad[:, j * LANES : (j + 1) * LANES] = rotate_tile(u, cosine[...], -sine[...], first).astype(BF)
                for other in range(outers):
                    kv_core(other).wait_recv()
                for by in range(1, outers):
                    goal = ring.after(by)
                    kv_out[by - 1] = (
                        kv_grad[goal * 2 + k].astype(F32) + kv_core_in[goal].astype(F32)
                    ).astype(BF)
                    kv_outer(by).start()
                to_planes(UP, up)
                from_planes(DOWN)
                down_share.start()
                kv_sum = kv_grad[c].astype(F32) + kv_core_in[o].astype(F32)
                for by in range(1, outers):
                    kv_outer(by).wait_recv()
                    kv_sum = kv_sum + kv_outer_in[by - 1].astype(F32)
                for i in range(n_kv):
                    at = query_cols + i * LANES
                    qkv_grad[:, at : at + LANES] = rotate_tile(kv_sum[i], cosine[...], -sine[...], first).astype(BF)
                    qkv_grad[:, at + kv_cols : at + kv_cols + LANES] = kv_sum[n_kv + i].astype(BF)
                for other in range(outers):
                    kv_core(other).wait_send()
                for by in range(1, outers):
                    kv_outer(by).wait_send()

                qkv_load.wait()

                def tile_of(at):
                    return dot_t(qkv_grad[...], qkv_w[pl.ds(pl.multiple_of(at, WIDE), WIDE), :])

                @pl.loop(0, n_half)
                def _(j):
                    here = pl.ds(pl.multiple_of(j * WIDE, WIDE), WIDE)
                    first_x_out[:, here] = tile_of(other_cols + j * WIDE).astype(BF)

                first_swap.start()

                @pl.loop(0, n_half)
                def _(j):
                    here = pl.ds(pl.multiple_of(j * WIDE, WIDE), WIDE)
                    own[:, here] = tile_of(own_cols + j * WIDE)

                first_swap.wait()

                def input_finish(r, back):
                    input_grad[r, :] = (mid_keep[r, :] + back).astype(BF)

                norm_back(
                    lambda r: own[r, :] + first_x_in[r, :].astype(F32),
                    lambda r: tok[r, :].astype(F32) * scales[0, r, 0:1],
                    input_finish, 0, 1,
                )

            pl.run_scoped(with_qkv, pltpu.VMEM((width, qkv_cols), BF), pltpu.VMEM((rows, half), F32))
            mid_swap.wait_send()

        tile_f32 = pltpu.VMEM((rows, half), F32)
        pl.run_scoped(
            attention,
            pltpu.VMEM((query_cols, width), BF),
            tile_f32,
            tile_f32,
            pltpu.VMEM((heads, rows, LANES), BF),
            pltpu.VMEM((contexts, 2 * n_kv, rows, LANES), BF),
            pltpu.VMEM((rows, half), BF),
            pltpu.VMEM((heads, rows, LANES), BF),
            pltpu.VMEM((heads, rows, LANES), F32),
            pltpu.VMEM((n_kv, seq_len, LANES), F32),
            pltpu.VMEM((n_kv, seq_len, LANES), F32),
            pltpu.VMEM((contexts, 2 * n_kv, rows, LANES), BF),
            pltpu.VMEM((lots, 2 * n_kv, rows, LANES), BF),
        )

        down_share.pass_on()
        from_planes(GATE)
        from_planes(UP)
        down_share.finish()
        for item in (DOWN, GATE, UP):
            for s in range(1, planes):
                strip_copy(item, s).wait_send()
        for reduction in (down, gate, up):
            reduction.outer_done()
        for i in range(max(planes - 2, 0), planes):
            norm_x(i).wait_send()
        for p in order:
            norm_z(p).wait_send()

    hbm = pl.BlockSpec(memory_space=pl.ANY)
    vmem = pl.BlockSpec(memory_space=pltpu.VMEM)
    dma = pltpu.SemaphoreType.DMA
    shape = jax.ShapeDtypeStruct
    acts = pltpu.VMEM((planes, rows, half), BF)
    arrivals = pltpu.VMEM((planes - 1, rows, half), BF)
    unit_acts = pltpu.VMEM((planes, rows, units), BF)
    return pl.pallas_call(
        kernel,
        name="back",
        out_shape=(
            shape((rows, half), BF),
            shape((strip, planes * units), BF),
            shape((strip, planes * units), BF),
            shape((planes, contexts, unit_strip, depth), BF),
            shape((rows, width), BF),
            shape((rows, qkv_cols), BF),
            shape((8, half), F32),
            shape((planes, rows, width), BF),
        ),
        in_specs=[hbm] * 14 + [vmem] * 7,
        out_specs=(vmem, hbm, hbm, hbm, vmem, vmem, vmem, hbm),
        scratch_shapes=[acts, arrivals, pltpu.VMEM((2, rows, half), BF), acts, pltpu.VMEM((2, rows, width), BF), unit_acts, pltpu.VMEM((units, width), BF)]
        + [
            pltpu.VMEM((outers, planes, strip, units), BF),
            pltpu.VMEM((outers, 1, unit_strip, width), BF),
            pltpu.VMEM((2, lots, planes, strip, units), BF),
            pltpu.VMEM((lots, 1, unit_strip, width), BF),
            pltpu.VMEM((2, lots, planes, strip, units), BF),
            pltpu.VMEM((lots, 1, unit_strip, width), BF),
            pltpu.VMEM((2, planes, strip, units), BF),
            pltpu.VMEM((1, unit_strip, width), BF),
            pltpu.VMEM((outers, 2 * n_kv, rows, LANES), BF),
            pltpu.VMEM((lots, 2 * n_kv, rows, LANES), BF),
            pltpu.VMEM((2, rows, LANES), F32),
            pltpu.VMEM((2, rows, LANES), F32),
            pltpu.VMEM((rows, half), BF),
            pltpu.VMEM((rows, half), BF),
            dma((planes + 4,)),
            dma((planes + 4,)),
            dma((1, planes)),
            dma((1, planes)),
            dma((4, outers)),
            dma((4, outers)),
            dma((4, max(outers, 2))),
            dma((4, max(outers, 2))),
            dma((3, planes)),
            dma((3, planes)),
            dma((2, max(outers, 2))),
            dma((2, max(outers, 2))),
            dma((2, outers)),
            dma((2, outers)),
            dma((2 * planes + 6,)),
            dma((2,)),
            pltpu.SemaphoreType.REGULAR,
        ],
        compiler_params=pltpu.CompilerParams(
            collective_id=1, has_side_effects=True, vmem_limit_bytes=VMEM_LIMIT
        ),
        cost_estimate=pl.CostEstimate(flops=50 * 10**9, bytes_accessed=80 * 10**6, transcendentals=8 * 10**6),
    )


def build_grads(planes, contexts, rows, width, query_cols, kv_cols, units):
    outers = contexts // 2
    half = width // 2
    depth = width // planes
    strip = depth // contexts
    out_strip = query_cols // contexts
    unit_strip = units // contexts
    qkv_cols = query_cols + 2 * kv_cols
    lots = max(outers - 1, 1)
    per_half = planes // 2
    OUT, QKV, UP, GATE = range(4)

    def kernel(
        attn, mid_full, normed_one, qkv_grad, gain_rows, mid_own, gate_strip, up_strip, mlp_part,
        gate_out, up_out, out_out, qkv_out, gain_out, result,
        out_part, qkv_part, out_core, qkv_core, out_outer_out, qkv_outer_out, out_outer_in, qkv_outer_in,
        out_sum, qkv_sum, out_z, qkv_z, gain_z, gain_y, gain_k, gain_now, mlp_x_in, mlp_z_in, mlp_sum,
        k_send, k_recv, y_send, y_recv, z_send, z_recv, sk_send, sk_recv, sy_send, sy_recv, gain_send, gain_recv,
        mx_send, mx_recv, mz_send, mz_recv, own_sem,
    ):
        ring = Ring(planes, contexts)
        z, c, t, k, o = ring.z, ring.c, ring.t, ring.k, ring.o
        order = ring.by_distance()
        ring.greet()

        def rows_of(whole, size):
            return lambda q: whole.at[pl.ds(pl.multiple_of(q * size, size), size), :]

        share_sems = (sy_send, sy_recv, sk_send, sk_recv)
        up_share = Share(ring, UP, rows_of(up_out, strip), share_sems, up_strip)
        out_share = Share(ring, OUT, rows_of(out_out, out_strip), share_sems)
        qkv_share = Share(ring, QKV, rows_of(qkv_out, strip), share_sems)
        gate_share = Share(ring, GATE, rows_of(gate_out, strip), share_sems, gate_strip)
        gate_share.start()
        keeps = [
            pltpu.make_async_copy(gate_strip, rows_of(gate_out, strip)(c), own_sem.at[0]),
            pltpu.make_async_copy(up_strip, rows_of(up_out, strip)(c), own_sem.at[2]),
        ]
        for one in keeps:
            one.start()

        own_cols = pl.multiple_of(t * half, half)
        other_cols = pl.multiple_of((1 - t) * half, half)
        blocks = order[::-1] + [z]

        def mlp_x(p):
            return copy_to(
                mlp_part.at[p, :, pl.ds(other_cols, half)], mlp_x_in.at[p], mx_send.at[p], mx_recv.at[p], ring.at_x
            )

        def mlp_z(p):
            return copy_to(
                mlp_sum.at[p], mlp_z_in.at[lax.rem(z - p + planes, planes) - 1], mz_send.at[p], mz_recv.at[z],
                ring.at_z(p),
            )

        mlp_load = pltpu.make_async_copy(mlp_part.at[:, :, pl.ds(own_cols, half)], mlp_sum, own_sem.at[1])
        for p in blocks:
            mlp_x(p).start()
        mlp_load.start()

        def mlp_on(p):
            mlp_x(p).wait_recv()

            @pl.loop(0, rows // 64)
            def _(i):
                r = pl.ds(pl.multiple_of(i * 64, 64), 64)
                mlp_sum[p, r, :] = (mlp_sum[p, r, :].astype(F32) + mlp_x_in[p, r, :].astype(F32)).astype(BF)

        takes_part = z // per_half == t

        def gain_plane(j):
            return t * per_half + j

        def gain_copy(j):
            return copy_to(
                gain_rows.at[:, pl.ds(j * depth, depth)], gain_z.at[z], gain_send.at[j], gain_recv.at[z],
                ring.at_z(gain_plane(j)),
            )

        for j in range(per_half):

            @pl.when(gain_plane(j) != z)
            def _(j=j):
                gain_copy(j).start()

        gain_x = copy_to(
            gain_out, gain_out, gain_send.at[per_half], gain_recv.at[planes], ring.at_x
        )

        def gain_outer(by):
            return copy_to(
                gain_now.at[0], gain_y.at[by - 1], gain_send.at[per_half + by], gain_recv.at[planes + by],
                ring.at_o(ring.after(by)),
            )

        gain_core = copy_to(
            gain_now.at[1], gain_k, gain_send.at[per_half + outers], gain_recv.at[planes + outers], ring.at_k
        )

        def product(part, left, right):
            @pl.loop(0, left.shape[1] // TILE)
            def _(i):
                cols = pl.ds(pl.multiple_of(i * TILE, TILE), TILE)
                store_part(part, i, t_dot(left[:, cols], right[...]))

        sems = (k_send, k_recv, y_send, y_recv)
        out = Reduction(ring, 0, out_part, out_core, out_outer_out, out_outer_in, out_sum, sems)
        qkv = Reduction(ring, 1, qkv_part, qkv_core, qkv_outer_out, qkv_outer_in, qkv_sum, sems)
        product(qkv_part, normed_one, qkv_grad)
        qkv.to_core()
        product(out_part, attn, mid_full)
        qkv.from_core()
        out.to_core()

        @pl.when(takes_part)
        def _():
            mine = lax.rem(z, per_half) * depth
            total = gain_rows[:, pl.ds(pl.multiple_of(mine, depth), depth)]
            for s in range(1, planes):
                p = ring.plane(s)
                copy_to(gain_z.at[p], gain_z.at[p], gain_send.at[0], gain_recv.at[p], ring.at_k).wait_recv()
                total = total + gain_z[p]
            gain_now[0] = total
            for by in range(1, outers):
                gain_outer(by).start()

        out.from_core()
        mlp_load.wait()
        for p in blocks[:-1]:
            mlp_on(p)
            mlp_z(p).start()

        @pl.when(takes_part)
        def _():
            total = gain_now[0]
            for by in range(1, outers):
                gain_outer(by).wait()
                total = total + gain_y[by - 1]
            gain_now[1] = total
            gain_core.start()

        def piece(item, p):
            if item == OUT:
                return out_sum.at[0, :, pl.ds(pl.multiple_of(p * depth, depth), depth)]
            return qkv_sum.at[p]

        def landing(item, p):
            return (out_z if item == OUT else qkv_z).at[p]

        def z_copy(item, s):
            p = ring.plane(s)
            return copy_to(
                piece(item, p), landing(item, z), z_send.at[item, s], z_recv.at[item, z], ring.at_z(p)
            )

        def to_planes(item, reduction):
            reduction.from_outer()
            for s in range(1, planes):
                z_copy(item, s).start()

        def from_planes(item):
            for p in order:
                there = landing(item, p)
                copy_to(there, there, z_send.at[item, 0], z_recv.at[item, p], ring.at_k).wait_recv()
            size = out_strip if item == OUT else strip
            whole = out_out if item == OUT else qkv_out
            total = piece(item, z)[...].astype(F32)
            for p in order:
                total = total + landing(item, p)[...].astype(F32)
            whole[pl.ds(pl.multiple_of(c * size, size), size), :] = total.astype(BF)
            (out_share if item == OUT else qkv_share).start()

        to_planes(QKV, qkv)

        @pl.when(takes_part)
        def _():
            gain_core.wait()
            gain_out[...] = gain_now[1] + gain_k[...]
            gain_x.start()

        to_planes(OUT, out)
        up_share.start()
        from_planes(QKV)
        mlp_on(z)
        from_planes(OUT)
        total = mid_own[...] + mlp_sum[z].astype(F32)
        for p in order:
            there = mlp_z_in.at[lax.rem(p - z + planes, planes) - 1]
            copy_to(there, there, mz_send.at[p], mz_recv.at[p], ring.at_k).wait_recv()
            total = total + there[...].astype(F32)
        result[...] = total.astype(BF)
        for one in (gate_share, up_share, qkv_share, out_share):
            one.pass_on()
        for one in keeps:
            one.wait()
        for one in (gate_share, up_share, qkv_share, out_share):
            one.finish()
        for p in blocks:
            mlp_x(p).wait_send()
        for p in order:
            mlp_z(p).wait_send()
        for reduction in (out, qkv):
            reduction.core_done()
            reduction.outer_done()
        for item in (OUT, QKV):
            for s in range(1, planes):
                z_copy(item, s).wait_send()
        for j in range(per_half):

            @pl.when(gain_plane(j) != z)
            def _(j=j):
                gain_copy(j).wait_send()

        @pl.when(takes_part)
        def _():
            gain_x.wait_send()

        @pl.when(jnp.logical_not(takes_part))
        def _():
            gain_x.wait_recv()

    hbm = pl.BlockSpec(memory_space=pl.ANY)
    vmem = pl.BlockSpec(memory_space=pltpu.VMEM)
    dma = pltpu.SemaphoreType.DMA
    shape = jax.ShapeDtypeStruct
    return pl.pallas_call(
        kernel,
        name="grads",
        out_shape=(
            shape((depth, planes * units), BF),
            shape((depth, planes * units), BF),
            shape((query_cols, depth), BF),
            shape((depth, qkv_cols), BF),
            shape((8, depth), F32),
            shape((rows, half), BF),
        ),
        in_specs=[vmem] * 6 + [hbm] * 3,
        out_specs=(hbm, hbm, vmem, vmem, vmem, vmem),
        scratch_shapes=[
            pltpu.VMEM((1, contexts, out_strip, width), BF),
            pltpu.VMEM((planes, contexts, strip, qkv_cols), BF),
            pltpu.VMEM((outers, 1, out_strip, width), BF),
            pltpu.VMEM((outers, planes, strip, qkv_cols), BF),
            pltpu.VMEM((lots, 1, out_strip, width), BF),
            pltpu.VMEM((lots, planes, strip, qkv_cols), BF),
            pltpu.VMEM((lots, 1, out_strip, width), BF),
            pltpu.VMEM((lots, planes, strip, qkv_cols), BF),
            pltpu.VMEM((1, out_strip, width), BF),
            pltpu.VMEM((planes, strip, qkv_cols), BF),
            pltpu.VMEM((planes, out_strip, depth), BF),
            pltpu.VMEM((planes, strip, qkv_cols), BF),
            pltpu.VMEM((planes, 8, depth), F32),
            pltpu.VMEM((lots, 8, depth), F32),
            pltpu.VMEM((8, depth), F32),
            pltpu.VMEM((2, 8, depth), F32),
            pltpu.VMEM((planes, rows, half), BF),
            pltpu.VMEM((planes - 1, rows, half), BF),
            pltpu.VMEM((planes, rows, half), BF),
            dma((2, outers)),
            dma((2, outers)),
            dma((2, max(outers, 2))),
            dma((2, max(outers, 2))),
            dma((2, planes)),
            dma((2, planes)),
            dma((4, outers)),
            dma((4, outers)),
            dma((4, max(outers, 2))),
            dma((4, max(outers, 2))),
            dma((per_half + outers + 1,)),
            dma((planes + outers + 1,)),
            dma((planes,)),
            dma((planes,)),
            dma((planes,)),
            dma((planes,)),
            dma((3,)),
        ],
        compiler_params=pltpu.CompilerParams(
            collective_id=2, has_side_effects=True, vmem_limit_bytes=VMEM_LIMIT
        ),
        cost_estimate=pl.CostEstimate(flops=4 * 10**9, bytes_accessed=40 * 10**6, transcendentals=0),
    )


def shards(
    tokens,
    span_order,
    attn_gain,
    w_query,
    key_weight,
    value_weight,
    w_out,
    mlp_gain,
    w_gate,
    w_up,
    w_down,
    out_grad,
):
    planes = lax.axis_size("fsdp")
    contexts = lax.axis_size("context")
    tok_own, cot_own = tokens[0], out_grad[0]
    rows, own_cols = tok_own.shape
    width = own_cols * 2
    depth = width // planes
    units = w_gate.shape[1] // planes
    query_cols = w_query.shape[1]
    kv_cols = key_weight.shape[1]
    sizes = (planes, contexts, rows, width, query_cols, kv_cols, units)

    freqs = jnp.tile(rope_freqs(HEAD_WIDTH), LANES // (HEAD_WIDTH // 2))[None]
    (
        gate_w, up_w, down_w, cot_all, norm_all, qkv_w, out_w, hid, gate_grad, up_grad, gains, q_pad, kv_all, attn, log_sum, mid_own,
        normed_one, tok_all, scales, cosine_table, sine_table, pos_q, pos_k,
    ) = build_front(*sizes)(
        tok_own, cot_own, attn_gain[None], mlp_gain[None], w_query, key_weight, value_weight, w_out, w_gate, w_up,
        w_down, span_order, freqs,
    )
    input_grad, gate_strip, up_strip, down_out, mid_full, qkv_grad, gain_rows, mlp_part = build_back(*sizes)(
        gate_w, up_w, down_w, norm_all, cot_all, hid, gate_grad, up_grad, qkv_w, out_w, q_pad, kv_all, mid_own, tok_all, gains,
        cosine_table, sine_table, pos_q, pos_k, log_sum, scales,
    )
    gate_out, up_out, out_out, qkv_out, gain_out, result = build_grads(*sizes)(
        attn, mid_full, normed_one, qkv_grad, gain_rows, mid_own, gate_strip, up_strip, mlp_part
    )
    qkv_out = qkv_out.astype(F32)
    return (
        result[None],
        input_grad[None],
        gain_out[0],
        qkv_out[:, :query_cols],
        qkv_out[:, query_cols : query_cols + kv_cols],
        qkv_out[:, query_cols + kv_cols :],
        out_out.astype(F32),
        gain_out[1],
        gate_out.astype(F32),
        up_out.astype(F32),
        down_out.reshape(planes * units, depth).astype(F32),
    )


def solution(mesh):
    weight = P("fsdp", "tensor")
    turned = P("tensor", "fsdp")
    block = P("fsdp", "context", "tensor")
    gain = P("fsdp")
    return jax.shard_map(
        shards,
        mesh=mesh,
        in_specs=(
            block, P(), gain, weight, weight, weight, turned, gain, weight, weight, turned, block,
        ),
        out_specs=(
            block, block, gain, weight, weight, weight, turned, gain, weight, weight, turned,
        ),
        check_vma=False,
    )
```
